32 devices in a mesh: seq: 8 (over z, x), blk: 4 (over y, core).
Axes of the slice: x: 2, y: 2, z: 4, core: 2. Of those that a mesh axis runs over, the one named last changes fastest.
Arguments:
- tokens: bfloat16 [1024, 4, 512], P('seq', 'blk'), may hold values from -6 to 6
- lengths: int32 [4, 8], replicated, may hold values from 0 to 1024, as said below
- norm_gain: float32 [2, 512], replicated, may hold values from 0.5 to 1.5
- in_proj: bfloat16 [2, 512, 2, 384], replicated, may hold values from -0.25 to 0.25
- out_proj: bfloat16 [2, 2, 384, 512], replicated, may hold values from -1.25 to 1.25
- skip_gain: float32 [2, 512], replicated, may hold values from -1 to 1
- glu_weight: bfloat16 [2, 512, 512], replicated, may hold values from -0.25 to 0.25
- glu_bias: float32 [2, 512], replicated, may hold values from -3 to 3
- decay_log: float32 [2, 384], replicated, may hold values from -3.9 to 0
- frequency: float32 [2, 384], replicated, may hold values from -30 to 30
- step_log: float32 [2, 384], replicated, may hold values from -6.9 to -3
- cotangent: bfloat16 [1024, 4, 512], P('seq', 'blk'), may hold values from -6 to 6
Outputs:
- activations: bfloat16 [1024, 4, 512], P('seq', 'blk')
- tokens_grad: float32 [1024, 4, 512], P('seq', 'blk')
- norm_gain_grad: float32 [2, 512], P(None, ('seq', 'blk'))
- in_proj_grad: float32 [2, 512, 2, 384], P(None, ('seq', 'blk'))
- out_proj_grad: float32 [2, 2, 384, 512], P(None, None, None, ('seq', 'blk'))
- skip_gain_grad: float32 [2, 512], P(None, ('seq', 'blk'))
- glu_weight_grad: float32 [2, 512, 512], P(None, ('seq', 'blk'))
- glu_bias_grad: float32 [2, 512], P(None, ('seq', 'blk'))
- decay_log_grad: float32 [2, 384], replicated
- frequency_grad: float32 [2, 384], replicated
- step_log_grad: float32 [2, 384], replicated
The draws below stay inside these ranges and needn't reach their ends.
Inputs may be any that keep to these rules, and one draw needn't show every extreme that they name: `lengths`: each row sums to 1024. In one row, chosen by the seed, the first item fills the whole stream and the others are empty; every other row holds 8 items of 64 to 192 positions each, in random order.
All inputs are finite; a program needn't handle non-finite values.
Results may differ from the reference program's by a relative error of at most 0.015.
Values may be sent and summed in bfloat16 or wider, within the bound.
A program may use at most 192 MiB of HBM per device.

```python
import jax
import jax.numpy as jnp
from jax import lax

H = 512
P_SIZE = 384
STREAMS = 4
STREAM_LEN = 1024


def draw_lengths(key, part):
    key = jax.random.fold_in(key, 11)
    shift_key, order_key, pick_key = jax.random.split(key, 3)
    base_len = STREAM_LEN // 8
    reach = STREAM_LEN // 16
    shifts = jax.random.randint(shift_key, (STREAMS, 4), -reach, reach + 1)
    paired = jnp.concatenate([base_len + shifts, base_len - shifts], axis=1)
    scores = jax.random.randint(order_key, (STREAMS, 8), 0, 1 << 20) * 8 + jnp.arange(8, dtype=jnp.int32)[None, :]
    order = jnp.argsort(scores, axis=1)
    paired = jnp.take_along_axis(paired, order, axis=1)
    chosen = jnp.arange(STREAMS, dtype=jnp.int32) == jax.random.randint(pick_key, (), 0, STREAMS)
    single = jnp.where(jnp.arange(8, dtype=jnp.int32) == 0, STREAM_LEN, 0)
    return jnp.where(chosen[:, None], single[None, :], paired).astype(jnp.int32)


def steps_of(own_key, dims, cuts, smallest, top_value):
    def one(axis_at, shards_of):
        steps = jax.random.uniform(jax.random.fold_in(jax.random.fold_in(own_key, 6), axis_at), (shards_of,), jnp.float32, smallest / len(cuts), top_value / len(cuts))
        return jnp.repeat(jnp.exp(steps), dims[axis_at] // shards_of).reshape((-1,) + (1,) * (len(dims) - axis_at - 1))

    loudness = one(*cuts[0])
    for cut in cuts[1:]:
        loudness = loudness * one(*cut)
    return loudness


def bell_draw(key, shape, spread, most, cuts=(), kind=jnp.bfloat16):
    values = jax.random.normal(key, shape, jnp.float32) * spread
    if len(cuts) > 0:
        values = steps_of(key, shape, cuts, -0.22, 0.18) * values
    return jnp.clip(values, min=-most, max=most).astype(kind)


def setup_inputs(seed: int = 0) -> dict:
    streams_of = jax.random.split(jax.random.key(seed), 13)
    return {
        "tokens": bell_draw(streams_of[0], (STREAM_LEN, STREAMS, H), 1.0, 6.0, ((0, 8), (1, 4))),
        "lengths": draw_lengths(jax.random.fold_in(streams_of[12], 71), 0),
        "norm_gain": jnp.clip(1.0 + 0.1 * jax.random.normal(streams_of[2], (2, H), jnp.float32), 0.5, 1.5),
        "in_proj": bell_draw(streams_of[3], (2, H, 2, P_SIZE), H ** -0.5, 0.25),
        "out_proj": bell_draw(streams_of[4], (2, 2, P_SIZE, H), (P_SIZE // 16) ** -0.5, 1.25),
        "skip_gain": jnp.clip(jax.random.uniform(streams_of[5], (2, H), jnp.float32, -1.0, 1.0), -1.0, 1.0),
        "glu_weight": bell_draw(streams_of[6], (2, H, H), H ** -0.5, 0.25),
        "glu_bias": bell_draw(streams_of[7], (2, H), 0.5, 3.0, (), jnp.float32),
        "decay_log": jnp.clip(jax.random.uniform(streams_of[8], (2, P_SIZE), jnp.float32, -3.9, 0.0), -3.9, 0.0),
        "frequency": jnp.clip(jax.random.uniform(streams_of[9], (2, P_SIZE), jnp.float32, -30.0, 30.0), -30.0, 30.0),
        "step_log": jnp.clip(jax.random.uniform(streams_of[10], (2, P_SIZE), jnp.float32, -6.9, -3.0), -6.9, -3.0),
        "cotangent": bell_draw(streams_of[11], (STREAM_LEN, STREAMS, H), 1.0, 6.0, ((0, 8), (1, 4))),
    }


EPS = 1e-06
HIGHEST = lax.Precision.HIGHEST

@jax.custom_vjp
def low(v):
    return lax.optimization_barrier(v.astype(jnp.bfloat16)).astype(jnp.float32)

@jax.custom_vjp
def low_back(v):
    return v

def low_keep(v):
    return (low(v), None)

def low_pass(kept, grad):
    return (grad,)

def back_keep(v):
    return (v, None)

def back_low(kept, grad):
    return (low(grad),)
low.defvjp(low_keep, low_pass)
low_back.defvjp(back_keep, back_low)

def combine(earlier, later):
    prior_re, prior_im, prior_sre, prior_sim = earlier
    next_re, next_im, next_sre, next_sim = later
    return (next_re * prior_re - next_im * prior_im, next_re * prior_im + next_im * prior_re, next_re * prior_sre - next_im * prior_sim + next_sre, next_re * prior_sim + next_im * prior_sre + next_sim)

def discretize(decay_vec, freq_vec, step_vec):
    lam_re = -jnp.exp(decay_vec)
    step_size = jnp.exp(step_vec)
    rotation = freq_vec * step_size
    shrink = jnp.expm1(lam_re * step_size)
    cosine = jnp.cos(rotation)
    sine_part = jnp.sin(rotation)
    magnitude = shrink + 1.0
    bar_re = magnitude * cosine
    bar_im = magnitude * sine_part
    minus_re = shrink * cosine - 2.0 * jnp.sin(0.5 * rotation) ** 2
    minus_im = bar_im
    denominator = lam_re * lam_re + freq_vec * freq_vec
    coef_re = (minus_re * lam_re + minus_im * freq_vec) / denominator
    coef_im = (minus_im * lam_re - minus_re * freq_vec) / denominator
    return (bar_re, bar_im, coef_re, coef_im)

def normalize(values, gain_vec):
    inv_scale = lax.rsqrt(lax.optimization_barrier(jnp.mean(values * values, axis=-1, keepdims=True)) + EPS)
    return values * inv_scale * gain_vec

def recurrence(bar_re, bar_im, keep_mask, drive_re, drive_im, backward):
    pieces = (bar_re[:, None] * keep_mask, bar_im[:, None] * keep_mask, drive_re, drive_im)
    if backward:
        pieces = tuple((jnp.flip(piece, -1) for piece in pieces))
    result = lax.associative_scan(combine, pieces, axis=-1)
    state_re, state_im = (result[2], result[3])
    if backward:
        state_re, state_im = (jnp.flip(state_re, -1), jnp.flip(state_im, -1))
    return (state_re, state_im)

def layer(layer_in, weights, keep_mask, backward):
    gain_vec, in_weight, out_weight, skip_vec, glu_matrix, glu_shift, decay_vec, freq_vec, step_vec = weights
    normed = normalize(layer_in, gain_vec)
    normed_low = low(normed)
    projected = low_back(low(jnp.einsum('th,hcp->cpt', normed_low, in_weight, precision=HIGHEST)))
    bar_re, bar_im, coef_re, coef_im = discretize(decay_vec, freq_vec, step_vec)
    drive_re = coef_re[:, None] * projected[0] - coef_im[:, None] * projected[1]
    drive_im = coef_re[:, None] * projected[1] + coef_im[:, None] * projected[0]
    state_re, state_im = recurrence(bar_re, bar_im, keep_mask, drive_re, drive_im, backward)
    state_low = low_back(low(jnp.stack([state_re, state_im])))
    mixed = jnp.einsum('cpt,cph->th', state_low, out_weight, precision=HIGHEST) + skip_vec * normed
    mixed = low_back(mixed)
    activated = jax.nn.gelu(mixed)
    gate_pre = low_back(jnp.dot(low(activated), glu_matrix, precision=HIGHEST) + glu_shift)
    return layer_in + activated * jax.nn.sigmoid(gate_pre)

def one_stream(stream_in, lengths_row, weights):
    length_total = stream_in.shape[0]
    position = jnp.arange(length_total, dtype=jnp.int32)
    item_ends = jnp.cumsum(lengths_row)
    item_starts = item_ends - lengths_row
    keep_start = 1.0 - jnp.any(position[:, None] == item_starts[None, :], axis=1).astype(jnp.float32)
    keep_end = 1.0 - jnp.any(position[:, None] == (item_ends - 1)[None, :], axis=1).astype(jnp.float32)
    first_out = layer(stream_in, tuple((param[0] for param in weights)), keep_start, False)
    return layer(first_out, tuple((param[1] for param in weights)), keep_end, True)

def reference(tokens, lengths, norm_gain, in_proj, out_proj, skip_gain, glu_weight, glu_bias, decay_log, frequency, step_log, cotangent):
    params = (norm_gain, in_proj.astype(jnp.float32), out_proj.astype(jnp.float32), skip_gain, glu_weight.astype(jnp.float32), glu_bias, decay_log, frequency, step_log)
    stepper = jax.checkpoint(one_stream)

    def forward(inputs, weights):
        streams = jnp.transpose(inputs, (1, 0, 2))
        outputs = lax.map(lambda stream_item: stepper(stream_item[0], stream_item[1], weights), (streams, lengths))
        return jnp.transpose(outputs, (1, 0, 2))
    outputs, pullback = jax.vjp(forward, tokens.astype(jnp.float32), params)
    tokens_grad, grads = pullback(cotangent.astype(jnp.float32))
    return (outputs.astype(jnp.bfloat16), tokens_grad, grads[0], grads[1], grads[2], grads[3], grads[4], grads[5], grads[6], grads[7], grads[8])
```

```python
import types

import jax
import jax.numpy as jnp
from jax import lax
from jax.experimental import pallas as pl
from jax.experimental.pallas import tpu as pltpu
from jax.sharding import PartitionSpec as P

EPS = 1e-6
F32 = jnp.float32
LOW = jnp.bfloat16
GELU_A = 0.7978845608028654
GELU_B = 0.044715
LANES = 128
SUB = 8
BLOCK = 16
LINKS = 112


def cmul(are, aim, bre, bim):
    return are * bre - aim * bim, are * bim + aim * bre


def expm1(value):
    series = jnp.ones_like(value)
    for order in range(9, 1, -1):
        series = 1.0 + value * series * (1.0 / order)
    return jnp.where(value > -0.35, value * series, jnp.exp(value) - 1.0)


def discretize(decay, freq, step_log):
    lam_re = -jnp.exp(decay)
    step = jnp.exp(step_log)
    rotation = freq * step
    shrink = expm1(lam_re * step)
    cosine, sine = jnp.cos(rotation), jnp.sin(rotation)
    half = jnp.sin(0.5 * rotation)
    bar_re = (shrink + 1.0) * cosine
    bar_im = (shrink + 1.0) * sine
    minus_re = shrink * cosine - 2.0 * half * half
    scale = 1.0 / (lam_re * lam_re + freq * freq)
    coef_re = (minus_re * lam_re + bar_im * freq) * scale
    coef_im = (bar_im * lam_re - minus_re * freq) * scale
    return types.SimpleNamespace(
        lam_re=lam_re, freq=freq, step=step, scale=scale,
        bar_re=bar_re, bar_im=bar_im, coef_re=coef_re, coef_im=coef_im,
    )


def discretize_grad(d, bar_gre, bar_gim, coef_gre, coef_gim):
    over_re, over_im = d.lam_re * d.scale, d.freq * d.scale
    part_re, part_im = cmul(coef_gre, coef_gim, over_re, over_im)
    all_re, all_im = bar_gre + part_re, bar_gim + part_im
    one_re, one_im = cmul(all_re, all_im, d.bar_re, -d.bar_im)
    two_re, two_im = cmul(part_re, part_im, d.coef_re, -d.coef_im)
    lam_gre = one_re * d.step - two_re
    lam_gim = one_im * d.step - two_im
    step_g = one_re * d.lam_re + one_im * d.freq
    return lam_gre * d.lam_re, lam_gim, step_g * d.step


def mm(a, b):
    return jnp.dot(a, b, preferred_element_type=F32)


def mm_nt(a, b):
    return lax.dot_general(a, b, (((1,), (1,)), ((), ())), preferred_element_type=F32)


def wide(mask, width):
    return jnp.concatenate([mask] * (width // LANES), axis=1)


class Wire:
    def __init__(self, send_sems, recv_sems):
        self.send_sems, self.recv_sems = send_sems, recv_sems
        self.count = 0
        self.open = []

    def send(self, src, dst, device):
        at = self.count
        self.count += 1
        copy = pltpu.make_async_remote_copy(
            src_ref=src, dst_ref=dst,
            send_sem=self.send_sems.at[at], recv_sem=self.recv_sems.at[at],
            device_id=device, device_id_type=pl.DeviceIdType.MESH,
        )
        copy.start()
        self.open.append(copy)
        return copy

    def close(self):
        for copy in self.open:
            copy.wait_send()


def make_kernel(names, z):
    T, H, N, S, nseq, nblk, fused = z.T, z.H, z.N, z.S, z.nseq, z.nblk, z.fused
    W = 2 * N
    CE = H + W

    def kernel(*refs):
        r = types.SimpleNamespace(**dict(zip(names, refs, strict=True)))
        seq = lax.axis_index("seq")
        blk = lax.axis_index("blk")
        wire = Wire(r.send_sems, r.recv_sems)
        core, yy = blk % 2, blk // 2
        xx, zz = seq % 2, seq // 2
        nz = nseq // 2
        sibling = {"blk": yy * 2 + (1 - core)}
        y_peer = {"blk": (1 - yy) * 2 + core}
        x_peer = {"seq": zz * 2 + (1 - xx)}

        loads = {}

        def load(name, src, dst):
            copy = pltpu.make_async_copy(src, dst, r.load_sems.at[len(loads)])
            copy.start()
            loads[name] = copy

        load("tok", r.tokens, r.tok)
        load("wi0", r.in_proj.at[0], r.wi.at[0])
        load("wo0", r.out_proj.at[0], r.wo.at[0])
        load("wg0", r.glu_weight.at[0], r.wg.at[0])
        load("wi1", r.in_proj.at[1], r.wi.at[1])
        load("wo1", r.out_proj.at[1], r.wo.at[1])
        load("wg1", r.glu_weight.at[1], r.wg.at[1])
        load("cot", r.cotangent, r.cot)

        barrier = pltpu.get_barrier_semaphore()
        greeted = [{"seq": (seq + o) % nseq} for o in range(1, nseq)]
        if fused:
            greeted += [sibling, y_peer]
        for device in greeted:
            pl.semaphore_signal(barrier, inc=1, device_id=device, device_id_type=pl.DeviceIdType.MESH)

        disc, powers = [], []
        for l in range(2):
            d = discretize(
                r.decay_log[l : l + 1, :], r.frequency[l : l + 1, :], r.step_log[l : l + 1, :]
            )
            disc.append(d)
            chain = [(d.bar_re, d.bar_im)]
            while len(chain) < 12:
                chain.append(cmul(*chain[-1], *chain[-1]))
            powers.append(chain)
        step_bits = S.bit_length() - 1
        seg_bits = T.bit_length() - 1

        def power_rows(l, first, exponent, bits):
            rows = exponent.shape[0]
            out_re = jnp.ones((rows, N), F32)
            out_im = jnp.zeros((rows, N), F32)
            for bit in range(bits):
                use = wide(((exponent >> bit) & 1) == 1, N)
                pre, pim = powers[l][first + bit]
                new_re, new_im = cmul(out_re, out_im, pre, pim)
                out_re = jnp.where(use, new_re, out_re)
                out_im = jnp.where(use, new_im, out_im)
            return out_re, out_im

        ends, starts = [], []
        total = jnp.int32(0)
        for i in range(r.lengths.shape[1]):
            starts.append(total)
            total = total + r.lengths[blk, i]
            ends.append(total - 1)

        def keep(position, marks):
            hit = position == marks[0]
            for mark in marks[1:]:
                hit = hit | (position == mark)
            return jnp.where(hit, 0.0, 1.0).astype(F32)

        row = lax.broadcasted_iota(jnp.int32, (T, LANES), 0)
        here = seq * T + (row % SUB) * S + row // SUB
        r.keep[0] = keep(here, starts)
        r.keep[1] = keep(here, ends)
        offset = lax.broadcasted_iota(jnp.int32, (nseq, T), 0)
        lane = lax.broadcasted_iota(jnp.int32, (nseq, T), 1)
        there = ((seq - offset + nseq) % nseq) * T + lane
        k8 = lax.broadcasted_iota(jnp.int32, (SUB, LANES), 0)
        n_row = lax.broadcasted_iota(jnp.int32, (nseq, LANES), 0)
        for way in range(2):
            chunk = jnp.ones((SUB, LANES), F32)
            for s in range(S):
                chunk = chunk * r.keep[way, s * SUB : (s + 1) * SUB, :]
            for level in range(3):
                delta = 1 << level
                if way == 0:
                    inside, rolled = k8 >= delta, pltpu.roll(chunk, delta, 0)
                else:
                    inside, rolled = k8 < SUB - delta, pltpu.roll(chunk, SUB - delta, 0)
                r.chunk_keep[way, level] = jnp.where(inside, chunk, 0.0)
                chunk = jnp.where(inside, chunk * rolled, chunk)
            if way == 0:
                before = jnp.where(k8 >= 1, pltpu.roll(chunk, 1, 0), 1.0)
                chunks_before = k8
            else:
                before = jnp.where(k8 < SUB - 1, pltpu.roll(chunk, SUB - 1, 0), 1.0)
                chunks_before = SUB - 1 - k8
            whole = jnp.min(keep(there, starts if way == 0 else ends), axis=1, keepdims=True)
            whole = jnp.broadcast_to(whole, (nseq, LANES))
            gates = [None] * nseq
            running = jnp.ones((1, LANES), F32)
            for o in range(1, nseq) if way == 0 else range(nseq - 1, 0, -1):
                gates[o] = running
                running = running * whole[o : o + 1, :]
            gates[0] = jnp.zeros((1, LANES), F32)
            gate = jnp.concatenate(gates, axis=0)
            if way == 0:
                valid = (n_row >= 1) & (n_row <= seq)
                hops = n_row - 1
            else:
                valid = n_row > seq
                hops = nseq - 1 - n_row
            gate = jnp.where(valid, gate, 0.0)
            hops = jnp.where(valid, hops, 0)
            for l in range(2):
                index = (0, 2)[l] if way == 0 else (3, 1)[l]
                sign = 1.0 if index < 2 else -1.0
                pre, pim = power_rows(l, step_bits, chunks_before, 3)
                r.chunk_table[index, :, 0:N] = pre * wide(before, N)
                r.chunk_table[index, :, N:W] = pim * wide(before, N) * sign
                pre, pim = power_rows(l, seg_bits, hops, (nseq - 1).bit_length())
                r.seq_table[index, :, 0:N] = pre * wide(gate, N)
                r.seq_table[index, :, N:W] = pim * wide(gate, N) * sign
        for index in range(4):
            r.carry_in[index, 0] = jnp.zeros((1, W), F32)

        def scan(index, l, way, conj, source, between, sink):
            bre, bim = disc[l].bar_re, disc[l].bar_im
            sign = -1.0 if conj else 1.0
            bre = jnp.broadcast_to(bre, (SUB, N))
            bim = jnp.broadcast_to(bim * sign, (SUB, N))
            order = list(range(S)) if way == 0 else list(range(S - 1, -1, -1))

            def advance(s, yre, yim, dre, dim):
                k = wide(r.keep[way, s * SUB : (s + 1) * SUB, :], N)
                pre, pim = cmul(bre, bim, yre * k, yim * k)
                return pre + dre, pim + dim

            yre = jnp.zeros((SUB, N), F32)
            yim = jnp.zeros((SUB, N), F32)
            for s in order:
                dre, dim = source(s, True)
                yre, yim = advance(s, yre, yim, dre, dim)
            for level in range(3):
                delta = 1 << level
                shift = delta if way == 0 else SUB - delta
                m = wide(r.chunk_keep[way, level], N)
                pre, pim = powers[l][step_bits + level]
                gre, gim = cmul(pre, pim * sign, pltpu.roll(yre, shift, 0) * m, pltpu.roll(yim, shift, 0) * m)
                yre, yim = yre + gre, yim + gim
            last = SUB - 1 if way == 0 else 0
            r.carry_out[index, 0:1, 0:N] = yre[last : last + 1, :]
            r.carry_out[index, 0:1, N:W] = yim[last : last + 1, :]
            if index == 0:
                pl.semaphore_wait(barrier, len(greeted))
            copies = [
                wire.send(r.carry_out.at[index], r.carry_in.at[index, o], {"seq": (seq + o) % nseq})
                for o in range(1, nseq)
            ]
            edge = wide(k8 >= 1 if way == 0 else k8 < SUB - 1, N)
            shift = 1 if way == 0 else SUB - 1
            yre = jnp.where(edge, pltpu.roll(yre, shift, 0), 0.0)
            yim = jnp.where(edge, pltpu.roll(yim, shift, 0), 0.0)
            between()
            for copy in copies:
                copy.wait_recv()
            got = r.carry_in[index, :, 0, :]
            gre, gim = cmul(got[:, 0:N], got[:, N:W], r.seq_table[index, :, 0:N], r.seq_table[index, :, N:W])
            gre = jnp.sum(gre, axis=0, keepdims=True)
            gim = jnp.sum(gim, axis=0, keepdims=True)
            gre, gim = cmul(gre, gim, r.chunk_table[index, :, 0:N], r.chunk_table[index, :, N:W])
            yre, yim = yre + gre, yim + gim
            if not conj:
                r.x_first[l, :, 0:N] = yre
                r.x_first[l, :, N:W] = yim
            held = None
            for s in order:
                dre, dim = source(s, False)
                yre, yim = advance(s, yre, yim, dre, dim)
                out = sink(s, yre, yim)
                if held is None:
                    held = out
                else:
                    pair = (held, out) if way == 0 else (out, held)
                    first = s - 1 if way == 0 else s
                    for c in range(2):
                        both = jnp.concatenate([pair[0][c], pair[1][c]], axis=0).astype(LOW)
                        dest, at = sink.dest
                        dest[l, first * SUB : (first + 2) * SUB, at + c * N : at + (c + 1) * N] = both
                    held = None

        def chunks(body, init=0, unroll=2):
            def step(i, carry):
                return body(pl.ds(pl.multiple_of(i * BLOCK, BLOCK), BLOCK), carry)

            return lax.fori_loop(0, T // BLOCK, step, init, unroll=unroll)

        def turn(l, value_ref, lt, rt):
            for j in range(H // LANES):
                block = value_ref[:, j * LANES : (j + 1) * LANES].T
                lt[l, 4 * j : 4 * j + 4] = block.reshape(4, 2, BLOCK, LANES)
            if fused:
                return wire.send(lt.at[l, :, 1 - core], rt.at[l], sibling)

        def share(l, ref, first, last):
            if fused:
                return wire.send(
                    ref.at[l, 0:T, first:last], ref.at[l, T : 2 * T, first:last], sibling
                )

        def outer(l, lt, rt, right, first, last, dest, waits, at):
            if fused:
                for copy in waits:
                    copy.wait_recv()
                mine = lt[l, :, core].reshape(H // 2, LANES)
                left = jnp.concatenate([mine, rt[l].reshape(H // 2, LANES)], axis=1)
                for c in range(first, last, 256):
                    g = mm(left, right[l, :, c : c + 256]).astype(LOW)
                    dest[l, :, :, :, :, c : c + 256] = g.reshape(nz, 2, 2, BLOCK, 256)
            else:
                left = lt[l].reshape(H, LANES)
                for c in range(first, last, 256):
                    r.matrix_sums[l, :, at + c - first : at + c - first + 256] = mm(
                        left, right[l, 0:T, c : c + 256]
                    )

        def rs_start(l, u):
            half = u.p.shape[-1] // 2
            u.first[l] = (
                wire.send(u.p.at[l, :, 1 - xx, :, :, 0:half], u.r1.at[l, 0], x_peer),
                wire.send(u.p.at[l, :, :, 1 - yy, :, half : 2 * half], u.r1.at[l, 1], y_peer),
            )

        def rs_second(l, u):
            half = u.p.shape[-1] // 2
            u.first[l][0].wait_recv()
            for q in range(nz):
                u.s1[l, 0, q] = u.p[l, q, xx, :, :, 0:half] + u.r1[l, 0, q]
            to_y = wire.send(u.s1.at[l, 0, :, 1 - yy], u.r2.at[l, 0], y_peer)
            u.first[l][1].wait_recv()
            for q in range(nz):
                u.s1[l, 1, q] = u.p[l, q, :, yy, :, half : 2 * half] + u.r1[l, 1, q]
            to_x = wire.send(u.s1.at[l, 1, :, 1 - xx], u.r2.at[l, 1], x_peer)
            u.second[l] = (to_y, to_x)

        def rs_third(l, u):
            u.third[l] = []
            for part, mine in ((0, yy), (1, xx)):
                u.second[l][part].wait_recv()
                u.s2[l, part] = u.s1[l, part, :, mine] + u.r2[l, part]
                for o in range(1, nz):
                    to = (zz + o) % nz
                    u.third[l].append(
                        wire.send(
                            u.s2.at[l, part, to], u.r3.at[l, part, o - 1], {"seq": to * 2 + xx}
                        )
                    )

        def rs_end(l, u):
            for copy in u.third[l]:
                copy.wait_recv()
            halves = []
            for part in range(2):
                value = u.s2[l, part, zz].astype(F32)
                for o in range(1, nz):
                    value = value + u.r3[l, part, o - 1].astype(F32)
                halves.append(value)
            return jnp.concatenate(halves, axis=1)

        def vec_start(l):
            r.vec_copy[l] = wire.send(r.vec.at[l, 0], r.vec_in.at[l, 0], sibling)

        def vec_next(l, stage):
            r.vec_copy[l].wait_recv()
            r.vec[l, stage] = r.vec[l, stage - 1] + r.vec_in[l, stage - 1]
            r.vec_copy[l] = wire.send(
                r.vec.at[l, stage], r.vec_in.at[l, stage], (sibling, x_peer, y_peer)[stage]
            )

        def vec_last(l):
            r.vec_copy[l].wait_recv()
            total = r.vec[l, 2] + r.vec_in[l, 2]
            r.vec_z[l, zz] = total
            r.vec_copy[l] = [
                wire.send(
                    r.vec_z.at[l, zz], r.vec_z.at[l, zz], {"seq": ((zz + o) % nz) * 2 + xx}
                )
                for o in range(1, nz)
            ]

        def vec_end(l):
            for copy in r.vec_copy[l]:
                copy.wait_recv()
            total = r.vec_z[l, 0]
            for o in range(1, nz):
                total = total + r.vec_z[l, o]
            return total

        r.vec_copy = [None, None]
        early = late = None
        if fused:
            early = types.SimpleNamespace(p=r.p_e, r1=r.r1_e, s1=r.s1_e, r2=r.r2_e, s2=r.s2_e, r3=r.r3_e, first={}, second={}, third={})
            late = types.SimpleNamespace(p=r.p_n, r1=r.r1_n, s1=r.s1_n, r2=r.r2_n, s2=r.s2_n, r3=r.r3_n, first={}, second={}, third={})
        waits = {}

        def gain(l):
            return r.norm_gain[l : l + 1, :]

        def skip(l):
            return r.skip_gain[l : l + 1, :]

        def forward_in(l):
            def norm(rows, carry):
                u = r.u[l, rows, :]
                inv = lax.rsqrt(jnp.mean(u * u, axis=1, keepdims=True) + EPS)
                normed = u * inv * gain(l)
                r.inv[l, rows, :] = jnp.broadcast_to(inv, (BLOCK, LANES))
                r.normed[l, rows, :] = normed
                r.normed_low[l, rows, :] = normed.astype(LOW)
                return carry

            chunks(norm)
            loads[f"wi{l}"].wait()
            r.proj[l] = mm(r.normed_low[l], r.wi[l])

        def states(l, between):
            cre = jnp.broadcast_to(disc[l].coef_re, (SUB, N))
            cim = jnp.broadcast_to(disc[l].coef_im, (SUB, N))

            def source(s, first):
                rows = slice(s * SUB, (s + 1) * SUB)
                if first:
                    dre, dim = cmul(cre, cim, r.proj[l, rows, 0:N], r.proj[l, rows, N:W])
                    r.drive[rows, 0:N] = dre
                    r.drive[rows, N:W] = dim
                    return dre, dim
                return r.drive[rows, 0:N], r.drive[rows, N:W]

            def sink(s, yre, yim):
                rows = slice(s * SUB, (s + 1) * SUB)
                r.x[l, rows, 0:N] = yre
                r.x[l, rows, N:W] = yim
                return yre, yim

            sink.dest = (r.right_e, H)
            scan(l, l, l, False, source, between, sink)

        def forward_out(l):
            waits["x", l] = share(l, r.right_e, H, CE)
            loads[f"wo{l}"].wait()
            r.mixed[l] = mm(r.right_e[l, 0:T, H:CE], r.wo[l])

            def gelu(rows, carry):
                mixed = r.mixed[l, rows, :] + skip(l) * r.normed[l, rows, :]
                th = jnp.tanh(GELU_A * (mixed + GELU_B * (mixed * mixed * mixed)))
                r.mixed[l, rows, :] = mixed
                r.th[l, rows, :] = th
                r.act_low[l, rows, :] = (0.5 * mixed * (1.0 + th)).astype(LOW)
                return carry

            chunks(gelu)
            loads[f"wg{l}"].wait()
            r.gate[l] = mm(r.act_low[l], r.wg[l])

            def out(rows, carry):
                gate = jax.nn.sigmoid(r.gate[l, rows, :] + r.glu_bias[l : l + 1, :])
                r.gate[l, rows, :] = gate
                act = 0.5 * r.mixed[l, rows, :] * (1.0 + r.th[l, rows, :])
                value = r.u[l, rows, :] + act * gate
                if l == 0:
                    r.u[1, rows, :] = value
                else:
                    r.act_out[rows, :] = value.astype(LOW)
                return carry

            chunks(out)

        def backward_in(l):
            def glu(rows, bias):
                g = r.og[rows, :]
                gate = r.gate[l, rows, :]
                act = 0.5 * r.mixed[l, rows, :] * (1.0 + r.th[l, rows, :])
                gate_grad = (g * act * gate * (1.0 - gate)).astype(LOW)
                r.right_e[l, rows, 0:H] = gate_grad
                wide_grad = gate_grad.astype(F32)
                return bias + wide_grad[0:SUB] + wide_grad[SUB:BLOCK]

            bias = chunks(glu, jnp.zeros((SUB, H), F32))
            r.vec[l, 0, 2:3, :] = jnp.sum(bias, axis=0, keepdims=True)
            waits["gate", l] = share(l, r.right_e, 0, H)
            r.tmp[...] = mm_nt(r.right_e[l, 0:T, 0:H], r.wg[l])

            def gelu(rows, total):
                act_grad = r.og[rows, :] * r.gate[l, rows, :] + r.tmp[rows, :]
                mixed, th = r.mixed[l, rows, :], r.th[l, rows, :]
                inner = GELU_A * (1.0 + 3.0 * GELU_B * mixed * mixed)
                slope = 0.5 * (1.0 + th) + 0.5 * mixed * (1.0 - th * th) * inner
                low = (act_grad * slope).astype(LOW)
                r.mixed_grad[l, rows, :] = low
                part = low.astype(F32) * r.normed[l, rows, :]
                return total + part[0:SUB] + part[SUB:BLOCK]

            total = chunks(gelu, jnp.zeros((SUB, H), F32))
            r.vec[l, 0, 0:1, :] = jnp.sum(total, axis=0, keepdims=True)
            r.xg[...] = mm_nt(r.mixed_grad[l], r.wo[l])

        def adjoints(l, between):
            d = disc[l]
            cre = jnp.broadcast_to(d.coef_re, (SUB, N))
            cim = jnp.broadcast_to(d.coef_im, (SUB, N))
            way = 1 - l
            sums = [jnp.zeros((SUB, N), F32) for _ in range(4)]

            def source(s, first):
                rows = slice(s * SUB, (s + 1) * SUB)
                return r.xg[rows, 0:N], r.xg[rows, N:W]

            def sink(s, are, aim):
                rows = slice(s * SUB, (s + 1) * SUB)
                at = s - 1 if l == 0 else s + 1
                if 0 <= at < S:
                    old = slice(at * SUB, (at + 1) * SUB)
                    xre, xim = r.x[l, old, 0:N], r.x[l, old, N:W]
                else:
                    xre, xim = r.x_first[l, :, 0:N], r.x_first[l, :, N:W]
                k = wide(r.keep[l, rows, :], N)
                xre, xim = xre * k, xim * k
                pre, pim = r.proj[l, rows, 0:N], r.proj[l, rows, N:W]
                sums[0] = sums[0] + (are * xre + aim * xim)
                sums[1] = sums[1] + (aim * xre - are * xim)
                sums[2] = sums[2] + (are * pre + aim * pim)
                sums[3] = sums[3] + (aim * pre - are * pim)
                return cre * are + cim * aim, cre * aim - cim * are

            sink.dest = (r.right_n, 0)
            scan(3 - l, l, way, True, source, between, sink)
            pad = jnp.zeros((1, H - N), F32)
            for i in range(4):
                value = jnp.sum(sums[i], axis=0, keepdims=True)
                r.vec[l, 0, 3 + i : 4 + i, :] = jnp.concatenate([value, pad], axis=1)

        def backward_out(l):
            waits["pg", l] = share(l, r.right_n, 0, W)
            r.tmp[...] = mm_nt(r.right_n[l, 0:T, :], r.wi[l])

            def norm(rows, total):
                u = r.u[l, rows, :]
                inv = wide(r.inv[l, rows, :], H)
                ng = r.tmp[rows, :] + skip(l) * r.mixed_grad[l, rows, :].astype(F32)
                v = gain(l) * ng
                uv = jnp.mean(u * v, axis=1, keepdims=True)
                out = r.og[rows, :] + inv * v - u * (inv * inv * inv) * uv
                r.og[rows, :] = out
                part = ng * u * inv
                return total + part[0:SUB] + part[SUB:BLOCK]

            total = chunks(norm, jnp.zeros((SUB, H), F32))
            r.vec[l, 0, 1:2, :] = jnp.sum(total, axis=0, keepdims=True)
            r.vec[l, 0, 7:8, :] = jnp.zeros((1, H), F32)

        loads["tok"].wait()
        at = lax.broadcasted_iota(jnp.int32, (T, T), 0)
        of = lax.broadcasted_iota(jnp.int32, (T, T), 1)
        to_rows = jnp.where(of == (at % SUB) * S + at // SUB, 1.0, 0.0).astype(LOW)
        to_time = jnp.where(at == (of % SUB) * S + of // SUB, 1.0, 0.0).astype(LOW)
        r.u[0] = mm(to_rows, r.tok[...])
        forward_in(0)

        def fill0():
            waits["ln", 0] = turn(0, r.normed_low.at[0], r.lt_n, r.rt_n)

        states(0, fill0)
        forward_out(0)

        forward_in(1)

        def fill1():
            waits["lg", 0] = turn(0, r.act_low.at[0], r.lt_g, r.rt_g)
            waits["ln", 1] = turn(1, r.normed_low.at[1], r.lt_n, r.rt_n)
            loads["cot"].wait()
            r.og[...] = mm(to_rows, r.cot[...])

        states(1, fill1)
        forward_out(1)
        backward_in(1)

        def early_products(l):
            outer(l, r.lt_g, r.rt_g, r.right_e, 0, H, early and early.p, (waits["lg", l], waits["gate", l]), 0)
            outer(l, r.lt_o, r.rt_o, r.right_e, H, CE, early and early.p, (waits["lo", l], waits["x", l]), H)
            if fused:
                rs_start(l, early)

        def late_products(l):
            outer(l, r.lt_n, r.rt_n, r.right_n, 0, W, late and late.p, (waits["ln", l], waits["pg", l]), CE)
            if fused:
                rs_start(l, late)

        def fill2():
            waits["lo", 1] = turn(1, r.mixed_grad.at[1], r.lt_o, r.rt_o)
            waits["lg", 1] = turn(1, r.act_low.at[1], r.lt_g, r.rt_g)
            r.activations[...] = mm(to_time, r.act_out[...]).astype(LOW)
            early_products(1)

        adjoints(1, fill2)
        backward_out(1)
        if fused:
            vec_start(1)
        late_products(1)
        backward_in(0)

        def fill3():
            waits["lo", 0] = turn(0, r.mixed_grad.at[0], r.lt_o, r.rt_o)
            if fused:
                rs_second(1, early)
                vec_next(1, 1)
            early_products(0)
            if fused:
                rs_second(1, late)
                vec_next(1, 2)
                rs_third(1, early)

        adjoints(0, fill3)
        backward_out(0)
        if fused:
            vec_start(0)
        late_products(0)

        for s in range(S):
            for j in range(H // LANES):
                r.tokens_grad[pl.ds(s * (H // LANES) + j, SUB, stride=S * (H // LANES)), :] = r.og[
                    s * SUB : (s + 1) * SUB, j * LANES : (j + 1) * LANES
                ]

        if not fused:
            r.vector_sums[...] = r.vec[:, 0]
            wire.close()
            return

        rs_third(1, late)
        vec_last(1)
        rs_second(0, early)
        vec_next(0, 1)
        rs_second(0, late)
        vec_next(0, 2)
        rs_third(0, early)
        rs_third(0, late)
        vec_last(0)
        device = seq * nblk + blk
        for l in (1, 0):
            g = rs_end(l, early)
            r.glu_weight_grad[l] = g[:, 0:H]
            r.out_proj_grad[l, 0] = g[:, H : H + N]
            r.out_proj_grad[l, 1] = g[:, H + N : CE]
            g = rs_end(l, late)
            for c in range(2):
                r.in_proj_grad[l, :, c, :] = g[:, c * N : (c + 1) * N]
            total = vec_end(l)
            mine = pltpu.roll(total, (H - device * BLOCK) % H, 1)[:, 0:BLOCK]
            r.skip_gain_grad[l : l + 1, :] = mine[0:1]
            r.norm_gain_grad[l : l + 1, :] = mine[1:2]
            r.glu_bias_grad[l : l + 1, :] = mine[2:3]
            grads = discretize_grad(disc[l], *(total[3 + i : 4 + i, 0:N] for i in range(4)))
            r.decay_log_grad[l : l + 1, :] = grads[0]
            r.frequency_grad[l : l + 1, :] = grads[1]
            r.step_log_grad[l : l + 1, :] = grads[2]
        wire.close()

    return kernel


def solution(mesh):
    nseq, nblk = mesh.shape["seq"], mesh.shape["blk"]

    def on_device(
        tokens, lengths, norm_gain, in_proj, out_proj, skip_gain,
        glu_weight, glu_bias, decay_log, frequency, step_log, cotangent,
    ):
        T, streams, H = tokens.shape
        N = decay_log.shape[1]
        W = 2 * N
        CE = H + W
        assert streams == 1 and T == LANES and H == 512
        fused = nseq == 8 and nblk == 4
        z = types.SimpleNamespace(T=T, H=H, N=N, S=T // SUB, nseq=nseq, nblk=nblk, fused=fused)
        any_space = pl.BlockSpec(memory_space=pl.ANY)
        vmem = pl.BlockSpec(memory_space=pltpu.VMEM)
        smem = pl.BlockSpec(memory_space=pltpu.SMEM)
        operands = {
            "tokens": (tokens.reshape(T, H), any_space),
            "lengths": (lengths, smem),
            "norm_gain": (norm_gain, vmem),
            "in_proj": (in_proj.reshape(2, H, W), any_space),
            "out_proj": (out_proj.reshape(2, W, H), any_space),
            "skip_gain": (skip_gain, vmem),
            "glu_weight": (glu_weight, any_space),
            "glu_bias": (glu_bias, vmem),
            "decay_log": (decay_log, vmem),
            "frequency": (frequency, vmem),
            "step_log": (step_log, vmem),
            "cotangent": (cotangent.reshape(T, H), any_space),
        }
        results = {
            "activations": ((T, H), LOW),
            "tokens_grad": ((T * H // LANES, LANES), F32),
        }
        if fused:
            results |= {
                "norm_gain_grad": ((2, BLOCK), F32),
                "in_proj_grad": ((2, BLOCK, 2, N), F32),
                "out_proj_grad": ((2, 2, BLOCK, N), F32),
                "skip_gain_grad": ((2, BLOCK), F32),
                "glu_weight_grad": ((2, BLOCK, H), F32),
                "glu_bias_grad": ((2, BLOCK), F32),
                "decay_log_grad": ((2, N), F32),
                "frequency_grad": ((2, N), F32),
                "step_log_grad": ((2, N), F32),
            }
        else:
            results |= {"matrix_sums": ((2, H, CE + W), F32), "vector_sums": ((2, 8, H), F32)}
        dma = pltpu.SemaphoreType.DMA
        scratch = {
            "wi": pltpu.VMEM((2, H, W), LOW),
            "wo": pltpu.VMEM((2, W, H), LOW),
            "wg": pltpu.VMEM((2, H, H), LOW),
            "tok": pltpu.VMEM((T, H), LOW),
            "cot": pltpu.VMEM((T, H), LOW),
            "u": pltpu.VMEM((2, T, H), F32),
            "inv": pltpu.VMEM((2, T, LANES), F32),
            "normed": pltpu.VMEM((2, T, H), F32),
            "normed_low": pltpu.VMEM((2, T, H), LOW),
            "proj": pltpu.VMEM((2, T, W), F32),
            "drive": pltpu.VMEM((T, W), F32),
            "x": pltpu.VMEM((2, T, W), F32),
            "x_first": pltpu.VMEM((2, SUB, W), F32),
            "mixed": pltpu.VMEM((2, T, H), F32),
            "th": pltpu.VMEM((2, T, H), F32),
            "gate": pltpu.VMEM((2, T, H), F32),
            "act_low": pltpu.VMEM((2, T, H), LOW),
            "act_out": pltpu.VMEM((T, H), LOW),
            "og": pltpu.VMEM((T, H), F32),
            "tmp": pltpu.VMEM((T, H), F32),
            "xg": pltpu.VMEM((T, W), F32),
            "mixed_grad": pltpu.VMEM((2, T, H), LOW),
            "right_e": pltpu.VMEM((2, 2 * T, CE), LOW),
            "right_n": pltpu.VMEM((2, 2 * T, W), LOW),
            "keep": pltpu.VMEM((2, T, LANES), F32),
            "chunk_keep": pltpu.VMEM((2, 3, SUB, LANES), F32),
            "chunk_table": pltpu.VMEM((4, SUB, W), F32),
            "seq_table": pltpu.VMEM((4, nseq, W), F32),
            "carry_out": pltpu.VMEM((4, 1, W), F32),
            "carry_in": pltpu.VMEM((4, nseq, 1, W), F32),
            "vec": pltpu.VMEM((2, 3, 8, H), F32),
        }
        for name in "gon":
            scratch[f"lt_{name}"] = pltpu.VMEM((2, H // 32, 2, BLOCK, LANES), LOW)
            scratch[f"rt_{name}"] = pltpu.VMEM((2, H // 32, BLOCK, LANES), LOW)
        if fused:
            nz = nseq // 2
            for name, width in (("e", CE), ("n", W)):
                half = width // 2
                scratch[f"p_{name}"] = pltpu.VMEM((2, nz, 2, 2, BLOCK, width), LOW)
                scratch[f"r1_{name}"] = pltpu.VMEM((2, 2, nz, 2, BLOCK, half), LOW)
                scratch[f"s1_{name}"] = pltpu.VMEM((2, 2, nz, 2, BLOCK, half), LOW)
                scratch[f"r2_{name}"] = pltpu.VMEM((2, 2, nz, BLOCK, half), LOW)
                scratch[f"s2_{name}"] = pltpu.VMEM((2, 2, nz, BLOCK, half), LOW)
                scratch[f"r3_{name}"] = pltpu.VMEM((2, 2, nz - 1, BLOCK, half), LOW)
            scratch["vec_in"] = pltpu.VMEM((2, 3, 8, H), F32)
            scratch["vec_z"] = pltpu.VMEM((2, nz, 8, H), F32)
        links = LINKS if fused else 4 * (nseq - 1)
        scratch["send_sems"] = dma((links,))
        scratch["recv_sems"] = dma((links,))
        scratch["load_sems"] = dma((8,))
        names = list(operands) + list(results) + list(scratch)
        outs = pl.pallas_call(
            make_kernel(names, z),
            out_shape=[jax.ShapeDtypeStruct(*v) for v in results.values()],
            in_specs=[spec for _, spec in operands.values()],
            out_specs=[vmem] * len(results),
            scratch_shapes=list(scratch.values()),
            compiler_params=pltpu.CompilerParams(
                collective_id=0, has_side_effects=True, vmem_limit_bytes=48 * 2**20
            ),
            name="two_layers",
        )(*(value for value, _ in operands.values()))
        o = types.SimpleNamespace(**dict(zip(results, outs)))
        activations = o.activations.reshape(T, 1, H)
        tokens_grad = o.tokens_grad.reshape(T, 1, H)
        if fused:
            return (
                activations, tokens_grad, o.norm_gain_grad, o.in_proj_grad,
                jnp.swapaxes(o.out_proj_grad, 2, 3), o.skip_gain_grad, o.glu_weight_grad,
                o.glu_bias_grad, o.decay_log_grad, o.frequency_grad, o.step_log_grad,
            )
        both = ("seq", "blk")
        sums = lax.psum_scatter(o.matrix_sums, both, scatter_dimension=1, tiled=True)
        rows = sums.shape[1]
        vectors = lax.psum(o.vector_sums, both)
        mine = lax.dynamic_slice_in_dim(vectors, lax.axis_index(both) * rows, rows, 2)
        grads = discretize_grad(
            discretize(decay_log, frequency, step_log), *(vectors[:, 3 + i, 0:N] for i in range(4))
        )
        return (
            activations, tokens_grad, mine[:, 1], sums[:, :, CE:].reshape(2, rows, 2, N),
            jnp.moveaxis(sums[:, :, H:CE].reshape(2, rows, 2, N), 1, 3), mine[:, 0], sums[:, :, 0:H],
            mine[:, 2], *grads,
        )

    split = P("seq", "blk", None)
    owned = ("seq", "blk")
    return jax.shard_map(
        on_device,
        mesh=mesh,
        in_specs=(split,) + (P(),) * 10 + (split,),
        out_specs=(
            split, split, P(None, owned), P(None, owned, None, None), P(None, None, None, owned),
            P(None, owned), P(None, owned, None), P(None, owned), P(), P(), P(),
        ),
        check_vma=False,
    )
```

```python
import types

import jax
import jax.numpy as jnp
from jax import lax
from jax.experimental import pallas as pl
from jax.experimental.pallas import tpu as pltpu
from jax.sharding import PartitionSpec as P

EPS = 1e-6
F32 = jnp.float32
LOW = jnp.bfloat16
GELU_A = 0.7978845608028654
GELU_B = 0.044715
LANES = 128
SUB = 8
BLOCK = 16
LINKS = 112


def cmul(are, aim, bre, bim):
    return are * bre - aim * bim, are * bim + aim * bre


def expm1(value):
    series = jnp.ones_like(value)
    for order in range(9, 1, -1):
        series = 1.0 + value * series * (1.0 / order)
    return jnp.where(value > -0.35, value * series, jnp.exp(value) - 1.0)


def discretize(decay, freq, step_log):
    lam_re = -jnp.exp(decay)
    step = jnp.exp(step_log)
    rotation = freq * step
    shrink = expm1(lam_re * step)
    cosine, sine = jnp.cos(rotation), jnp.sin(rotation)
    half = jnp.sin(0.5 * rotation)
    bar_re = (shrink + 1.0) * cosine
    bar_im = (shrink + 1.0) * sine
    minus_re = shrink * cosine - 2.0 * half * half
    scale = 1.0 / (lam_re * lam_re + freq * freq)
    coef_re = (minus_re * lam_re + bar_im * freq) * scale
    coef_im = (bar_im * lam_re - minus_re * freq) * scale
    return types.SimpleNamespace(
        lam_re=lam_re, freq=freq, step=step, scale=scale,
        bar_re=bar_re, bar_im=bar_im, coef_re=coef_re, coef_im=coef_im,
    )


def discretize_grad(d, bar_gre, bar_gim, coef_gre, coef_gim):
    over_re, over_im = d.lam_re * d.scale, d.freq * d.scale
    part_re, part_im = cmul(coef_gre, coef_gim, over_re, over_im)
    all_re, all_im = bar_gre + part_re, bar_gim + part_im
    one_re, one_im = cmul(all_re, all_im, d.bar_re, -d.bar_im)
    two_re, two_im = cmul(part_re, part_im, d.coef_re, -d.coef_im)
    lam_gre = one_re * d.step - two_re
    lam_gim = one_im * d.step - two_im
    step_g = one_re * d.lam_re + one_im * d.freq
    return lam_gre * d.lam_re, lam_gim, step_g * d.step


def mm(a, b):
    return jnp.dot(a, b, preferred_element_type=F32)


def mm_nt(a, b):
    return lax.dot_general(a, b, (((1,), (1,)), ((), ())), preferred_element_type=F32)


def wide(mask, width):
    return jnp.concatenate([mask] * (width // LANES), axis=1)


class Wire:
    def __init__(self, send_sems, recv_sems):
        self.send_sems, self.recv_sems = send_sems, recv_sems
        self.count = 0
        self.open = []

    def send(self, src, dst, device):
        at = self.count
        self.count += 1
        copy = pltpu.make_async_remote_copy(
            src_ref=src, dst_ref=dst,
            send_sem=self.send_sems.at[at], recv_sem=self.recv_sems.at[at],
            device_id=device, device_id_type=pl.DeviceIdType.MESH,
        )
        copy.start()
        self.open.append(copy)
        return copy

    def close(self):
        for copy in self.open:
            copy.wait_send()


def hand_out(*refs):
    count = len(refs) // 2
    copies = [
        pltpu.make_async_copy(refs[i], refs[count + i], refs[-1].at[i]) for i in range(count)
    ]
    for copy in copies:
        copy.start()
    for copy in copies:
        copy.wait()


def make_kernel(names, z):
    T, H, N, S, nseq, nblk, fused = z.T, z.H, z.N, z.S, z.nseq, z.nblk, z.fused
    W = 2 * N
    CE = H + W

    def kernel(*refs):
        r = types.SimpleNamespace(**dict(zip(names, refs, strict=True)))
        seq = lax.axis_index("seq")
        blk = lax.axis_index("blk")
        wire = Wire(r.send_sems, r.recv_sems)
        core, yy = blk % 2, blk // 2
        xx, zz = seq % 2, seq // 2
        nz = nseq // 2
        sibling = {"blk": yy * 2 + (1 - core)}
        y_peer = {"blk": (1 - yy) * 2 + core}
        x_peer = {"seq": zz * 2 + (1 - xx)}

        loads = {}

        def load(name, src, dst):
            copy = pltpu.make_async_copy(src, dst, r.load_sems.at[len(loads)])
            copy.start()
            loads[name] = copy

        load("tok", r.tokens, r.tok)
        load("wi0", r.in_proj.at[0], r.wi_raw.at[0])
        load("wo0", r.out_proj.at[0], r.wo.at[0])
        load("wg0", r.glu_weight.at[0], r.wg.at[0])
        load("wi1", r.in_proj.at[1], r.wi_raw.at[1])
        load("wo1", r.out_proj.at[1], r.wo.at[1])
        load("wg1", r.glu_weight.at[1], r.wg.at[1])
        load("cot", r.cotangent, r.cot)

        barrier = pltpu.get_barrier_semaphore()
        greeted = [{"seq": (seq + o) % nseq} for o in range(1, nseq)]
        if fused:
            greeted += [sibling, y_peer]
        for device in greeted:
            pl.semaphore_signal(barrier, inc=1, device_id=device, device_id_type=pl.DeviceIdType.MESH)

        disc, powers = [], []
        for l in range(2):
            d = discretize(
                r.decay_log[l : l + 1, :], r.frequency[l : l + 1, :], r.step_log[l : l + 1, :]
            )
            disc.append(d)
            chain = [(d.bar_re, d.bar_im)]
            while len(chain) < 12:
                chain.append(cmul(*chain[-1], *chain[-1]))
            powers.append(chain)
        step_bits = S.bit_length() - 1
        seg_bits = T.bit_length() - 1

        def power_rows(l, first, exponent, bits):
            rows = exponent.shape[0]
            out_re = jnp.ones((rows, N), F32)
            out_im = jnp.zeros((rows, N), F32)
            for bit in range(bits):
                use = wide(((exponent >> bit) & 1) == 1, N)
                pre, pim = powers[l][first + bit]
                new_re, new_im = cmul(out_re, out_im, pre, pim)
                out_re = jnp.where(use, new_re, out_re)
                out_im = jnp.where(use, new_im, out_im)
            return out_re, out_im

        ends, starts = [], []
        total = jnp.int32(0)
        for i in range(r.lengths.shape[1]):
            starts.append(total)
            total = total + r.lengths[blk, i]
            ends.append(total - 1)

        def keep(position, marks):
            hit = position == marks[0]
            for mark in marks[1:]:
                hit = hit | (position == mark)
            return jnp.where(hit, 0.0, 1.0).astype(F32)

        row = lax.broadcasted_iota(jnp.int32, (T, LANES), 0)
        here = seq * T + (row % SUB) * S + row // SUB
        r.keep[0] = keep(here, starts)
        r.keep[1] = keep(here, ends)
        offset = lax.broadcasted_iota(jnp.int32, (nseq, T), 0)
        lane = lax.broadcasted_iota(jnp.int32, (nseq, T), 1)
        there = ((seq - offset + nseq) % nseq) * T + lane
        k8 = lax.broadcasted_iota(jnp.int32, (SUB, LANES), 0)
        n_row = lax.broadcasted_iota(jnp.int32, (nseq, LANES), 0)
        for way in range(2):
            chunk = jnp.ones((SUB, LANES), F32)
            for s in range(S):
                chunk = chunk * r.keep[way, s * SUB : (s + 1) * SUB, :]
            for level in range(3):
                delta = 1 << level
                if way == 0:
                    inside, rolled = k8 >= delta, pltpu.roll(chunk, delta, 0)
                else:
                    inside, rolled = k8 < SUB - delta, pltpu.roll(chunk, SUB - delta, 0)
                r.chunk_keep[way, level] = jnp.where(inside, chunk, 0.0)
                chunk = jnp.where(inside, chunk * rolled, chunk)
            if way == 0:
                before = jnp.where(k8 >= 1, pltpu.roll(chunk, 1, 0), 1.0)
                chunks_before = k8
            else:
                before = jnp.where(k8 < SUB - 1, pltpu.roll(chunk, SUB - 1, 0), 1.0)
                chunks_before = SUB - 1 - k8
            whole = jnp.min(keep(there, starts if way == 0 else ends), axis=1, keepdims=True)
            whole = jnp.broadcast_to(whole, (nseq, LANES))
            gates = [None] * nseq
            running = jnp.ones((1, LANES), F32)
            for o in range(1, nseq) if way == 0 else range(nseq - 1, 0, -1):
                gates[o] = running
                running = running * whole[o : o + 1, :]
            gates[0] = jnp.zeros((1, LANES), F32)
            gate = jnp.concatenate(gates, axis=0)
            if way == 0:
                valid = (n_row >= 1) & (n_row <= seq)
                hops = n_row - 1
            else:
                valid = n_row > seq
                hops = nseq - 1 - n_row
            gate = jnp.where(valid, gate, 0.0)
            hops = jnp.where(valid, hops, 0)
            for l in range(2):
                index = (0, 2)[l] if way == 0 else (3, 1)[l]
                sign = 1.0 if index < 2 else -1.0
                pre, pim = power_rows(l, step_bits, chunks_before, 3)
                r.chunk_table[index, :, 0:N] = pre * wide(before, N)
                r.chunk_table[index, :, N:W] = pim * wide(before, N) * sign
                pre, pim = power_rows(l, seg_bits, hops, (nseq - 1).bit_length())
                r.seq_table[index, :, 0:N] = pre * wide(gate, N)
                r.seq_table[index, :, N:W] = pim * wide(gate, N) * sign
        for index in range(4):
            r.carry_in[index, 0] = jnp.zeros((1, W), F32)

        def scan(index, l, way, conj, source, between, sink):
            bre, bim = disc[l].bar_re, disc[l].bar_im
            sign = -1.0 if conj else 1.0
            bre = jnp.broadcast_to(bre, (SUB, N))
            bim = jnp.broadcast_to(bim * sign, (SUB, N))
            order = list(range(S)) if way == 0 else list(range(S - 1, -1, -1))

            def advance(s, yre, yim, dre, dim):
                k = wide(r.keep[way, s * SUB : (s + 1) * SUB, :], N)
                pre, pim = cmul(bre, bim, yre * k, yim * k)
                return pre + dre, pim + dim

            yre = jnp.zeros((SUB, N), F32)
            yim = jnp.zeros((SUB, N), F32)
            for s in order:
                dre, dim = source(s, True)
                yre, yim = advance(s, yre, yim, dre, dim)
            for level in range(3):
                delta = 1 << level
                shift = delta if way == 0 else SUB - delta
                m = wide(r.chunk_keep[way, level], N)
                pre, pim = powers[l][step_bits + level]
                gre, gim = cmul(pre, pim * sign, pltpu.roll(yre, shift, 0) * m, pltpu.roll(yim, shift, 0) * m)
                yre, yim = yre + gre, yim + gim
            last = SUB - 1 if way == 0 else 0
            r.carry_out[index, 0:1, 0:N] = yre[last : last + 1, :]
            r.carry_out[index, 0:1, N:W] = yim[last : last + 1, :]
            if index == 0:
                pl.semaphore_wait(barrier, len(greeted))
            copies = [
                wire.send(r.carry_out.at[index], r.carry_in.at[index, o], {"seq": (seq + o) % nseq})
                for o in range(1, nseq)
            ]
            edge = wide(k8 >= 1 if way == 0 else k8 < SUB - 1, N)
            shift = 1 if way == 0 else SUB - 1
            yre = jnp.where(edge, pltpu.roll(yre, shift, 0), 0.0)
            yim = jnp.where(edge, pltpu.roll(yim, shift, 0), 0.0)
            between()
            for copy in copies:
                copy.wait_recv()
            got = r.carry_in[index, :, 0, :]
            gre, gim = cmul(got[:, 0:N], got[:, N:W], r.seq_table[index, :, 0:N], r.seq_table[index, :, N:W])
            gre = jnp.sum(gre, axis=0, keepdims=True)
            gim = jnp.sum(gim, axis=0, keepdims=True)
            gre, gim = cmul(gre, gim, r.chunk_table[index, :, 0:N], r.chunk_table[index, :, N:W])
            yre, yim = yre + gre, yim + gim
            if not conj:
                r.x_first[l, :, 0:N] = yre
                r.x_first[l, :, N:W] = yim
            held = None
            for s in order:
                dre, dim = source(s, False)
                yre, yim = advance(s, yre, yim, dre, dim)
                out = sink(s, yre, yim)
                if held is None:
                    held = out
                else:
                    pair = (held, out) if way == 0 else (out, held)
                    first = s - 1 if way == 0 else s
                    for c in range(2):
                        both = jnp.concatenate([pair[0][c], pair[1][c]], axis=0).astype(LOW)
                        dest, at = sink.dest
                        dest[l, first * SUB : (first + 2) * SUB, at + c * N : at + (c + 1) * N] = both
                    held = None

        def chunks(body, init=0, unroll=2):
            def step(i, carry):
                return body(pl.ds(pl.multiple_of(i * BLOCK, BLOCK), BLOCK), carry)

            return lax.fori_loop(0, T // BLOCK, step, init, unroll=unroll)

        def turn(l, value_ref, lt, rt):
            for j in range(H // LANES):
                block = value_ref[:, j * LANES : (j + 1) * LANES].T
                lt[l, 4 * j : 4 * j + 4] = block.reshape(4, 2, BLOCK, LANES)
            if fused:
                return wire.send(lt.at[l, :, 1 - core], rt.at[l], sibling)

        def share(l, ref, first, last):
            if fused:
                return wire.send(
                    ref.at[l, 0:T, first:last], ref.at[l, T : 2 * T, first:last], sibling
                )

        def outer(l, lt, rt, right, first, last, dest, waits, at):
            if fused:
                for copy in waits:
                    copy.wait_recv()
                mine = lt[l, :, core].reshape(H // 2, LANES)
                left = jnp.concatenate([mine, rt[l].reshape(H // 2, LANES)], axis=1)
                for c in range(first, last, 256):
                    g = mm(left, right[l, :, c : c + 256]).astype(LOW)
                    dest[l, :, :, :, :, c : c + 256] = g.reshape(nz, 2, 2, BLOCK, 256)
            else:
                left = lt[l].reshape(H, LANES)
                for c in range(first, last, 256):
                    r.matrix_sums[l, :, at + c - first : at + c - first + 256] = mm(
                        left, right[l, 0:T, c : c + 256]
                    )

        place = {"z": zz, "x": xx, "y": yy}

        def peers(axis):
            if axis == "x":
                return [(1 - xx, x_peer)]
            if axis == "y":
                return [(1 - yy, y_peer)]
            return [((zz + o) % nz, {"seq": ((zz + o) % nz) * 2 + xx}) for o in range(1, nz)]

        class Part:
            def __init__(self, whole, first, last, order, got, sums):
                self.ref, self.columns = whole, pl.ds(first, last - first)
                self.axes, self.order, self.stage = ["z", "x", "y"], order, 0
                self.got, self.sums = got, sums

            def begin(self):
                axis = self.order[self.stage]
                self.where = self.axes.index(axis)
                rest = len(self.axes) - 1 - self.where
                self.copies = []
                for i, (to, device) in enumerate(peers(axis)):
                    index = (slice(None),) * self.where + (to,) + (slice(None),) * (rest + 1)
                    self.copies.append(
                        wire.send(self.ref.at[index + (self.columns,)], self.got[self.stage].at[i], device)
                    )

            def total(self):
                for copy in self.copies:
                    copy.wait_recv()
                axis, got = self.order[self.stage], self.got[self.stage]
                mine, wait = place[axis], len(self.copies)
                rest = [a for a in self.axes if a != axis]
                if not rest:
                    value = self.ref[mine, :, self.columns].astype(F32)
                    for i in range(wait):
                        value = value + got[i].astype(F32)
                    return value
                out = self.sums[self.stage]
                for q in range(out.shape[0]):
                    if self.where == 0:
                        index = (mine, q)
                    else:
                        index = (q,) + (slice(None),) * (self.where - 1) + (mine,)
                    index += (slice(None),) * (len(self.axes) - len(index) + 1) + (self.columns,)
                    if wait == 1:
                        out[q] = self.ref[index] + got[0, q]
                    else:
                        value = self.ref[index].astype(F32)
                        for i in range(wait):
                            value = value + got[i, q].astype(F32)
                        out[q] = value.astype(LOW)
                self.ref, self.columns = out, slice(None)
                self.axes = rest
                self.stage += 1

            def step(self):
                self.total()
                self.begin()

        def parts_of(l, name):
            whole = getattr(r, f"p_{name}")
            out = []
            for i, (first, last, order) in enumerate(z.plan[name]):
                got = [getattr(r, f"got_{name}{i}{stage}").at[l] for stage in range(3)]
                sums = [getattr(r, f"sum_{name}{i}{stage}").at[l] for stage in range(2)]
                out.append(Part(whole.at[l], first, last, order, got, sums))
            return out

        def rs_start(parts):
            for part in parts:
                part.begin()

        def rs_step(parts):
            for part in parts:
                part.step()

        def rs_end(parts):
            return jnp.concatenate([part.total() for part in parts], axis=1)

        def vec_start(l):
            r.vec_copy[l] = wire.send(r.vec.at[l, 0], r.vec_in.at[l, 0], sibling)

        def vec_next(l, stage):
            r.vec_copy[l].wait_recv()
            r.vec[l, stage] = r.vec[l, stage - 1] + r.vec_in[l, stage - 1]
            r.vec_copy[l] = wire.send(
                r.vec.at[l, stage], r.vec_in.at[l, stage], (sibling, x_peer, y_peer)[stage]
            )

        def vec_last(l):
            r.vec_copy[l].wait_recv()
            total = r.vec[l, 2] + r.vec_in[l, 2]
            r.vec_z[l, zz] = total
            r.vec_copy[l] = [
                wire.send(
                    r.vec_z.at[l, zz], r.vec_z.at[l, zz], {"seq": ((zz + o) % nz) * 2 + xx}
                )
                for o in range(1, nz)
            ]

        def vec_end(l):
            for copy in r.vec_copy[l]:
                copy.wait_recv()
            total = r.vec_z[l, 0]
            for o in range(1, nz):
                total = total + r.vec_z[l, o]
            return total

        r.vec_copy = [None, None]
        early = [parts_of(l, "e") if fused else None for l in range(2)]
        late = [parts_of(l, "n") if fused else None for l in range(2)]
        waits = {}

        def gain(l):
            return r.norm_gain[l : l + 1, :]

        def skip(l):
            return r.skip_gain[l : l + 1, :]

        def pack_in(l):
            loads[f"wi{l}"].wait()

            def step(i, carry):
                rows = pl.ds(pl.multiple_of(i * BLOCK, BLOCK), BLOCK)
                r.wi[l, rows, :] = r.wi_raw[l, rows].reshape(BLOCK, W)
                return carry

            lax.fori_loop(0, H // BLOCK, step, 0, unroll=2)

        def forward_in(l):
            def norm(rows, carry):
                u = r.u[l, rows, :]
                inv = lax.rsqrt(jnp.mean(u * u, axis=1, keepdims=True) + EPS)
                normed = u * inv * gain(l)
                r.inv[l, rows, :] = jnp.broadcast_to(inv, (BLOCK, LANES))
                r.normed[l, rows, :] = normed
                r.normed_low[l, rows, :] = normed.astype(LOW)
                return carry

            chunks(norm)
            r.proj[l] = mm(r.normed_low[l], r.wi[l])

        def states(l, between):
            cre = jnp.broadcast_to(disc[l].coef_re, (SUB, N))
            cim = jnp.broadcast_to(disc[l].coef_im, (SUB, N))

            def source(s, first):
                rows = slice(s * SUB, (s + 1) * SUB)
                if first:
                    dre, dim = cmul(cre, cim, r.proj[l, rows, 0:N], r.proj[l, rows, N:W])
                    r.drive[rows, 0:N] = dre
                    r.drive[rows, N:W] = dim
                    return dre, dim
                return r.drive[rows, 0:N], r.drive[rows, N:W]

            def sink(s, yre, yim):
                rows = slice(s * SUB, (s + 1) * SUB)
                r.x[l, rows, 0:N] = yre
                r.x[l, rows, N:W] = yim
                return yre, yim

            sink.dest = (r.right_e, H)
            scan(l, l, l, False, source, between, sink)

        def forward_out(l):
            waits["x", l] = share(l, r.right_e, H, CE)
            loads[f"wo{l}"].wait()
            r.mixed[l] = mm(r.right_e[l, 0:T, H:CE], r.wo[l])

            def gelu(rows, carry):
                mixed = r.mixed[l, rows, :] + skip(l) * r.normed[l, rows, :]
                th = jnp.tanh(GELU_A * (mixed + GELU_B * (mixed * mixed * mixed)))
                r.mixed[l, rows, :] = mixed
                r.th[l, rows, :] = th
                r.act_low[l, rows, :] = (0.5 * mixed * (1.0 + th)).astype(LOW)
                return carry

            chunks(gelu)
            loads[f"wg{l}"].wait()
            r.gate[l] = mm(r.act_low[l], r.wg[l])

            def out(rows, carry):
                gate = jax.nn.sigmoid(r.gate[l, rows, :] + r.glu_bias[l : l + 1, :])
                r.gate[l, rows, :] = gate
                act = 0.5 * r.mixed[l, rows, :] * (1.0 + r.th[l, rows, :])
                value = r.u[l, rows, :] + act * gate
                if l == 0:
                    r.u[1, rows, :] = value
                else:
                    r.act_out[rows, :] = value.astype(LOW)
                return carry

            chunks(out)

        def backward_in(l):
            def glu(rows, bias):
                g = r.og[rows, :]
                gate = r.gate[l, rows, :]
                act = 0.5 * r.mixed[l, rows, :] * (1.0 + r.th[l, rows, :])
                gate_grad = (g * act * gate * (1.0 - gate)).astype(LOW)
                r.right_e[l, rows, 0:H] = gate_grad
                wide_grad = gate_grad.astype(F32)
                return bias + wide_grad[0:SUB] + wide_grad[SUB:BLOCK]

            bias = chunks(glu, jnp.zeros((SUB, H), F32))
            r.vec[l, 0, 2:3, :] = jnp.sum(bias, axis=0, keepdims=True)
            waits["gate", l] = share(l, r.right_e, 0, H)
            r.tmp[...] = mm_nt(r.right_e[l, 0:T, 0:H], r.wg[l])

            def gelu(rows, total):
                act_grad = r.og[rows, :] * r.gate[l, rows, :] + r.tmp[rows, :]
                mixed, th = r.mixed[l, rows, :], r.th[l, rows, :]
                inner = GELU_A * (1.0 + 3.0 * GELU_B * mixed * mixed)
                slope = 0.5 * (1.0 + th) + 0.5 * mixed * (1.0 - th * th) * inner
                low = (act_grad * slope).astype(LOW)
                r.mixed_grad[l, rows, :] = low
                part = low.astype(F32) * r.normed[l, rows, :]
                return total + part[0:SUB] + part[SUB:BLOCK]

            total = chunks(gelu, jnp.zeros((SUB, H), F32))
            r.vec[l, 0, 0:1, :] = jnp.sum(total, axis=0, keepdims=True)
            r.xg[...] = mm_nt(r.mixed_grad[l], r.wo[l])

        def adjoints(l, between):
            d = disc[l]
            cre = jnp.broadcast_to(d.coef_re, (SUB, N))
            cim = jnp.broadcast_to(d.coef_im, (SUB, N))
            way = 1 - l
            sums = [jnp.zeros((SUB, N), F32) for _ in range(4)]

            def source(s, first):
                rows = slice(s * SUB, (s + 1) * SUB)
                return r.xg[rows, 0:N], r.xg[rows, N:W]

            def sink(s, are, aim):
                rows = slice(s * SUB, (s + 1) * SUB)
                at = s - 1 if l == 0 else s + 1
                if 0 <= at < S:
                    old = slice(at * SUB, (at + 1) * SUB)
                    xre, xim = r.x[l, old, 0:N], r.x[l, old, N:W]
                else:
                    xre, xim = r.x_first[l, :, 0:N], r.x_first[l, :, N:W]
                k = wide(r.keep[l, rows, :], N)
                xre, xim = xre * k, xim * k
                pre, pim = r.proj[l, rows, 0:N], r.proj[l, rows, N:W]
                sums[0] = sums[0] + (are * xre + aim * xim)
                sums[1] = sums[1] + (aim * xre - are * xim)
                sums[2] = sums[2] + (are * pre + aim * pim)
                sums[3] = sums[3] + (aim * pre - are * pim)
                return cre * are + cim * aim, cre * aim - cim * are

            sink.dest = (r.right_n, 0)
            scan(3 - l, l, way, True, source, between, sink)
            pad = jnp.zeros((1, H - N), F32)
            for i in range(4):
                value = jnp.sum(sums[i], axis=0, keepdims=True)
                r.vec[l, 0, 3 + i : 4 + i, :] = jnp.concatenate([value, pad], axis=1)

        def backward_out(l):
            waits["pg", l] = share(l, r.right_n, 0, W)
            r.tmp[...] = mm_nt(r.right_n[l, 0:T, :], r.wi[l])

            def norm(rows, total):
                u = r.u[l, rows, :]
                inv = wide(r.inv[l, rows, :], H)
                ng = r.tmp[rows, :] + skip(l) * r.mixed_grad[l, rows, :].astype(F32)
                v = gain(l) * ng
                uv = jnp.mean(u * v, axis=1, keepdims=True)
                out = r.og[rows, :] + inv * v - u * (inv * inv * inv) * uv
                r.og[rows, :] = out
                part = ng * u * inv
                return total + part[0:SUB] + part[SUB:BLOCK]

            total = chunks(norm, jnp.zeros((SUB, H), F32))
            r.vec[l, 0, 1:2, :] = jnp.sum(total, axis=0, keepdims=True)
            r.vec[l, 0, 7:8, :] = jnp.zeros((1, H), F32)

        def early_products(l):
            dest = r.p_e if fused else None
            outer(l, r.lt_g, r.rt_g, r.right_e, 0, H, dest, (waits["lg", l], waits["gate", l]), 0)
            outer(l, r.lt_o, r.rt_o, r.right_e, H, CE, dest, (waits["lo", l], waits["x", l]), H)

        def late_products(l):
            dest = r.p_n if fused else None
            outer(l, r.lt_n, r.rt_n, r.right_n, 0, W, dest, (waits["ln", l], waits["pg", l]), CE)

        loads["tok"].wait()
        at = lax.broadcasted_iota(jnp.int32, (T, T), 0)
        of = lax.broadcasted_iota(jnp.int32, (T, T), 1)
        to_rows = jnp.where(of == (at % SUB) * S + at // SUB, 1.0, 0.0).astype(LOW)
        to_time = jnp.where(at == (of % SUB) * S + of // SUB, 1.0, 0.0).astype(LOW)
        r.u[0] = mm(to_rows, r.tok[...])
        pack_in(0)
        forward_in(0)

        def fill0():
            pack_in(1)
            waits["ln", 0] = turn(0, r.normed_low.at[0], r.lt_n, r.rt_n)

        states(0, fill0)
        forward_out(0)

        forward_in(1)

        def fill1():
            waits["lg", 0] = turn(0, r.act_low.at[0], r.lt_g, r.rt_g)
            waits["ln", 1] = turn(1, r.normed_low.at[1], r.lt_n, r.rt_n)
            loads["cot"].wait()
            r.og[...] = mm(to_rows, r.cot[...])

        states(1, fill1)
        forward_out(1)
        backward_in(1)

        def fill2():
            waits["lo", 1] = turn(1, r.mixed_grad.at[1], r.lt_o, r.rt_o)
            waits["lg", 1] = turn(1, r.act_low.at[1], r.lt_g, r.rt_g)
            r.activations[...] = mm(to_time, r.act_out[...]).astype(LOW)
            early_products(1)
            if fused:
                rs_start(early[1])

        adjoints(1, fill2)
        backward_out(1)
        backward_in(0)

        def fill3():
            late_products(1)
            if fused:
                rs_start(late[1])
                vec_start(1)
            waits["lo", 0] = turn(0, r.mixed_grad.at[0], r.lt_o, r.rt_o)
            if fused:
                rs_step(early[1])
            early_products(0)
            if fused:
                rs_start(early[0])
                vec_next(1, 1)

        adjoints(0, fill3)
        backward_out(0)
        if fused:
            vec_start(0)
            rs_step(late[1])
        late_products(0)
        if fused:
            rs_start(late[0])

        for s in range(S):
            for j in range(H // LANES):
                r.tokens_grad[pl.ds(s * (H // LANES) + j, SUB, stride=S * (H // LANES)), :] = r.og[
                    s * SUB : (s + 1) * SUB, j * LANES : (j + 1) * LANES
                ]

        if not fused:
            r.vector_sums[...] = r.vec[:, 0]
            wire.close()
            return

        vec_next(1, 2)
        rs_step(early[1])
        vec_next(0, 1)
        rs_step(early[0])
        rs_step(late[1])
        vec_last(1)
        rs_step(late[0])
        vec_next(0, 2)
        rs_step(early[0])
        vec_last(0)
        rs_step(late[0])
        device = seq * nblk + blk
        for l in (1, 0):
            g = rs_end(early[l])
            r.glu_weight_grad[l] = g[:, 0:H]
            r.out_proj_grad[l, 0] = g[:, H : H + N]
            r.out_proj_grad[l, 1] = g[:, H + N : CE]
            g = rs_end(late[l])
            for c in range(2):
                r.in_proj_grad[l, :, c, :] = g[:, c * N : (c + 1) * N]
            total = vec_end(l)
            mine = pltpu.roll(total, (H - device * BLOCK) % H, 1)[:, 0:BLOCK]
            r.skip_gain_grad[l : l + 1, :] = mine[0:1]
            r.norm_gain_grad[l : l + 1, :] = mine[1:2]
            r.glu_bias_grad[l : l + 1, :] = mine[2:3]
            grads = discretize_grad(disc[l], *(total[3 + i : 4 + i, 0:N] for i in range(4)))
            r.decay_log_grad[l : l + 1, :] = grads[0]
            r.frequency_grad[l : l + 1, :] = grads[1]
            r.step_log_grad[l : l + 1, :] = grads[2]
        wire.close()

    return kernel


def solution(mesh):
    nseq, nblk = mesh.shape["seq"], mesh.shape["blk"]

    def on_device(
        tokens, lengths, norm_gain, in_proj, out_proj, skip_gain,
        glu_weight, glu_bias, decay_log, frequency, step_log, cotangent,
    ):
        T, streams, H = tokens.shape
        N = decay_log.shape[1]
        W = 2 * N
        CE = H + W
        assert streams == 1 and T == LANES and H == 512
        fused = nseq == 8 and nblk == 4
        plan = {
            "e": ((0, 384, "xyz"), (384, 896, "yxz"), (896, CE, "zxy")),
            "n": ((0, N, "xyz"), (N, W, "yxz")),
        }
        z = types.SimpleNamespace(
            T=T, H=H, N=N, S=T // SUB, nseq=nseq, nblk=nblk, fused=fused, plan=plan
        )
        any_space = pl.BlockSpec(memory_space=pl.ANY)
        vmem = pl.BlockSpec(memory_space=pltpu.VMEM)
        smem = pl.BlockSpec(memory_space=pltpu.SMEM)
        operands = {
            "tokens": (tokens.reshape(T, H), any_space),
            "lengths": (lengths, smem),
            "norm_gain": (norm_gain, vmem),
            "in_proj": (in_proj, any_space),
            "out_proj": (out_proj.reshape(2, W, H), any_space),
            "skip_gain": (skip_gain, vmem),
            "glu_weight": (glu_weight, any_space),
            "glu_bias": (glu_bias, vmem),
            "decay_log": (decay_log, vmem),
            "frequency": (frequency, vmem),
            "step_log": (step_log, vmem),
            "cotangent": (cotangent.reshape(T, H), any_space),
        }
        results = {
            "activations": ((T, H), LOW),
            "tokens_grad": ((T * H // LANES, LANES), F32),
        }
        if fused:
            results |= {
                "norm_gain_grad": ((2, BLOCK), F32),
                "in_proj_grad": ((2, BLOCK, 2, N), F32),
                "out_proj_grad": ((2, 2, BLOCK, N), F32),
                "skip_gain_grad": ((2, BLOCK), F32),
                "glu_weight_grad": ((2, BLOCK, H), F32),
                "glu_bias_grad": ((2, BLOCK), F32),
                "decay_log_grad": ((2, N), F32),
                "frequency_grad": ((2, N), F32),
                "step_log_grad": ((2, N), F32),
            }
        else:
            results |= {"matrix_sums": ((2, H, CE + W), F32), "vector_sums": ((2, 8, H), F32)}
        dma = pltpu.SemaphoreType.DMA
        scratch = {
            "wi_raw": pltpu.VMEM((2, H, 2, N), LOW),
            "wi": pltpu.VMEM((2, H, W), LOW),
            "wo": pltpu.VMEM((2, W, H), LOW),
            "wg": pltpu.VMEM((2, H, H), LOW),
            "tok": pltpu.VMEM((T, H), LOW),
            "cot": pltpu.VMEM((T, H), LOW),
            "u": pltpu.VMEM((2, T, H), F32),
            "inv": pltpu.VMEM((2, T, LANES), F32),
            "normed": pltpu.VMEM((2, T, H), F32),
            "normed_low": pltpu.VMEM((2, T, H), LOW),
            "proj": pltpu.VMEM((2, T, W), F32),
            "drive": pltpu.VMEM((T, W), F32),
            "x": pltpu.VMEM((2, T, W), F32),
            "x_first": pltpu.VMEM((2, SUB, W), F32),
            "mixed": pltpu.VMEM((2, T, H), F32),
            "th": pltpu.VMEM((2, T, H), F32),
            "gate": pltpu.VMEM((2, T, H), F32),
            "act_low": pltpu.VMEM((2, T, H), LOW),
            "act_out": pltpu.VMEM((T, H), LOW),
            "og": pltpu.VMEM((T, H), F32),
            "tmp": pltpu.VMEM((T, H), F32),
            "xg": pltpu.VMEM((T, W), F32),
            "mixed_grad": pltpu.VMEM((2, T, H), LOW),
            "right_e": pltpu.VMEM((2, 2 * T, CE), LOW),
            "right_n": pltpu.VMEM((2, 2 * T, W), LOW),
            "keep": pltpu.VMEM((2, T, LANES), F32),
            "chunk_keep": pltpu.VMEM((2, 3, SUB, LANES), F32),
            "chunk_table": pltpu.VMEM((4, SUB, W), F32),
            "seq_table": pltpu.VMEM((4, nseq, W), F32),
            "carry_out": pltpu.VMEM((4, 1, W), F32),
            "carry_in": pltpu.VMEM((4, nseq, 1, W), F32),
            "vec": pltpu.VMEM((2, 3, 8, H), F32),
        }
        for name in "gon":
            scratch[f"lt_{name}"] = pltpu.VMEM((2, H // 32, 2, BLOCK, LANES), LOW)
            scratch[f"rt_{name}"] = pltpu.VMEM((2, H // 32, BLOCK, LANES), LOW)
        if fused:
            nz = nseq // 2
            for name, width in (("e", CE), ("n", W)):
                scratch[f"p_{name}"] = pltpu.VMEM((2, nz, 2, 2, BLOCK, width), LOW)
                for i, (first, last, order) in enumerate(z.plan[name]):
                    left = {"z": nz, "x": 2, "y": 2}
                    for stage, axis in enumerate(order):
                        others = left.pop(axis) - 1
                        shape = tuple(left.values()) + (BLOCK, last - first)
                        scratch[f"got_{name}{i}{stage}"] = pltpu.VMEM((2, others) + shape, LOW)
                        if left:
                            scratch[f"sum_{name}{i}{stage}"] = pltpu.VMEM((2,) + shape, LOW)
            scratch["vec_in"] = pltpu.VMEM((2, 3, 8, H), F32)
            scratch["vec_z"] = pltpu.VMEM((2, nz, 8, H), F32)
        links = LINKS if fused else 4 * (nseq - 1)
        scratch["send_sems"] = dma((links,))
        scratch["recv_sems"] = dma((links,))
        scratch["load_sems"] = dma((8,))
        names = list(operands) + list(results) + list(scratch)
        outs = pl.pallas_call(
            make_kernel(names, z),
            out_shape=[(pltpu.VMEM if fused else jax.ShapeDtypeStruct)(*v) for v in results.values()],
            in_specs=[spec for _, spec in operands.values()],
            out_specs=[vmem] * len(results),
            scratch_shapes=list(scratch.values()),
            compiler_params=pltpu.CompilerParams(
                collective_id=0, has_side_effects=True, vmem_limit_bytes=48 * 2**20
            ),
            name="two_layers",
        )(*(pltpu.with_memory_space_constraint(value, pltpu.HBM) for value, _ in operands.values()))
        if fused:
            outs = pl.pallas_call(
                hand_out,
                out_shape=[jax.ShapeDtypeStruct(*v) for v in results.values()],
                in_specs=[vmem] * len(results),
                out_specs=[any_space] * len(results),
                scratch_shapes=[dma((len(results),))],
                name="hand_out",
            )(*(pltpu.with_memory_space_constraint(out, pltpu.VMEM) for out in outs))
        o = types.SimpleNamespace(**dict(zip(results, outs)))
        activations = o.activations.reshape(T, 1, H)
        tokens_grad = o.tokens_grad.reshape(T, 1, H)
        if fused:
            return (
                activations, tokens_grad, o.norm_gain_grad, o.in_proj_grad,
                jnp.swapaxes(o.out_proj_grad, 2, 3), o.skip_gain_grad, o.glu_weight_grad,
                o.glu_bias_grad, o.decay_log_grad, o.frequency_grad, o.step_log_grad,
            )
        both = ("seq", "blk")
        sums = lax.psum_scatter(o.matrix_sums, both, scatter_dimension=1, tiled=True)
        rows = sums.shape[1]
        vectors = lax.psum(o.vector_sums, both)
        mine = lax.dynamic_slice_in_dim(vectors, lax.axis_index(both) * rows, rows, 2)
        grads = discretize_grad(
            discretize(decay_log, frequency, step_log), *(vectors[:, 3 + i, 0:N] for i in range(4))
        )
        return (
            activations, tokens_grad, mine[:, 1], sums[:, :, CE:].reshape(2, rows, 2, N),
            jnp.moveaxis(sums[:, :, H:CE].reshape(2, rows, 2, N), 1, 3), mine[:, 0], sums[:, :, 0:H],
            mine[:, 2], *grads,
        )

    split = P("seq", "blk", None)
    owned = ("seq", "blk")
    return jax.shard_map(
        on_device,
        mesh=mesh,
        in_specs=(split,) + (P(),) * 10 + (split,),
        out_specs=(
            split, split, P(None, owned), P(None, owned, None, None), P(None, None, None, owned),
            P(None, owned), P(None, owned, None), P(None, owned), P(), P(), P(),
        ),
        check_vma=False,
    )
```

```python
import types

import jax
import jax.numpy as jnp
from jax import lax
from jax.experimental import pallas as pl
from jax.experimental.pallas import tpu as pltpu
from jax.sharding import PartitionSpec as P

EPS = 1e-6
F32 = jnp.float32
LOW = jnp.bfloat16
GELU_A = 0.7978845608028654
GELU_B = 0.044715
LANES = 128
SUB = 8
BLOCK = 16
LINKS = 160
SMALL = ("lengths", "norm_gain", "skip_gain", "glu_bias", "decay_log", "frequency", "step_log")

PLAN = {
    "e1": ((384, "zxy"), (256, "yzx"), (640, "xyz")),
    "n1": ((256, "yzx"), (128, "xyz"), (256, "xyz"), (128, "yxz")),
    "e0": ((384, "xyz"), (512, "yxz"), (384, "zxy")),
    "n0": ((256, "xyz"), (512, "xyz")),
}
SCHEDULE = (
    "E1 Be10 Be11 Be12",
    "N1 M0 e11 Bn10 Bn11 Bn12 e12 va E0 Be00 e10 Be01 Be02 n11 n10",
    "e11 OUT n12 va N0 vb Bn00 e12 Bn01 Bn13 e00 e10 e11 vb e01 e02 n11 n00 n12 n10 va n13 e00 e12 n01 e10 vb"
    " n00 n11 n12 e01 va e02 n10 n13 e00 n01 vb e02 n00 e01 n13 n01",
)


def cmul(are, aim, bre, bim):
    return are * bre - aim * bim, are * bim + aim * bre


def expm1(value):
    series = jnp.ones_like(value)
    for order in range(9, 1, -1):
        series = 1.0 + value * series * (1.0 / order)
    return jnp.where(value > -0.35, value * series, jnp.exp(value) - 1.0)


def discretize(decay, freq, step_log):
    lam_re = -jnp.exp(decay)
    step = jnp.exp(step_log)
    rotation = freq * step
    shrink = expm1(lam_re * step)
    cosine, sine = jnp.cos(rotation), jnp.sin(rotation)
    half = jnp.sin(0.5 * rotation)
    bar_re = (shrink + 1.0) * cosine
    bar_im = (shrink + 1.0) * sine
    minus_re = shrink * cosine - 2.0 * half * half
    scale = 1.0 / (lam_re * lam_re + freq * freq)
    coef_re = (minus_re * lam_re + bar_im * freq) * scale
    coef_im = (bar_im * lam_re - minus_re * freq) * scale
    return types.SimpleNamespace(
        lam_re=lam_re, freq=freq, step=step, scale=scale,
        bar_re=bar_re, bar_im=bar_im, coef_re=coef_re, coef_im=coef_im,
    )


def discretize_grad(d, bar_gre, bar_gim, coef_gre, coef_gim):
    over_re, over_im = d.lam_re * d.scale, d.freq * d.scale
    part_re, part_im = cmul(coef_gre, coef_gim, over_re, over_im)
    all_re, all_im = bar_gre + part_re, bar_gim + part_im
    one_re, one_im = cmul(all_re, all_im, d.bar_re, -d.bar_im)
    two_re, two_im = cmul(part_re, part_im, d.coef_re, -d.coef_im)
    lam_gre = one_re * d.step - two_re
    lam_gim = one_im * d.step - two_im
    step_g = one_re * d.lam_re + one_im * d.freq
    return lam_gre * d.lam_re, lam_gim, step_g * d.step


def mm(a, b):
    return jnp.dot(a, b, preferred_element_type=F32)


def mm_nt(a, b):
    return lax.dot_general(a, b, (((1,), (1,)), ((), ())), preferred_element_type=F32)


def wide(mask, width):
    return jnp.concatenate([mask] * (width // LANES), axis=1)


class Wire:
    def __init__(self, send_sems, recv_sems):
        self.send_sems, self.recv_sems = send_sems, recv_sems
        self.count = 0
        self.open = []

    def send(self, src, dst, device):
        at = self.count
        self.count += 1
        copy = pltpu.make_async_remote_copy(
            src_ref=src, dst_ref=dst,
            send_sem=self.send_sems.at[at], recv_sem=self.recv_sems.at[at],
            device_id=device, device_id_type=pl.DeviceIdType.MESH,
        )
        copy.start()
        self.open.append(copy)
        return copy

    def close(self):
        for copy in self.open:
            copy.wait_send()


def hand_out(*refs):
    count = len(refs) // 2
    copies = [
        pltpu.make_async_copy(refs[i], refs[count + i], refs[-1].at[i]) for i in range(count)
    ]
    for copy in copies:
        copy.start()
    for copy in copies:
        copy.wait()


def make_kernel(names, z):
    T, H, N, S, nseq, nblk, fused = z.T, z.H, z.N, z.S, z.nseq, z.nblk, z.fused
    W = 2 * N
    CE = H + W

    def kernel(*refs):
        r = types.SimpleNamespace(**dict(zip(names, refs, strict=True)))
        seq = lax.axis_index("seq")
        blk = lax.axis_index("blk")
        wire = Wire(r.send_sems, r.recv_sems)
        core, yy = blk % 2, blk // 2
        xx, zz = seq % 2, seq // 2
        nz = nseq // 2
        sibling = {"blk": yy * 2 + (1 - core)}
        y_peer = {"blk": (1 - yy) * 2 + core}
        x_peer = {"seq": zz * 2 + (1 - xx)}

        loads = {}

        def load(name, src, dst):
            copy = pltpu.make_async_copy(src, dst, r.load_sems.at[len(loads)])
            copy.start()
            loads[name] = copy

        load("tok", r.tokens, r.tok)
        for name in SMALL:
            load(name, getattr(r, name), getattr(r, name + "_here"))
            setattr(r, name, getattr(r, name + "_here"))
        load("wi0", r.in_proj.at[0], r.wi_raw.at[0])
        load("wo0", r.out_proj.at[0], r.wo.at[0])
        load("wg0", r.glu_weight.at[0], r.wg.at[0])
        load("wi1", r.in_proj.at[1], r.wi_raw.at[1])
        load("wo1", r.out_proj.at[1], r.wo.at[1])
        load("wg1", r.glu_weight.at[1], r.wg.at[1])
        load("cot", r.cotangent, r.cot)

        barrier = pltpu.get_barrier_semaphore()
        greeted = [{"seq": (seq + o) % nseq} for o in range(1, nseq)]
        if fused:
            greeted += [sibling, y_peer]
        for device in greeted:
            pl.semaphore_signal(barrier, inc=1, device_id=device, device_id_type=pl.DeviceIdType.MESH)

        for name in SMALL:
            loads[name].wait()
        disc, powers = [], []
        for l in range(2):
            d = discretize(
                r.decay_log[l : l + 1, :], r.frequency[l : l + 1, :], r.step_log[l : l + 1, :]
            )
            disc.append(d)
            chain = [(d.bar_re, d.bar_im)]
            while len(chain) < 12:
                chain.append(cmul(*chain[-1], *chain[-1]))
            powers.append(chain)
        step_bits = S.bit_length() - 1
        seg_bits = T.bit_length() - 1

        def power_rows(l, first, exponent, bits):
            rows = exponent.shape[0]
            out_re = jnp.ones((rows, N), F32)
            out_im = jnp.zeros((rows, N), F32)
            for bit in range(bits):
                use = wide(((exponent >> bit) & 1) == 1, N)
                pre, pim = powers[l][first + bit]
                new_re, new_im = cmul(out_re, out_im, pre, pim)
                out_re = jnp.where(use, new_re, out_re)
                out_im = jnp.where(use, new_im, out_im)
            return out_re, out_im

        ends, starts = [], []
        total = jnp.int32(0)
        for i in range(r.lengths.shape[1]):
            starts.append(total)
            total = total + r.lengths[blk, i]
            ends.append(total - 1)

        def keep(position, marks):
            hit = position == marks[0]
            for mark in marks[1:]:
                hit = hit | (position == mark)
            return jnp.where(hit, 0.0, 1.0).astype(F32)

        row = lax.broadcasted_iota(jnp.int32, (T, LANES), 0)
        here = seq * T + (row % SUB) * S + row // SUB
        r.keep[0] = keep(here, starts)
        r.keep[1] = keep(here, ends)
        offset = lax.broadcasted_iota(jnp.int32, (nseq, T), 0)
        lane = lax.broadcasted_iota(jnp.int32, (nseq, T), 1)
        there = ((seq - offset + nseq) % nseq) * T + lane
        k8 = lax.broadcasted_iota(jnp.int32, (SUB, LANES), 0)
        n_row = lax.broadcasted_iota(jnp.int32, (nseq, LANES), 0)
        for way in range(2):
            chunk = jnp.ones((SUB, LANES), F32)
            for s in range(S):
                chunk = chunk * r.keep[way, s * SUB : (s + 1) * SUB, :]
            for level in range(3):
                delta = 1 << level
                if way == 0:
                    inside, rolled = k8 >= delta, pltpu.roll(chunk, delta, 0)
                else:
                    inside, rolled = k8 < SUB - delta, pltpu.roll(chunk, SUB - delta, 0)
                r.chunk_keep[way, level] = jnp.where(inside, chunk, 0.0)
                chunk = jnp.where(inside, chunk * rolled, chunk)
            if way == 0:
                before = jnp.where(k8 >= 1, pltpu.roll(chunk, 1, 0), 1.0)
                chunks_before = k8
            else:
                before = jnp.where(k8 < SUB - 1, pltpu.roll(chunk, SUB - 1, 0), 1.0)
                chunks_before = SUB - 1 - k8
            whole = jnp.min(keep(there, starts if way == 0 else ends), axis=1, keepdims=True)
            whole = jnp.broadcast_to(whole, (nseq, LANES))
            gates = [None] * nseq
            running = jnp.ones((1, LANES), F32)
            for o in range(1, nseq) if way == 0 else range(nseq - 1, 0, -1):
                gates[o] = running
                running = running * whole[o : o + 1, :]
            gates[0] = jnp.zeros((1, LANES), F32)
            gate = jnp.concatenate(gates, axis=0)
            if way == 0:
                valid = (n_row >= 1) & (n_row <= seq)
                hops = n_row - 1
            else:
                valid = n_row > seq
                hops = nseq - 1 - n_row
            gate = jnp.where(valid, gate, 0.0)
            hops = jnp.where(valid, hops, 0)
            for l in range(2):
                index = (0, 2)[l] if way == 0 else (3, 1)[l]
                sign = 1.0 if index < 2 else -1.0
                pre, pim = power_rows(l, step_bits, chunks_before, 3)
                r.chunk_table[index, :, 0:N] = pre * wide(before, N)
                r.chunk_table[index, :, N:W] = pim * wide(before, N) * sign
                pre, pim = power_rows(l, seg_bits, hops, (nseq - 1).bit_length())
                r.seq_table[index, :, 0:N] = pre * wide(gate, N)
                r.seq_table[index, :, N:W] = pim * wide(gate, N) * sign
        for index in range(4):
            r.carry_in[index, 0] = jnp.zeros((1, W), F32)

        def scan(index, l, way, conj, source, between, sink):
            bre, bim = disc[l].bar_re, disc[l].bar_im
            sign = -1.0 if conj else 1.0
            bre = jnp.broadcast_to(bre, (SUB, N))
            bim = jnp.broadcast_to(bim * sign, (SUB, N))
            order = list(range(S)) if way == 0 else list(range(S - 1, -1, -1))

            def advance(s, yre, yim, dre, dim):
                k = wide(r.keep[way, s * SUB : (s + 1) * SUB, :], N)
                pre, pim = cmul(bre, bim, yre * k, yim * k)
                return pre + dre, pim + dim

            yre = jnp.zeros((SUB, N), F32)
            yim = jnp.zeros((SUB, N), F32)
            for s in order:
                dre, dim = source(s, True)
                yre, yim = advance(s, yre, yim, dre, dim)
            for level in range(3):
                delta = 1 << level
                shift = delta if way == 0 else SUB - delta
                m = wide(r.chunk_keep[way, level], N)
                pre, pim = powers[l][step_bits + level]
                gre, gim = cmul(pre, pim * sign, pltpu.roll(yre, shift, 0) * m, pltpu.roll(yim, shift, 0) * m)
                yre, yim = yre + gre, yim + gim
            last = SUB - 1 if way == 0 else 0
            r.carry_out[index, 0:1, 0:N] = yre[last : last + 1, :]
            r.carry_out[index, 0:1, N:W] = yim[last : last + 1, :]
            if index == 0:
                pl.semaphore_wait(barrier, len(greeted))
            copies = [
                wire.send(r.carry_out.at[index], r.carry_in.at[index, o], {"seq": (seq + o) % nseq})
                for o in range(1, nseq)
            ]
            edge = wide(k8 >= 1 if way == 0 else k8 < SUB - 1, N)
            shift = 1 if way == 0 else SUB - 1
            yre = jnp.where(edge, pltpu.roll(yre, shift, 0), 0.0)
            yim = jnp.where(edge, pltpu.roll(yim, shift, 0), 0.0)
            between()
            for copy in copies:
                copy.wait_recv()
            got = r.carry_in[index, :, 0, :]
            gre, gim = cmul(got[:, 0:N], got[:, N:W], r.seq_table[index, :, 0:N], r.seq_table[index, :, N:W])
            gre = jnp.sum(gre, axis=0, keepdims=True)
            gim = jnp.sum(gim, axis=0, keepdims=True)
            gre, gim = cmul(gre, gim, r.chunk_table[index, :, 0:N], r.chunk_table[index, :, N:W])
            yre, yim = yre + gre, yim + gim
            if not conj:
                r.x_first[l, :, 0:N] = yre
                r.x_first[l, :, N:W] = yim
            held = None
            for s in order:
                dre, dim = source(s, False)
                yre, yim = advance(s, yre, yim, dre, dim)
                out = sink(s, yre, yim)
                if held is None:
                    held = out
                else:
                    pair = (held, out) if way == 0 else (out, held)
                    first = s - 1 if way == 0 else s
                    for c in range(2):
                        both = jnp.concatenate([pair[0][c], pair[1][c]], axis=0).astype(LOW)
                        dest, at = sink.dest
                        dest[l, first * SUB : (first + 2) * SUB, at + c * N : at + (c + 1) * N] = both
                    held = None

        def chunks(body, init=0, unroll=T // BLOCK):
            def step(i, carry):
                return body(pl.ds(pl.multiple_of(i * BLOCK, BLOCK), BLOCK), carry)

            return lax.fori_loop(0, T // BLOCK, step, init, unroll=unroll)

        def turn(l, value_ref, lt, rt):
            for j in range(H // LANES):
                block = value_ref[:, j * LANES : (j + 1) * LANES].T
                lt[l, 4 * j : 4 * j + 4] = block.reshape(4, 2, BLOCK, LANES)
            if fused:
                return wire.send(lt.at[l, :, 1 - core], rt.at[l], sibling)

        def share(l, ref, first, last):
            if fused:
                return wire.send(
                    ref.at[l, 0:T, first:last], ref.at[l, T : 2 * T, first:last], sibling
                )

        def outer(l, lt, rt, right, first, last, dest, waits, at):
            if fused:
                for copy in waits:
                    copy.wait_recv()
                mine = lt[l, :, core].reshape(H // 2, LANES)
                left = jnp.concatenate([mine, rt[l].reshape(H // 2, LANES)], axis=1)
                for c in range(first, last, 256):
                    g = mm(left, right[l, :, c : c + 256]).astype(LOW)
                    dest[l, :, :, :, :, c : c + 256] = g.reshape(nz, 2, 2, BLOCK, 256)
            else:
                left = lt[l].reshape(H, LANES)
                for c in range(first, last, 256):
                    r.matrix_sums[l, :, at + c - first : at + c - first + 256] = mm(
                        left, right[l, 0:T, c : c + 256]
                    )

        place = {"z": zz, "x": xx, "y": yy}

        def peers(axis):
            if axis == "x":
                return [(1 - xx, x_peer)]
            if axis == "y":
                return [(1 - yy, y_peer)]
            return [((zz + o) % nz, {"seq": ((zz + o) % nz) * 2 + xx}) for o in range(1, nz)]

        class Part:
            def __init__(self, whole, first, last, order, got, sums):
                self.ref, self.columns = whole, pl.ds(first, last - first)
                self.axes, self.order, self.stage = ["z", "x", "y"], order, 0
                self.got, self.sums = got, sums

            def begin(self):
                axis = self.order[self.stage]
                self.where = self.axes.index(axis)
                rest = len(self.axes) - 1 - self.where
                self.copies = []
                for i, (to, device) in enumerate(peers(axis)):
                    index = (slice(None),) * self.where + (to,) + (slice(None),) * (rest + 1)
                    self.copies.append(
                        wire.send(self.ref.at[index + (self.columns,)], self.got[self.stage].at[i], device)
                    )

            def total(self):
                for copy in self.copies:
                    copy.wait_recv()
                axis, got = self.order[self.stage], self.got[self.stage]
                mine, wait = place[axis], len(self.copies)
                rest = [a for a in self.axes if a != axis]
                if not rest:
                    value = self.ref[mine, :, self.columns].astype(F32)
                    for i in range(wait):
                        value = value + got[i].astype(F32)
                    return value
                out = self.sums[self.stage]
                for q in range(out.shape[0]):
                    if self.where == 0:
                        index = (mine, q)
                    else:
                        index = (q,) + (slice(None),) * (self.where - 1) + (mine,)
                    index += (slice(None),) * (len(self.axes) - len(index) + 1) + (self.columns,)
                    if wait == 1:
                        out[q] = self.ref[index] + got[0, q]
                    else:
                        value = self.ref[index].astype(F32)
                        for i in range(wait):
                            value = value + got[i, q].astype(F32)
                        out[q] = value.astype(LOW)
                self.ref, self.columns = out, slice(None)
                self.axes = rest
                self.stage += 1

            def step(self):
                value = self.total()
                if value is None:
                    self.begin()
                else:
                    self.sink(value)

        along = {}

        def sink_of(l, name, first, last):
            def early(value):
                for low, high, out in (
                    (0, H, r.glu_weight_grad.at[l]),
                    (H, H + N, r.out_proj_grad.at[l, 0]),
                    (H + N, CE, r.out_proj_grad.at[l, 1]),
                ):
                    a, b = max(low, first), min(high, last)
                    if a < b:
                        out[:, a - low : b - low] = value[:, a - first : b - first]

            def late(value):
                for c in range(2):
                    a, b = max(c * N, first), min((c + 1) * N, last)
                    if a < b:
                        r.in_proj_grad[l, :, c, a - c * N : b - c * N] = value[:, a - first : b - first]
                weights = r.wi[l, own_rows, first:last].astype(F32)
                along.setdefault(l, []).append(jnp.sum(value * weights, axis=1, keepdims=True))

            return early if name == "e" else late

        parts = {}
        for l, name in z.plan:
            for i, (first, last, order) in enumerate(z.plan[l, name]):
                label = f"{name}{l}{i}"
                got = [getattr(r, f"got_{label}_{stage}") for stage in range(3)]
                sums = [getattr(r, f"sum_{label}_{stage}") for stage in range(2)]
                part = Part(getattr(r, f"p_{name}").at[l], first, last, order, got, sums)
                part.sink = sink_of(l, name, first, last)
                parts[label] = part

        device = seq * nblk + blk
        own_rows = pl.ds(pl.multiple_of(device * BLOCK, BLOCK), BLOCK)

        def owned(value):
            return pltpu.roll(value, (H - device * BLOCK) % H, 1)[:, 0:BLOCK]

        def out_vectors(l, totals):
            grads = discretize_grad(disc[l], *totals)
            r.decay_log_grad[l : l + 1, :] = grads[0]
            r.frequency_grad[l : l + 1, :] = grads[1]
            r.step_log_grad[l : l + 1, :] = grads[2]

        class Vector:
            def __init__(self, own, got, last):
                self.own, self.got, self.last, self.stage = own, got, last, 0

            def begin(self):
                device = (sibling, x_peer, y_peer)[self.stage]
                self.copy = wire.send(self.own.at[self.stage], self.got.at[self.stage], device)

            def step(self):
                if self.stage == 3:
                    return self.sink(self.total())
                self.copy.wait_recv()
                total = self.own[self.stage] + self.got[self.stage]
                self.stage += 1
                if self.stage < 3:
                    self.own[self.stage] = total
                    return self.begin()
                self.last[zz] = total
                self.copies = [
                    wire.send(self.last.at[zz], self.last.at[zz], {"seq": ((zz + o) % nz) * 2 + xx})
                    for o in range(1, nz)
                ]

            def total(self):
                for copy in self.copies:
                    copy.wait_recv()
                value = self.last[0]
                for o in range(1, nz):
                    value = value + self.last[o]
                return value

        if fused:
            first_vector = Vector(r.vec_a, r.vec_a_in, r.vec_a_z)
            last_vector = Vector(r.vec_b, r.vec_b_in, r.vec_b_z)

            def first_sink(sums):
                mine["sums"] = owned(sums)
                for l, at in ((1, 0), (0, 6)):
                    r.skip_gain_grad[l : l + 1, :] = mine["sums"][at : at + 1]
                    r.glu_bias_grad[l : l + 1, :] = mine["sums"][at + 1 : at + 2]
                out_vectors(1, [sums[2 + i : 3 + i, 0:N] for i in range(4)])

            mine = {}
            first_vector.sink = first_sink
            last_vector.sink = lambda sums: out_vectors(0, [sums[i : i + 1] for i in range(4)])
            parts["va"], parts["vb"] = first_vector, last_vector
        waits = {}

        def gain(l):
            return r.norm_gain[l : l + 1, :]

        def skip(l):
            return r.skip_gain[l : l + 1, :]

        def pack_in(l):
            loads[f"wi{l}"].wait()

            def step(i, carry):
                rows = pl.ds(pl.multiple_of(i * BLOCK, BLOCK), BLOCK)
                r.wi[l, rows, :] = r.wi_raw[l, rows].reshape(BLOCK, W)
                return carry

            lax.fori_loop(0, H // BLOCK, step, 0, unroll=4)

        def forward_in(l):
            def norm(rows, carry):
                u = r.u[l, rows, :]
                inv = lax.rsqrt(jnp.mean(u * u, axis=1, keepdims=True) + EPS)
                normed = u * inv * gain(l)
                r.inv[l, rows, :] = jnp.broadcast_to(inv, (BLOCK, LANES))
                r.normed[l, rows, :] = normed
                r.normed_low[l, rows, :] = normed.astype(LOW)
                return carry

            chunks(norm)
            r.proj[l] = mm(r.normed_low[l], r.wi[l])

        def states(l, between):
            cre = jnp.broadcast_to(disc[l].coef_re, (SUB, N))
            cim = jnp.broadcast_to(disc[l].coef_im, (SUB, N))

            def source(s, first):
                rows = slice(s * SUB, (s + 1) * SUB)
                if first:
                    dre, dim = cmul(cre, cim, r.proj[l, rows, 0:N], r.proj[l, rows, N:W])
                    r.drive[rows, 0:N] = dre
                    r.drive[rows, N:W] = dim
                    return dre, dim
                return r.drive[rows, 0:N], r.drive[rows, N:W]

            def sink(s, yre, yim):
                rows = slice(s * SUB, (s + 1) * SUB)
                r.x[l, rows, 0:N] = yre
                r.x[l, rows, N:W] = yim
                return yre, yim

            sink.dest = (r.right_e, H)
            scan(l, l, l, False, source, between, sink)

        def forward_out(l):
            waits["x", l] = share(l, r.right_e, H, CE)
            loads[f"wo{l}"].wait()
            r.mixed[l] = mm(r.right_e[l, 0:T, H:CE], r.wo[l])

            def gelu(rows, carry):
                mixed = r.mixed[l, rows, :] + skip(l) * r.normed[l, rows, :]
                th = jnp.tanh(GELU_A * (mixed + GELU_B * (mixed * mixed * mixed)))
                r.mixed[l, rows, :] = mixed
                r.th[l, rows, :] = th
                r.act_low[l, rows, :] = (0.5 * mixed * (1.0 + th)).astype(LOW)
                return carry

            chunks(gelu)
            loads[f"wg{l}"].wait()
            r.gate[l] = mm(r.act_low[l], r.wg[l])

            def out(rows, carry):
                gate = jax.nn.sigmoid(r.gate[l, rows, :] + r.glu_bias[l : l + 1, :])
                r.gate[l, rows, :] = gate
                act = 0.5 * r.mixed[l, rows, :] * (1.0 + r.th[l, rows, :])
                value = r.u[l, rows, :] + act * gate
                if l == 0:
                    r.u[1, rows, :] = value
                else:
                    r.act_out[rows, :] = value.astype(LOW)
                return carry

            chunks(out)

        def backward_in(l):
            def glu(rows, bias):
                g = r.og[rows, :]
                gate = r.gate[l, rows, :]
                act = 0.5 * r.mixed[l, rows, :] * (1.0 + r.th[l, rows, :])
                gate_grad = (g * act * gate * (1.0 - gate)).astype(LOW)
                r.right_e[l, rows, 0:H] = gate_grad
                wide_grad = gate_grad.astype(F32)
                return bias + wide_grad[0:SUB] + wide_grad[SUB:BLOCK]

            bias = chunks(glu, jnp.zeros((SUB, H), F32))
            r.vec_a[0, 1 if l == 1 else 7, :] = jnp.sum(bias, axis=0)
            waits["gate", l] = share(l, r.right_e, 0, H)
            r.tmp[...] = mm_nt(r.right_e[l, 0:T, 0:H], r.wg[l])

            def gelu(rows, total):
                act_grad = r.og[rows, :] * r.gate[l, rows, :] + r.tmp[rows, :]
                mixed, th = r.mixed[l, rows, :], r.th[l, rows, :]
                inner = GELU_A * (1.0 + 3.0 * GELU_B * mixed * mixed)
                slope = 0.5 * (1.0 + th) + 0.5 * mixed * (1.0 - th * th) * inner
                low = (act_grad * slope).astype(LOW)
                r.mixed_grad[l, rows, :] = low
                part = low.astype(F32) * r.normed[l, rows, :]
                return total + part[0:SUB] + part[SUB:BLOCK]

            total = chunks(gelu, jnp.zeros((SUB, H), F32))
            r.vec_a[0, 0 if l == 1 else 6, :] = jnp.sum(total, axis=0)
            r.xg[...] = mm_nt(r.mixed_grad[l], r.wo[l])

        def adjoints(l, between):
            d = disc[l]
            cre = jnp.broadcast_to(d.coef_re, (SUB, N))
            cim = jnp.broadcast_to(d.coef_im, (SUB, N))
            way = 1 - l
            sums = [jnp.zeros((SUB, N), F32) for _ in range(4)]

            def source(s, first):
                rows = slice(s * SUB, (s + 1) * SUB)
                return r.xg[rows, 0:N], r.xg[rows, N:W]

            def sink(s, are, aim):
                rows = slice(s * SUB, (s + 1) * SUB)
                at = s - 1 if l == 0 else s + 1
                if 0 <= at < S:
                    old = slice(at * SUB, (at + 1) * SUB)
                    xre, xim = r.x[l, old, 0:N], r.x[l, old, N:W]
                else:
                    xre, xim = r.x_first[l, :, 0:N], r.x_first[l, :, N:W]
                k = wide(r.keep[l, rows, :], N)
                xre, xim = xre * k, xim * k
                pre, pim = r.proj[l, rows, 0:N], r.proj[l, rows, N:W]
                sums[0] = sums[0] + (are * xre + aim * xim)
                sums[1] = sums[1] + (aim * xre - are * xim)
                sums[2] = sums[2] + (are * pre + aim * pim)
                sums[3] = sums[3] + (aim * pre - are * pim)
                return cre * are + cim * aim, cre * aim - cim * are

            sink.dest = (r.right_n, 0)
            scan(3 - l, l, way, True, source, between, sink)
            pad = jnp.zeros((1, H - N), F32)
            for i in range(4):
                value = jnp.sum(sums[i], axis=0, keepdims=True)
                if l == 1:
                    r.vec_a[0, 2 + i : 3 + i, :] = jnp.concatenate([value, pad], axis=1)
                else:
                    r.vec_b[0, i : i + 1, :] = value

        def backward_out(l):
            r.tmp[...] = mm_nt(r.right_n[l, 0:T, :], r.wi[l])

            def norm(rows, carry):
                u = r.u[l, rows, :]
                inv = wide(r.inv[l, rows, :], H)
                ng = r.tmp[rows, :] + skip(l) * r.mixed_grad[l, rows, :].astype(F32)
                v = gain(l) * ng
                uv = jnp.mean(u * v, axis=1, keepdims=True)
                out = r.og[rows, :] + inv * v - u * (inv * inv * inv) * uv
                r.og[rows, :] = out
                return carry

            chunks(norm)

        def early_products(l):
            dest = r.p_e if fused else None
            outer(l, r.lt_g, r.rt_g, r.right_e, 0, H, dest, (waits["lg", l], waits["gate", l]), 0)
            outer(l, r.lt_o, r.rt_o, r.right_e, H, CE, dest, (waits["lo", l], waits["x", l]), H)

        def late_products(l):
            dest = r.p_n if fused else None
            outer(l, r.lt_n, r.rt_n, r.right_n, 0, W, dest, (waits["ln", l], waits["pg", l]), CE)

        loads["tok"].wait()
        at = lax.broadcasted_iota(jnp.int32, (T, T), 0)
        of = lax.broadcasted_iota(jnp.int32, (T, T), 1)
        to_rows = jnp.where(of == (at % SUB) * S + at // SUB, 1.0, 0.0).astype(LOW)
        to_time = jnp.where(at == (of % SUB) * S + of // SUB, 1.0, 0.0).astype(LOW)
        r.u[0] = mm(to_rows, r.tok[...])
        pack_in(0)
        forward_in(0)

        def fill0():
            pack_in(1)
            waits["ln", 0] = turn(0, r.normed_low.at[0], r.lt_n, r.rt_n)

        states(0, fill0)
        forward_out(0)

        forward_in(1)

        def fill1():
            waits["lg", 0] = turn(0, r.act_low.at[0], r.lt_g, r.rt_g)
            waits["ln", 1] = turn(1, r.normed_low.at[1], r.lt_n, r.rt_n)
            loads["cot"].wait()
            r.og[...] = mm(to_rows, r.cot[...])

        states(1, fill1)
        forward_out(1)
        backward_in(1)

        def run(tokens):
            for token in tokens:
                if token in tasks:
                    tasks[token]()
                elif fused and token[0] == "B":
                    parts[token[1:]].begin()
                elif fused:
                    parts[token].step()

        def task_n1():
            late_products(1)
            if fused:
                first_vector.begin()

        def task_m0():
            waits["lo", 0] = turn(0, r.mixed_grad.at[0], r.lt_o, r.rt_o)

        def task_out():
            backward_out(0)
            for s in range(S):
                for j in range(H // LANES):
                    into = pl.ds(s * (H // LANES) + j, SUB, stride=S * (H // LANES))
                    r.tokens_grad[into, :] = r.og[s * SUB : (s + 1) * SUB, j * LANES : (j + 1) * LANES]

        tasks = {
            "N1": task_n1, "M0": task_m0, "E0": lambda: early_products(0),
            "N0": lambda: late_products(0), "OUT": task_out, "E1": lambda: early_products(1),
        }

        def fill2():
            waits["lo", 1] = turn(1, r.mixed_grad.at[1], r.lt_o, r.rt_o)
            waits["lg", 1] = turn(1, r.act_low.at[1], r.lt_g, r.rt_g)
            r.activations[...] = mm(to_time, r.act_out[...]).astype(LOW)
            run(z.schedule[0])

        adjoints(1, fill2)
        waits["pg", 1] = share(1, r.right_n, 0, W)
        backward_out(1)
        backward_in(0)
        adjoints(0, lambda: run(z.schedule[1]))
        waits["pg", 0] = share(0, r.right_n, 0, W)
        if fused:
            last_vector.begin()
        run(z.schedule[2])

        if not fused:
            r.vector_sums[...] = r.vec_a[0]
            r.last_vector_sums[...] = r.vec_b[0]
            wire.close()
            return

        gains = owned(jnp.concatenate([r.norm_gain[...], r.skip_gain[...], jnp.zeros((4, H), F32)], axis=0))
        diagonal = lax.broadcasted_iota(jnp.int32, (BLOCK, BLOCK), 0) == lax.broadcasted_iota(
            jnp.int32, (BLOCK, BLOCK), 1
        )
        for l, at in ((1, 0), (0, 6)):
            total = jnp.sum(jnp.where(diagonal, sum(along[l]), 0.0), axis=0, keepdims=True)
            total = total + gains[2 + l : 3 + l] * mine["sums"][at : at + 1]
            r.norm_gain_grad[l : l + 1, :] = total / gains[l : l + 1]
        wire.close()

    return kernel


def solution(mesh):
    nseq, nblk = mesh.shape["seq"], mesh.shape["blk"]

    def on_device(
        tokens, lengths, norm_gain, in_proj, out_proj, skip_gain,
        glu_weight, glu_bias, decay_log, frequency, step_log, cotangent,
    ):
        T, streams, H = tokens.shape
        N = decay_log.shape[1]
        W = 2 * N
        CE = H + W
        assert streams == 1 and T == LANES and H == 512
        fused = nseq == 8 and nblk == 4
        plan = {}
        for unit, pieces in PLAN.items():
            first = 0
            cuts = []
            for width, order in pieces:
                cuts.append((first, first + width, order))
                first += width
            assert first == (CE if unit[0] == "e" else W)
            plan[int(unit[1]), unit[0]] = cuts
        z = types.SimpleNamespace(
            T=T, H=H, N=N, S=T // SUB, nseq=nseq, nblk=nblk, fused=fused, plan=plan if fused else {},
            schedule=[line.split() for line in SCHEDULE],
        )
        any_space = pl.BlockSpec(memory_space=pl.ANY)
        vmem = pl.BlockSpec(memory_space=pltpu.VMEM)
        operands = {
            "tokens": (tokens.reshape(T, H), any_space),
            "lengths": (lengths, any_space),
            "norm_gain": (norm_gain, any_space),
            "in_proj": (in_proj, any_space),
            "out_proj": (out_proj.reshape(2, W, H), any_space),
            "skip_gain": (skip_gain, any_space),
            "glu_weight": (glu_weight, any_space),
            "glu_bias": (glu_bias, any_space),
            "decay_log": (decay_log, any_space),
            "frequency": (frequency, any_space),
            "step_log": (step_log, any_space),
            "cotangent": (cotangent.reshape(T, H), any_space),
        }
        results = {
            "activations": ((T, H), LOW),
            "tokens_grad": ((T * H // LANES, LANES), F32),
        }
        if fused:
            results |= {
                "norm_gain_grad": ((2, BLOCK), F32),
                "in_proj_grad": ((2, BLOCK, 2, N), F32),
                "out_proj_grad": ((2, 2, BLOCK, N), F32),
                "skip_gain_grad": ((2, BLOCK), F32),
                "glu_weight_grad": ((2, BLOCK, H), F32),
                "glu_bias_grad": ((2, BLOCK), F32),
                "decay_log_grad": ((2, N), F32),
                "frequency_grad": ((2, N), F32),
                "step_log_grad": ((2, N), F32),
            }
        else:
            results |= {
                "matrix_sums": ((2, H, CE + W), F32),
                "vector_sums": ((8, H), F32),
                "last_vector_sums": ((4, N), F32),
            }
        dma = pltpu.SemaphoreType.DMA
        scratch = {
            "wi_raw": pltpu.VMEM((2, H, 2, N), LOW),
            "wi": pltpu.VMEM((2, H, W), LOW),
            "wo": pltpu.VMEM((2, W, H), LOW),
            "wg": pltpu.VMEM((2, H, H), LOW),
            "tok": pltpu.VMEM((T, H), LOW),
            "cot": pltpu.VMEM((T, H), LOW),
            "u": pltpu.VMEM((2, T, H), F32),
            "inv": pltpu.VMEM((2, T, LANES), F32),
            "normed": pltpu.VMEM((2, T, H), F32),
            "normed_low": pltpu.VMEM((2, T, H), LOW),
            "proj": pltpu.VMEM((2, T, W), F32),
            "drive": pltpu.VMEM((T, W), F32),
            "x": pltpu.VMEM((2, T, W), F32),
            "x_first": pltpu.VMEM((2, SUB, W), F32),
            "mixed": pltpu.VMEM((2, T, H), F32),
            "th": pltpu.VMEM((2, T, H), F32),
            "gate": pltpu.VMEM((2, T, H), F32),
            "act_low": pltpu.VMEM((2, T, H), LOW),
            "act_out": pltpu.VMEM((T, H), LOW),
            "og": pltpu.VMEM((T, H), F32),
            "tmp": pltpu.VMEM((T, H), F32),
            "xg": pltpu.VMEM((T, W), F32),
            "mixed_grad": pltpu.VMEM((2, T, H), LOW),
            "right_e": pltpu.VMEM((2, 2 * T, CE), LOW),
            "right_n": pltpu.VMEM((2, 2 * T, W), LOW),
            "keep": pltpu.VMEM((2, T, LANES), F32),
            "chunk_keep": pltpu.VMEM((2, 3, SUB, LANES), F32),
            "chunk_table": pltpu.VMEM((4, SUB, W), F32),
            "seq_table": pltpu.VMEM((4, nseq, W), F32),
            "carry_out": pltpu.VMEM((4, 1, W), F32),
            "carry_in": pltpu.VMEM((4, nseq, 1, W), F32),
            "vec_a": pltpu.VMEM((3, 8, H), F32),
            "vec_b": pltpu.VMEM((3, 4, N), F32),
        }
        for name in "gon":
            scratch[f"lt_{name}"] = pltpu.VMEM((2, H // 32, 2, BLOCK, LANES), LOW)
            scratch[f"rt_{name}"] = pltpu.VMEM((2, H // 32, BLOCK, LANES), LOW)
        if fused:
            nz = nseq // 2
            for name, width in (("e", CE), ("n", W)):
                scratch[f"p_{name}"] = pltpu.VMEM((2, nz, 2, 2, BLOCK, width), LOW)
            for l, name in plan:
                for i, (first, last, order) in enumerate(plan[l, name]):
                    left = {"z": nz, "x": 2, "y": 2}
                    for stage, axis in enumerate(order):
                        others = left.pop(axis) - 1
                        shape = tuple(left.values()) + (BLOCK, last - first)
                        scratch[f"got_{name}{l}{i}_{stage}"] = pltpu.VMEM((others,) + shape, LOW)
                        if left:
                            scratch[f"sum_{name}{l}{i}_{stage}"] = pltpu.VMEM(shape, LOW)
            for name, shape in (("a", (8, H)), ("b", (4, N))):
                scratch[f"vec_{name}_in"] = pltpu.VMEM((3,) + shape, F32)
                scratch[f"vec_{name}_z"] = pltpu.VMEM((nz,) + shape, F32)
        links = LINKS if fused else 4 * (nseq - 1)
        scratch["send_sems"] = dma((links,))
        scratch["recv_sems"] = dma((links,))
        scratch["load_sems"] = dma((8 + len(SMALL),))
        for name in SMALL:
            value = operands[name][0]
            space = pltpu.SMEM if name == "lengths" else pltpu.VMEM
            scratch[name + "_here"] = space(value.shape, value.dtype)
        names = list(operands) + list(results) + list(scratch)
        outs = pl.pallas_call(
            make_kernel(names, z),
            out_shape=[(pltpu.VMEM if fused else jax.ShapeDtypeStruct)(*v) for v in results.values()],
            in_specs=[spec for _, spec in operands.values()],
            out_specs=[vmem] * len(results),
            scratch_shapes=list(scratch.values()),
            compiler_params=pltpu.CompilerParams(
                collective_id=0, has_side_effects=True, vmem_limit_bytes=48 * 2**20
            ),
            name="two_layers",
        )(*(pltpu.with_memory_space_constraint(value, pltpu.HBM) for value, _ in operands.values()))
        if fused:
            outs = pl.pallas_call(
                hand_out,
                out_shape=[jax.ShapeDtypeStruct(*v) for v in results.values()],
                in_specs=[vmem] * len(results),
                out_specs=[any_space] * len(results),
                scratch_shapes=[dma((len(results),))],
                name="hand_out",
            )(*(pltpu.with_memory_space_constraint(out, pltpu.VMEM) for out in outs))
        o = types.SimpleNamespace(**dict(zip(results, outs)))
        activations = o.activations.reshape(T, 1, H)
        tokens_grad = o.tokens_grad.reshape(T, 1, H)
        if fused:
            return (
                activations, tokens_grad, o.norm_gain_grad, o.in_proj_grad,
                jnp.swapaxes(o.out_proj_grad, 2, 3), o.skip_gain_grad, o.glu_weight_grad,
                o.glu_bias_grad, o.decay_log_grad, o.frequency_grad, o.step_log_grad,
            )
        both = ("seq", "blk")
        sums = lax.psum_scatter(o.matrix_sums, both, scatter_dimension=1, tiled=True)
        rows = sums.shape[1]
        vectors, last = lax.psum((o.vector_sums, o.last_vector_sums), both)
        start = lax.axis_index(both) * rows

        def owned(value, axis):
            return lax.dynamic_slice_in_dim(value, start, rows, axis)

        mine = owned(vectors, 1)
        skip_grad = jnp.stack([mine[6], mine[0]])
        bias_grad = jnp.stack([mine[7], mine[1]])
        totals = [jnp.stack([last[i], vectors[2 + i, 0:N]]) for i in range(4)]
        grads = discretize_grad(discretize(decay_log, frequency, step_log), *totals)
        in_grad = sums[:, :, CE:].reshape(2, rows, 2, N)
        along = jnp.sum(in_grad * owned(in_proj, 1).astype(F32), axis=(2, 3))
        gain_grad = (along + owned(skip_gain, 1) * skip_grad) / owned(norm_gain, 1)
        return (
            activations, tokens_grad, gain_grad, in_grad,
            jnp.moveaxis(sums[:, :, H:CE].reshape(2, rows, 2, N), 1, 3), skip_grad, sums[:, :, 0:H],
            bias_grad, *grads,
        )

    split = P("seq", "blk", None)
    owned = ("seq", "blk")
    return jax.shard_map(
        on_device,
        mesh=mesh,
        in_specs=(split,) + (P(),) * 10 + (split,),
        out_specs=(
            split, split, P(None, owned), P(None, owned, None, None), P(None, None, None, owned),
            P(None, owned), P(None, owned, None), P(None, owned), P(), P(), P(),
        ),
        check_vma=False,
    )
```

```python
import types

import jax
import jax.numpy as jnp
from jax import lax
from jax.experimental import pallas as pl
from jax.experimental.pallas import tpu as pltpu
from jax.sharding import PartitionSpec as P

EPS = 1e-6
F32 = jnp.float32
LOW = jnp.bfloat16
GELU_A = 0.7978845608028654
GELU_B = 0.044715
LANES = 128
SUB = 8
BLOCK = 16
LINKS = 160
SMALL = ("lengths", "norm_gain", "skip_gain", "glu_bias", "decay_log", "frequency", "step_log")

PLAN = {
    "e1": ((384, "ylhx"), (256, "lyxh"), (384, "ylhx"), (256, "zyx"),),
    "n1": ((128, "xhly"), (384, "hlxy"), (128, "yxz"), (128, "xhly"),),
    "e0": ((128, "lhyx"), (512, "xylh"), (384, "ylhx"), (256, "yxz"),),
    "n0": ((256, "yxz"), (256, "xyz"), (256, "xyz"),),
}
SCHEDULE = (
    ("E1", "Be10", "Be11", "Be12", "Be13",),
    ("N1", "V", "M0", "Bn12", "Bn11", "e11", "e10", "Bn10", "Bn13", "va", "E0", "Be02", "Be03", "Be00",)
    + ("Be01", "e13", "e12", "n12", "n10", "e11",),
    ("n13", "OUT", "va", "N0", "Bn00", "vb", "Bn01", "e10", "Bn02", "e02", "e00", "n11", "e01", "e03",)
    + ("e12", "n12", "e13", "e11", "va", "vb", "n10", "n13", "n01", "n00", "e10", "e02", "n02", "e01",)
    + ("e00", "n11", "vb", "e03", "e13", "n01", "e12", "n00", "e10", "e11", "n10", "n12", "n13", "n02",)
    + ("va", "n11", "e02", "e00", "e01", "va", "e12", "vb", "n10", "e03", "n13", "n01", "n11", "vb",)
    + ("e02", "n00", "e00", "n02", "e01",),
)


def cmul(are, aim, bre, bim):
    return are * bre - aim * bim, are * bim + aim * bre


def expm1(value):
    series = jnp.ones_like(value)
    for order in range(9, 1, -1):
        series = 1.0 + value * series * (1.0 / order)
    return jnp.where(value > -0.35, value * series, jnp.exp(value) - 1.0)


def discretize(decay, freq, step_log):
    lam_re = -jnp.exp(decay)
    step = jnp.exp(step_log)
    rotation = freq * step
    shrink = expm1(lam_re * step)
    cosine, sine = jnp.cos(rotation), jnp.sin(rotation)
    half = jnp.sin(0.5 * rotation)
    bar_re = (shrink + 1.0) * cosine
    bar_im = (shrink + 1.0) * sine
    minus_re = shrink * cosine - 2.0 * half * half
    scale = 1.0 / (lam_re * lam_re + freq * freq)
    coef_re = (minus_re * lam_re + bar_im * freq) * scale
    coef_im = (bar_im * lam_re - minus_re * freq) * scale
    return types.SimpleNamespace(
        lam_re=lam_re, freq=freq, step=step, scale=scale,
        bar_re=bar_re, bar_im=bar_im, coef_re=coef_re, coef_im=coef_im,
    )


def discretize_grad(d, bar_gre, bar_gim, coef_gre, coef_gim):
    over_re, over_im = d.lam_re * d.scale, d.freq * d.scale
    part_re, part_im = cmul(coef_gre, coef_gim, over_re, over_im)
    all_re, all_im = bar_gre + part_re, bar_gim + part_im
    one_re, one_im = cmul(all_re, all_im, d.bar_re, -d.bar_im)
    two_re, two_im = cmul(part_re, part_im, d.coef_re, -d.coef_im)
    lam_gre = one_re * d.step - two_re
    lam_gim = one_im * d.step - two_im
    step_g = one_re * d.lam_re + one_im * d.freq
    return lam_gre * d.lam_re, lam_gim, step_g * d.step


def mm(a, b):
    return jnp.dot(a, b, preferred_element_type=F32)


def mm_nt(a, b):
    return lax.dot_general(a, b, (((1,), (1,)), ((), ())), preferred_element_type=F32)


def wide(mask, width):
    return jnp.concatenate([mask] * (width // LANES), axis=1)


class Wire:
    def __init__(self, send_sems, recv_sems):
        self.send_sems, self.recv_sems = send_sems, recv_sems
        self.count = 0
        self.open = []

    def send(self, src, dst, device):
        at = self.count
        self.count += 1
        copy = pltpu.make_async_remote_copy(
            src_ref=src, dst_ref=dst,
            send_sem=self.send_sems.at[at], recv_sem=self.recv_sems.at[at],
            device_id=device, device_id_type=pl.DeviceIdType.MESH,
        )
        copy.start()
        self.open.append(copy)
        return copy

    def close(self):
        for copy in self.open:
            copy.wait_send()


def hand_out(*refs):
    count = len(refs) // 2
    copies = [
        pltpu.make_async_copy(refs[i], refs[count + i], refs[-1].at[i]) for i in range(count)
    ]
    for copy in copies:
        copy.start()
    for copy in copies:
        copy.wait()


def make_kernel(names, z):
    T, H, N, S, nseq, nblk, fused = z.T, z.H, z.N, z.S, z.nseq, z.nblk, z.fused
    W = 2 * N
    CE = H + W

    def kernel(*refs):
        r = types.SimpleNamespace(**dict(zip(names, refs, strict=True)))
        seq = lax.axis_index("seq")
        blk = lax.axis_index("blk")
        wire = Wire(r.send_sems, r.recv_sems)
        core, yy = blk % 2, blk // 2
        xx, zz = seq % 2, seq // 2
        nz = nseq // 2
        sibling = {"blk": yy * 2 + (1 - core)}
        y_peer = {"blk": (1 - yy) * 2 + core}
        x_peer = {"seq": zz * 2 + (1 - xx)}

        loads = {}

        def load(name, src, dst):
            copy = pltpu.make_async_copy(src, dst, r.load_sems.at[len(loads)])
            copy.start()
            loads[name] = copy

        load("tok", r.tokens, r.tok)
        for name in SMALL:
            load(name, getattr(r, name), getattr(r, name + "_here"))
            setattr(r, name, getattr(r, name + "_here"))
        load("wi0", r.in_proj.at[0], r.wi_raw.at[0])
        load("wo0", r.out_proj.at[0], r.wo.at[0])
        load("wg0", r.glu_weight.at[0], r.wg.at[0])
        load("wi1", r.in_proj.at[1], r.wi_raw.at[1])
        load("wo1", r.out_proj.at[1], r.wo.at[1])
        load("wg1", r.glu_weight.at[1], r.wg.at[1])
        load("cot", r.cotangent, r.cot)

        barrier = pltpu.get_barrier_semaphore()
        greeted = [{"seq": (seq + o) % nseq} for o in range(1, nseq)]
        if fused:
            greeted += [sibling, y_peer]
        for device in greeted:
            pl.semaphore_signal(barrier, inc=1, device_id=device, device_id_type=pl.DeviceIdType.MESH)

        for name in SMALL:
            loads[name].wait()
        disc, powers = [], []
        for l in range(2):
            d = discretize(
                r.decay_log[l : l + 1, :], r.frequency[l : l + 1, :], r.step_log[l : l + 1, :]
            )
            disc.append(d)
            chain = [(d.bar_re, d.bar_im)]
            while len(chain) < 12:
                chain.append(cmul(*chain[-1], *chain[-1]))
            powers.append(chain)
        step_bits = S.bit_length() - 1
        seg_bits = T.bit_length() - 1

        def power_rows(l, first, exponent, bits):
            rows = exponent.shape[0]
            out_re = jnp.ones((rows, N), F32)
            out_im = jnp.zeros((rows, N), F32)
            for bit in range(bits):
                use = wide(((exponent >> bit) & 1) == 1, N)
                pre, pim = powers[l][first + bit]
                new_re, new_im = cmul(out_re, out_im, pre, pim)
                out_re = jnp.where(use, new_re, out_re)
                out_im = jnp.where(use, new_im, out_im)
            return out_re, out_im

        ends, starts = [], []
        total = jnp.int32(0)
        for i in range(r.lengths.shape[1]):
            starts.append(total)
            total = total + r.lengths[blk, i]
            ends.append(total - 1)

        def keep(position, marks):
            hit = position == marks[0]
            for mark in marks[1:]:
                hit = hit | (position == mark)
            return jnp.where(hit, 0.0, 1.0).astype(F32)

        row = lax.broadcasted_iota(jnp.int32, (T, LANES), 0)
        here = seq * T + (row % SUB) * S + row // SUB
        r.keep[0] = keep(here, starts)
        r.keep[1] = keep(here, ends)
        offset = lax.broadcasted_iota(jnp.int32, (nseq, T), 0)
        lane = lax.broadcasted_iota(jnp.int32, (nseq, T), 1)
        there = ((seq - offset + nseq) % nseq) * T + lane
        k8 = lax.broadcasted_iota(jnp.int32, (SUB, LANES), 0)
        n_row = lax.broadcasted_iota(jnp.int32, (nseq, LANES), 0)
        for way in range(2):
            chunk = jnp.ones((SUB, LANES), F32)
            for s in range(S):
                chunk = chunk * r.keep[way, s * SUB : (s + 1) * SUB, :]
            for level in range(3):
                delta = 1 << level
                if way == 0:
                    inside, rolled = k8 >= delta, pltpu.roll(chunk, delta, 0)
                else:
                    inside, rolled = k8 < SUB - delta, pltpu.roll(chunk, SUB - delta, 0)
                r.chunk_keep[way, level] = jnp.where(inside, chunk, 0.0)
                chunk = jnp.where(inside, chunk * rolled, chunk)
            if way == 0:
                before = jnp.where(k8 >= 1, pltpu.roll(chunk, 1, 0), 1.0)
                chunks_before = k8
            else:
                before = jnp.where(k8 < SUB - 1, pltpu.roll(chunk, SUB - 1, 0), 1.0)
                chunks_before = SUB - 1 - k8
            whole = jnp.min(keep(there, starts if way == 0 else ends), axis=1, keepdims=True)
            whole = jnp.broadcast_to(whole, (nseq, LANES))
            gates = [None] * nseq
            running = jnp.ones((1, LANES), F32)
            for o in range(1, nseq) if way == 0 else range(nseq - 1, 0, -1):
                gates[o] = running
                running = running * whole[o : o + 1, :]
            gates[0] = jnp.zeros((1, LANES), F32)
            gate = jnp.concatenate(gates, axis=0)
            if way == 0:
                valid = (n_row >= 1) & (n_row <= seq)
                hops = n_row - 1
            else:
                valid = n_row > seq
                hops = nseq - 1 - n_row
            gate = jnp.where(valid, gate, 0.0)
            hops = jnp.where(valid, hops, 0)
            for l in range(2):
                index = (0, 2)[l] if way == 0 else (3, 1)[l]
                sign = 1.0 if index < 2 else -1.0
                pre, pim = power_rows(l, step_bits, chunks_before, 3)
                r.chunk_table[index, :, 0:N] = pre * wide(before, N)
                r.chunk_table[index, :, N:W] = pim * wide(before, N) * sign
                pre, pim = power_rows(l, seg_bits, hops, (nseq - 1).bit_length())
                r.seq_table[index, :, 0:N] = pre * wide(gate, N)
                r.seq_table[index, :, N:W] = pim * wide(gate, N) * sign
        for index in range(4):
            r.carry_in[index, 0] = jnp.zeros((1, W), F32)

        def scan(index, l, way, conj, source, between, sink):
            bre, bim = disc[l].bar_re, disc[l].bar_im
            sign = -1.0 if conj else 1.0
            bre = jnp.broadcast_to(bre, (SUB, N))
            bim = jnp.broadcast_to(bim * sign, (SUB, N))
            order = list(range(S)) if way == 0 else list(range(S - 1, -1, -1))

            def advance(s, yre, yim, dre, dim):
                k = wide(r.keep[way, s * SUB : (s + 1) * SUB, :], N)
                pre, pim = cmul(bre, bim, yre * k, yim * k)
                return pre + dre, pim + dim

            yre = jnp.zeros((SUB, N), F32)
            yim = jnp.zeros((SUB, N), F32)
            for s in order:
                dre, dim = source(s, True)
                yre, yim = advance(s, yre, yim, dre, dim)
            for level in range(3):
                delta = 1 << level
                shift = delta if way == 0 else SUB - delta
                m = wide(r.chunk_keep[way, level], N)
                pre, pim = powers[l][step_bits + level]
                gre, gim = cmul(pre, pim * sign, pltpu.roll(yre, shift, 0) * m, pltpu.roll(yim, shift, 0) * m)
                yre, yim = yre + gre, yim + gim
            last = SUB - 1 if way == 0 else 0
            r.carry_out[index, 0:1, 0:N] = yre[last : last + 1, :]
            r.carry_out[index, 0:1, N:W] = yim[last : last + 1, :]
            if index == 0:
                pl.semaphore_wait(barrier, len(greeted))
            copies = [
                wire.send(r.carry_out.at[index], r.carry_in.at[index, o], {"seq": (seq + o) % nseq})
                for o in range(1, nseq)
            ]
            edge = wide(k8 >= 1 if way == 0 else k8 < SUB - 1, N)
            shift = 1 if way == 0 else SUB - 1
            yre = jnp.where(edge, pltpu.roll(yre, shift, 0), 0.0)
            yim = jnp.where(edge, pltpu.roll(yim, shift, 0), 0.0)
            between()
            for copy in copies:
                copy.wait_recv()
            got = r.carry_in[index, :, 0, :]
            gre, gim = cmul(got[:, 0:N], got[:, N:W], r.seq_table[index, :, 0:N], r.seq_table[index, :, N:W])
            gre = jnp.sum(gre, axis=0, keepdims=True)
            gim = jnp.sum(gim, axis=0, keepdims=True)
            gre, gim = cmul(gre, gim, r.chunk_table[index, :, 0:N], r.chunk_table[index, :, N:W])
            yre, yim = yre + gre, yim + gim
            if not conj:
                r.x_first[l, :, 0:N] = yre
                r.x_first[l, :, N:W] = yim
            held = None
            for s in order:
                dre, dim = source(s, False)
                yre, yim = advance(s, yre, yim, dre, dim)
                out = sink(s, yre, yim)
                if held is None:
                    held = out
                else:
                    pair = (held, out) if way == 0 else (out, held)
                    first = s - 1 if way == 0 else s
                    for c in range(2):
                        both = jnp.concatenate([pair[0][c], pair[1][c]], axis=0).astype(LOW)
                        dest, at = sink.dest
                        dest[l, first * SUB : (first + 2) * SUB, at + c * N : at + (c + 1) * N] = both
                    held = None

        def each(body):
            for first in range(0, T, BLOCK):
                body(slice(first, first + BLOCK))

        def turn(l, value_ref, lt, rt):
            for j in range(H // LANES):
                block = value_ref[:, j * LANES : (j + 1) * LANES].T
                lt[l, 4 * j : 4 * j + 4] = block.reshape(4, 2, BLOCK, LANES)
            if fused:
                return wire.send(lt.at[l, :, 1 - core], rt.at[l], sibling)

        def share(l, ref, first, last):
            if fused:
                return wire.send(
                    ref.at[l, 0:T, first:last], ref.at[l, T : 2 * T, first:last], sibling
                )

        def outer(l, lt, rt, right, first, last, dest, waits, at):
            if fused:
                for copy in waits:
                    copy.wait_recv()
                mine = lt[l, :, core].reshape(H // 2, LANES)
                left = jnp.concatenate([mine, rt[l].reshape(H // 2, LANES)], axis=1)
                for c in range(first, last, 256):
                    g = mm(left, right[l, :, c : c + 256]).astype(LOW)
                    dest[l, :, :, :, :, :, c : c + 256] = g.reshape(2, 2, 2, 2, BLOCK, 256)
            else:
                left = lt[l].reshape(H, LANES)
                for c in range(first, last, 256):
                    r.matrix_sums[l, :, at + c - first : at + c - first + 256] = mm(
                        left, right[l, 0:T, c : c + 256]
                    )

        hh, ll = zz // 2, zz % 2
        place = {"h": hh, "l": ll, "x": xx, "y": yy}

        def z_peer(at):
            return {"seq": at * 2 + xx}

        def peers(axis):
            if axis == "z":
                others = [(zz + o) % nz for o in range(1, nz)]
                return [({"h": to // 2, "l": to % 2}, z_peer(to)) for to in others]
            device = {
                "x": x_peer, "y": y_peer, "l": z_peer(hh * 2 + 1 - ll), "h": z_peer((1 - hh) * 2 + ll),
            }
            return [({axis: 1 - place[axis]}, device[axis])]

        class Part:
            def __init__(self, whole, first, last, order, got, sums):
                self.ref, self.columns = whole, pl.ds(first, last - first)
                self.axes, self.order, self.stage = "hlxy", order, 0
                self.got, self.sums = got, sums

            def index(self, at):
                return tuple(at.get(a, slice(None)) for a in self.axes) + (slice(None), self.columns)

            def begin(self):
                self.copies = [
                    wire.send(self.ref.at[self.index(at)], self.got[self.stage].at[i], device)
                    for i, (at, device) in enumerate(peers(self.order[self.stage]))
                ]

            def total(self):
                for copy in self.copies:
                    copy.wait_recv()
                axis, got = self.order[self.stage], self.got[self.stage]
                gone = "hl" if axis == "z" else axis
                mine = {a: place[a] for a in gone}
                rest = "".join(a for a in self.axes if a not in gone)
                if not rest:
                    value = self.ref[self.index(mine)].astype(F32)
                    for i in range(len(self.copies)):
                        value = value + got[i].astype(F32)
                    return value
                out = self.sums[self.stage]
                for q in range(2):
                    here = self.ref[self.index(mine | {rest[0]: q})]
                    if len(self.copies) == 1:
                        out[q] = here + got[0, q]
                    else:
                        value = here.astype(F32)
                        for i in range(len(self.copies)):
                            value = value + got[i, q].astype(F32)
                        out[q] = value.astype(LOW)
                self.ref, self.columns, self.axes = out, slice(None), rest
                self.stage += 1

            def step(self):
                value = self.total()
                if value is None:
                    self.begin()
                else:
                    self.sink(value)

        along = {}

        def sink_of(l, name, first, last):
            def early(value):
                for low, high, out in (
                    (0, H, r.glu_weight_grad.at[l]),
                    (H, H + N, r.out_proj_grad.at[l, 0]),
                    (H + N, CE, r.out_proj_grad.at[l, 1]),
                ):
                    a, b = max(low, first), min(high, last)
                    if a < b:
                        out[:, a - low : b - low] = value[:, a - first : b - first]

            def late(value):
                for c in range(2):
                    a, b = max(c * N, first), min((c + 1) * N, last)
                    if a < b:
                        r.in_proj_grad[l, :, c, a - c * N : b - c * N] = value[:, a - first : b - first]
                weights = r.wi[l, own_rows, first:last].astype(F32)
                along.setdefault(l, []).append(jnp.sum(value * weights, axis=1, keepdims=True))

            return early if name == "e" else late

        parts = {}
        for l, name in z.plan:
            for i, (first, last, order) in enumerate(z.plan[l, name]):
                label = f"{name}{l}{i}"
                got = [getattr(r, f"got_{label}_{stage}") for stage in range(len(order))]
                sums = [getattr(r, f"sum_{label}_{stage}") for stage in range(len(order) - 1)]
                part = Part(getattr(r, f"p_{name}").at[l], first, last, order, got, sums)
                part.sink = sink_of(l, name, first, last)
                parts[label] = part

        device = seq * nblk + blk
        own_rows = pl.ds(pl.multiple_of(device * BLOCK, BLOCK), BLOCK)

        def owned(value):
            return pltpu.roll(value, (H - device * BLOCK) % H, 1)[:, 0:BLOCK]

        def out_vectors(l, totals):
            grads = discretize_grad(disc[l], *totals)
            r.decay_log_grad[l : l + 1, :] = grads[0]
            r.frequency_grad[l : l + 1, :] = grads[1]
            r.step_log_grad[l : l + 1, :] = grads[2]

        class Vector:
            def __init__(self, name):
                self.own, self.got = getattr(r, name), getattr(r, name + "_in")
                self.mid, self.mid_got = getattr(r, name + "_mid"), getattr(r, name + "_mid_in")
                self.last, self.full = getattr(r, name + "_z"), getattr(r, name + "_full")
                self.stage = 0

            def begin(self):
                self.copies = [wire.send(self.own, self.got, sibling)]

            def step(self):
                for copy in self.copies:
                    copy.wait_recv()
                stage = self.stage
                self.stage += 1
                if stage == 0:
                    self.mid[0] = self.own[core] + self.got[core]
                    self.copies = [wire.send(self.mid.at[0], self.mid_got.at[0], x_peer)]
                elif stage == 1:
                    self.mid[1] = self.mid[0] + self.mid_got[0]
                    self.copies = [wire.send(self.mid.at[1], self.mid_got.at[1], y_peer)]
                elif stage == 2:
                    self.last[zz] = self.mid[1] + self.mid_got[1]
                    mine = self.last.at[zz]
                    self.copies = [
                        wire.send(mine, mine, z_peer((zz + o) % nz)) for o in range(1, nz)
                    ]
                elif stage == 3:
                    total = self.last[0]
                    for o in range(1, nz):
                        total = total + self.last[o]
                    self.full[core] = total
                    mine = self.full.at[core]
                    self.copies = [wire.send(mine, mine, sibling)]
                else:
                    self.sink(jnp.concatenate([self.full[0], self.full[1]], axis=0))

        if fused:
            first_vector, last_vector = Vector("vec_a"), Vector("vec_b")

            def first_sink(sums):
                mine["sums"] = owned(sums)
                for l, at in ((1, 0), (0, 6)):
                    r.skip_gain_grad[l : l + 1, :] = mine["sums"][at : at + 1]
                    r.glu_bias_grad[l : l + 1, :] = mine["sums"][at + 1 : at + 2]
                out_vectors(1, [sums[2 + i : 3 + i, 0:N] for i in range(4)])

            mine = {}
            first_vector.sink = first_sink
            last_vector.sink = lambda sums: out_vectors(0, [sums[i : i + 1] for i in range(4)])
            parts["va"], parts["vb"] = first_vector, last_vector
        waits = {}

        def gain(l):
            return r.norm_gain[l : l + 1, :]

        def skip(l):
            return r.skip_gain[l : l + 1, :]

        def pack_in(l):
            loads[f"wi{l}"].wait()

            def step(i, carry):
                rows = pl.ds(pl.multiple_of(i * BLOCK, BLOCK), BLOCK)
                r.wi[l, rows, :] = r.wi_raw[l, rows].reshape(BLOCK, W)
                return carry

            lax.fori_loop(0, H // BLOCK, step, 0, unroll=4)

        def normalize(l, rows, u):
            inv = lax.rsqrt(jnp.mean(u * u, axis=1, keepdims=True) + EPS)
            unit = u * inv
            r.u[l, rows, :] = u
            r.inv[l, rows, :] = jnp.broadcast_to(inv, (BLOCK, LANES))
            r.unit[l, rows, :] = unit
            r.normed_low[l, rows, :] = (unit * gain(l)).astype(LOW)

        def states(l, between):
            cre = jnp.broadcast_to(disc[l].coef_re, (SUB, N))
            cim = jnp.broadcast_to(disc[l].coef_im, (SUB, N))

            def source(s, first):
                rows = slice(s * SUB, (s + 1) * SUB)
                if first:
                    dre, dim = cmul(cre, cim, r.proj[l, rows, 0:N], r.proj[l, rows, N:W])
                    r.drive[rows, 0:N] = dre
                    r.drive[rows, N:W] = dim
                    return dre, dim
                return r.drive[rows, 0:N], r.drive[rows, N:W]

            def sink(s, yre, yim):
                rows = slice(s * SUB, (s + 1) * SUB)
                r.x[l, rows, 0:N] = yre
                r.x[l, rows, N:W] = yim
                return yre, yim

            sink.dest = (r.right_e, H)
            scan(l, l, l, False, source, between, sink)

        def sigmoid(value):
            return 0.5 + 0.5 * jnp.tanh(0.5 * value)

        def mix(l):
            waits["x", l] = share(l, r.right_e, H, CE)
            loads[f"wo{l}"].wait()
            r.tmp[...] = mm(r.right_e[l, 0:T, H:CE], r.wo[l])
            through = skip(l) * gain(l)

            def gelu(rows):
                mixed = r.tmp[rows, :] + through * r.unit[l, rows, :]
                th = jnp.tanh(mixed * (GELU_A + (GELU_A * GELU_B) * (mixed * mixed)))
                half = 0.5 * mixed
                act = half + half * th
                r.mixed[l, rows, :] = mixed
                r.th[l, rows, :] = th
                r.act[l, rows, :] = act
                r.act_low[l, rows, :] = act.astype(LOW)

            each(gelu)
            loads[f"wg{l}"].wait()
            r.tmp[...] = mm(r.act_low[l], r.wg[l])

        def slope(l):
            def gelu_slope(rows):
                mixed, th = r.mixed[l, rows, :], r.th[l, rows, :]
                inner = mixed * (0.5 * GELU_A + (1.5 * GELU_A * GELU_B) * (mixed * mixed))
                r.slope[l, rows, :] = 0.5 + 0.5 * th + (1.0 - th * th) * inner

            each(gelu_slope)

        def adjoint_in(l):
            waits["gate", l] = share(l, r.right_e, 0, H)
            r.tmp[...] = mm_nt(r.right_e[l, 0:T, 0:H], r.wg[l])

            def gelu(rows):
                act_grad = r.og[rows, :] * r.gate[l, rows, :] + r.tmp[rows, :]
                r.mixed_grad[l, rows, :] = (act_grad * r.slope[l, rows, :]).astype(LOW)

            each(gelu)
            r.xg[...] = mm_nt(r.mixed_grad[l], r.wo[l])

        def beside_adjoint(l):
            sums = [jnp.zeros((SUB, H), F32), jnp.zeros((SUB, H), F32)]

            def add(rows):
                grad = r.mixed_grad[l, rows, :].astype(F32)
                r.mixed_skip[rows, :] = grad * (gain(l) * skip(l))
                grad = grad * r.unit[l, rows, :]
                gate_grad = r.right_e[l, rows, 0:H].astype(F32)
                sums[0] = sums[0] + grad[0:SUB] + grad[SUB:BLOCK]
                sums[1] = sums[1] + gate_grad[0:SUB] + gate_grad[SUB:BLOCK]

            each(add)
            at = 0 if l == 1 else 6
            r.vec_a[at // 4, at % 4, :] = jnp.sum(sums[0], axis=0) * r.norm_gain[l, :]
            r.vec_a[at // 4, at % 4 + 1, :] = jnp.sum(sums[1], axis=0)

        def adjoints(l, between):
            d = disc[l]
            cre = jnp.broadcast_to(d.coef_re, (SUB, N))
            cim = jnp.broadcast_to(d.coef_im, (SUB, N))
            way = 1 - l
            sums = [jnp.zeros((SUB, N), F32) for _ in range(4)]

            def source(s, first):
                rows = slice(s * SUB, (s + 1) * SUB)
                return r.xg[rows, 0:N], r.xg[rows, N:W]

            def sink(s, are, aim):
                rows = slice(s * SUB, (s + 1) * SUB)
                at = s - 1 if l == 0 else s + 1
                if 0 <= at < S:
                    old = slice(at * SUB, (at + 1) * SUB)
                    xre, xim = r.x[l, old, 0:N], r.x[l, old, N:W]
                else:
                    xre, xim = r.x_first[l, :, 0:N], r.x_first[l, :, N:W]
                k = wide(r.keep[l, rows, :], N)
                xre, xim = xre * k, xim * k
                pre, pim = r.proj[l, rows, 0:N], r.proj[l, rows, N:W]
                sums[0] = sums[0] + (are * xre + aim * xim)
                sums[1] = sums[1] + (aim * xre - are * xim)
                sums[2] = sums[2] + (are * pre + aim * pim)
                sums[3] = sums[3] + (aim * pre - are * pim)
                return cre * are + cim * aim, cre * aim - cim * are

            sink.dest = (r.right_n, 0)
            scan(3 - l, l, way, True, source, between, sink)
            pad = jnp.zeros((1, H - N), F32)
            for i in range(4):
                value = jnp.sum(sums[i], axis=0, keepdims=True)
                if l == 1:
                    row = (2 + i) % 4
                    r.vec_a[(2 + i) // 4, row : row + 1, :] = jnp.concatenate([value, pad], axis=1)
                else:
                    r.vec_b[i // 2, i % 2 : i % 2 + 1, :] = value

        def input_grad(l, rows):
            v = gain(l) * r.tmp[rows, :] + r.mixed_skip[rows, :]
            unit = r.unit[l, rows, :]
            along = jnp.mean(unit * v, axis=1, keepdims=True)
            out = r.og[rows, :] + wide(r.inv[l, rows, :], H) * (v - unit * along)
            r.og[rows, :] = out
            return out

        def early_products(l):
            dest = r.p_e if fused else None
            outer(l, r.lt_g, r.rt_g, r.right_e, 0, H, dest, (waits["lg", l], waits["gate", l]), 0)
            outer(l, r.lt_o, r.rt_o, r.right_e, H, CE, dest, (waits["lo", l], waits["x", l]), H)

        def late_products(l):
            dest = r.p_n if fused else None
            outer(l, r.lt_n, r.rt_n, r.right_n, 0, W, dest, (waits["ln", l], waits["pg", l]), CE)

        loads["tok"].wait()
        at = lax.broadcasted_iota(jnp.int32, (T, T), 0)
        of = lax.broadcasted_iota(jnp.int32, (T, T), 1)
        to_rows = jnp.where(of == (at % SUB) * S + at // SUB, 1.0, 0.0).astype(LOW)
        to_time = jnp.where(at == (of % SUB) * S + of // SUB, 1.0, 0.0).astype(LOW)
        r.tmp[...] = mm(to_rows, r.tok[...])
        each(lambda rows: normalize(0, rows, r.tmp[rows, :]))
        pack_in(0)
        r.proj[0] = mm(r.normed_low[0], r.wi[0])

        def fill0():
            pack_in(1)
            waits["ln", 0] = turn(0, r.normed_low.at[0], r.lt_n, r.rt_n)

        states(0, fill0)
        mix(0)

        def between_layers(rows):
            gate = sigmoid(r.tmp[rows, :] + r.glu_bias[0:1, :])
            r.gate[0, rows, :] = gate
            normalize(1, rows, r.u[0, rows, :] + r.act[0, rows, :] * gate)

        each(between_layers)
        r.proj[1] = mm(r.normed_low[1], r.wi[1])

        def fill1():
            waits["lg", 0] = turn(0, r.act_low.at[0], r.lt_g, r.rt_g)
            waits["ln", 1] = turn(1, r.normed_low.at[1], r.lt_n, r.rt_n)
            loads["cot"].wait()
            r.og[...] = mm(to_rows, r.cot[...])
            for j in range(W // LANES):
                r.wi_t[j * LANES : (j + 1) * LANES, :] = r.wi[1, :, j * LANES : (j + 1) * LANES].T
            slope(0)

            def gate_slope(rows):
                gate = r.gate[0, rows, :]
                r.gate_slope[rows, :] = r.act[0, rows, :] * (gate * (1.0 - gate))

            each(gate_slope)

        states(1, fill1)
        mix(1)
        slope(1)

        def last_gate(rows):
            gate = sigmoid(r.tmp[rows, :] + r.glu_bias[1:2, :])
            r.gate[1, rows, :] = gate
            grad = r.og[rows, :] * (r.act[1, rows, :] * (gate * (1.0 - gate)))
            r.right_e[1, rows, 0:H] = grad.astype(LOW)

        each(last_gate)
        adjoint_in(1)

        def run(tokens):
            for token in tokens:
                if token in tasks:
                    tasks[token]()
                elif fused and token[0] == "B":
                    parts[token[1:]].begin()
                elif fused:
                    parts[token].step()

        def task_vec():
            beside_adjoint(0)
            if fused:
                first_vector.begin()

        def task_m0():
            waits["lo", 0] = turn(0, r.mixed_grad.at[0], r.lt_o, r.rt_o)

        def task_out():
            r.tmp[...] = mm_nt(r.right_n[0, 0:T, :], r.wi[0])
            each(lambda rows: input_grad(0, rows))
            for s in range(S):
                for j in range(H // LANES):
                    into = pl.ds(s * (H // LANES) + j, SUB, stride=S * (H // LANES))
                    r.tokens_grad[into, :] = r.og[s * SUB : (s + 1) * SUB, j * LANES : (j + 1) * LANES]

        tasks = {
            "N1": lambda: late_products(1), "V": task_vec, "M0": task_m0, "E0": lambda: early_products(0),
            "N0": lambda: late_products(0), "OUT": task_out, "E1": lambda: early_products(1),
        }

        def fill2():
            waits["lo", 1] = turn(1, r.mixed_grad.at[1], r.lt_o, r.rt_o)
            waits["lg", 1] = turn(1, r.act_low.at[1], r.lt_g, r.rt_g)

            def result(rows):
                out = r.u[1, rows, :] + r.act[1, rows, :] * r.gate[1, rows, :]
                r.act_out[rows, :] = out.astype(LOW)

            each(result)
            beside_adjoint(1)
            run(z.schedule[0])
            r.activations[...] = mm(to_time, r.act_out[...]).astype(LOW)

        adjoints(1, fill2)
        waits["pg", 1] = share(1, r.right_n, 0, W)
        r.tmp[...] = mm(r.right_n[1, 0:T, :], r.wi_t[...])

        def between_adjoints(rows):
            grad = input_grad(1, rows)
            r.right_e[0, rows, 0:H] = (grad * r.gate_slope[rows, :]).astype(LOW)

        each(between_adjoints)
        adjoint_in(0)
        adjoints(0, lambda: run(z.schedule[1]))
        waits["pg", 0] = share(0, r.right_n, 0, W)
        if fused:
            last_vector.begin()
        run(z.schedule[2])

        if not fused:
            r.vector_sums[...] = r.vec_a[...]
            r.last_vector_sums[...] = r.vec_b[...]
            wire.close()
            return

        gains = owned(jnp.concatenate([r.norm_gain[...], r.skip_gain[...], jnp.zeros((4, H), F32)], axis=0))
        diagonal = lax.broadcasted_iota(jnp.int32, (BLOCK, BLOCK), 0) == lax.broadcasted_iota(
            jnp.int32, (BLOCK, BLOCK), 1
        )
        for l, at in ((1, 0), (0, 6)):
            total = jnp.sum(jnp.where(diagonal, sum(along[l]), 0.0), axis=0, keepdims=True)
            total = total + gains[2 + l : 3 + l] * mine["sums"][at : at + 1]
            r.norm_gain_grad[l : l + 1, :] = total / gains[l : l + 1]
        wire.close()

    return kernel


def solution(mesh):
    nseq, nblk = mesh.shape["seq"], mesh.shape["blk"]

    def on_device(
        tokens, lengths, norm_gain, in_proj, out_proj, skip_gain,
        glu_weight, glu_bias, decay_log, frequency, step_log, cotangent,
    ):
        T, streams, H = tokens.shape
        N = decay_log.shape[1]
        W = 2 * N
        CE = H + W
        assert streams == 1 and T == LANES and H == 512
        fused = nseq == 8 and nblk == 4
        plan = {}
        for unit, pieces in PLAN.items():
            first = 0
            cuts = []
            for width, order in pieces:
                cuts.append((first, first + width, order))
                first += width
            assert first == (CE if unit[0] == "e" else W)
            plan[int(unit[1]), unit[0]] = cuts
        z = types.SimpleNamespace(
            T=T, H=H, N=N, S=T // SUB, nseq=nseq, nblk=nblk, fused=fused, plan=plan if fused else {},
            schedule=SCHEDULE,
        )
        any_space = pl.BlockSpec(memory_space=pl.ANY)
        vmem = pl.BlockSpec(memory_space=pltpu.VMEM)
        operands = {
            "tokens": (tokens.reshape(T, H), any_space),
            "lengths": (lengths, any_space),
            "norm_gain": (norm_gain, any_space),
            "in_proj": (in_proj, any_space),
            "out_proj": (out_proj.reshape(2, W, H), any_space),
            "skip_gain": (skip_gain, any_space),
            "glu_weight": (glu_weight, any_space),
            "glu_bias": (glu_bias, any_space),
            "decay_log": (decay_log, any_space),
            "frequency": (frequency, any_space),
            "step_log": (step_log, any_space),
            "cotangent": (cotangent.reshape(T, H), any_space),
        }
        results = {
            "activations": ((T, H), LOW),
            "tokens_grad": ((T * H // LANES, LANES), F32),
        }
        if fused:
            results |= {
                "norm_gain_grad": ((2, BLOCK), F32),
                "in_proj_grad": ((2, BLOCK, 2, N), F32),
                "out_proj_grad": ((2, 2, BLOCK, N), F32),
                "skip_gain_grad": ((2, BLOCK), F32),
                "glu_weight_grad": ((2, BLOCK, H), F32),
                "glu_bias_grad": ((2, BLOCK), F32),
                "decay_log_grad": ((2, N), F32),
                "frequency_grad": ((2, N), F32),
                "step_log_grad": ((2, N), F32),
            }
        else:
            results |= {
                "matrix_sums": ((2, H, CE + W), F32),
                "vector_sums": ((2, 4, H), F32),
                "last_vector_sums": ((2, 2, N), F32),
            }
        dma = pltpu.SemaphoreType.DMA
        scratch = {
            "wi_raw": pltpu.VMEM((2, H, 2, N), LOW),
            "wi": pltpu.VMEM((2, H, W), LOW),
            "wi_t": pltpu.VMEM((W, H), LOW),
            "wo": pltpu.VMEM((2, W, H), LOW),
            "wg": pltpu.VMEM((2, H, H), LOW),
            "tok": pltpu.VMEM((T, H), LOW),
            "cot": pltpu.VMEM((T, H), LOW),
            "u": pltpu.VMEM((2, T, H), F32),
            "inv": pltpu.VMEM((2, T, LANES), F32),
            "unit": pltpu.VMEM((2, T, H), F32),
            "act": pltpu.VMEM((2, T, H), F32),
            "slope": pltpu.VMEM((2, T, H), F32),
            "gate_slope": pltpu.VMEM((T, H), F32),
            "mixed_skip": pltpu.VMEM((T, H), F32),
            "normed_low": pltpu.VMEM((2, T, H), LOW),
            "proj": pltpu.VMEM((2, T, W), F32),
            "drive": pltpu.VMEM((T, W), F32),
            "x": pltpu.VMEM((2, T, W), F32),
            "x_first": pltpu.VMEM((2, SUB, W), F32),
            "mixed": pltpu.VMEM((2, T, H), F32),
            "th": pltpu.VMEM((2, T, H), F32),
            "gate": pltpu.VMEM((2, T, H), F32),
            "act_low": pltpu.VMEM((2, T, H), LOW),
            "act_out": pltpu.VMEM((T, H), LOW),
            "og": pltpu.VMEM((T, H), F32),
            "tmp": pltpu.VMEM((T, H), F32),
            "xg": pltpu.VMEM((T, W), F32),
            "mixed_grad": pltpu.VMEM((2, T, H), LOW),
            "right_e": pltpu.VMEM((2, 2 * T, CE), LOW),
            "right_n": pltpu.VMEM((2, 2 * T, W), LOW),
            "keep": pltpu.VMEM((2, T, LANES), F32),
            "chunk_keep": pltpu.VMEM((2, 3, SUB, LANES), F32),
            "chunk_table": pltpu.VMEM((4, SUB, W), F32),
            "seq_table": pltpu.VMEM((4, nseq, W), F32),
            "carry_out": pltpu.VMEM((4, 1, W), F32),
            "carry_in": pltpu.VMEM((4, nseq, 1, W), F32),
            "vec_a": pltpu.VMEM((2, 4, H), F32),
            "vec_b": pltpu.VMEM((2, 2, N), F32),
        }
        for name in "gon":
            scratch[f"lt_{name}"] = pltpu.VMEM((2, H // 32, 2, BLOCK, LANES), LOW)
            scratch[f"rt_{name}"] = pltpu.VMEM((2, H // 32, BLOCK, LANES), LOW)
        if fused:
            nz = nseq // 2
            for name, width in (("e", CE), ("n", W)):
                scratch[f"p_{name}"] = pltpu.VMEM((2, 2, 2, 2, 2, BLOCK, width), LOW)
            for l, name in plan:
                for i, (first, last, order) in enumerate(plan[l, name]):
                    left = 4
                    for stage, axis in enumerate(order):
                        others = 3 if axis == "z" else 1
                        left -= 2 if axis == "z" else 1
                        shape = (2,) * left + (BLOCK, last - first)
                        scratch[f"got_{name}{l}{i}_{stage}"] = pltpu.VMEM((others,) + shape, LOW)
                        if left:
                            scratch[f"sum_{name}{l}{i}_{stage}"] = pltpu.VMEM(shape, LOW)
            for name, shape in (("vec_a", (4, H)), ("vec_b", (2, N))):
                scratch[name + "_in"] = pltpu.VMEM((2,) + shape, F32)
                scratch[name + "_mid"] = pltpu.VMEM((2,) + shape, F32)
                scratch[name + "_mid_in"] = pltpu.VMEM((2,) + shape, F32)
                scratch[name + "_z"] = pltpu.VMEM((nz,) + shape, F32)
                scratch[name + "_full"] = pltpu.VMEM((2,) + shape, F32)
        links = LINKS if fused else 4 * (nseq - 1)
        scratch["send_sems"] = dma((links,))
        scratch["recv_sems"] = dma((links,))
        scratch["load_sems"] = dma((8 + len(SMALL),))
        for name in SMALL:
            value = operands[name][0]
            space = pltpu.SMEM if name == "lengths" else pltpu.VMEM
            scratch[name + "_here"] = space(value.shape, value.dtype)
        names = list(operands) + list(results) + list(scratch)
        outs = pl.pallas_call(
            make_kernel(names, z),
            out_shape=[(pltpu.VMEM if fused else jax.ShapeDtypeStruct)(*v) for v in results.values()],
            in_specs=[spec for _, spec in operands.values()],
            out_specs=[vmem] * len(results),
            scratch_shapes=list(scratch.values()),
            compiler_params=pltpu.CompilerParams(
                collective_id=0, has_side_effects=True, vmem_limit_bytes=48 * 2**20
            ),
            name="two_layers",
        )(*(pltpu.with_memory_space_constraint(value, pltpu.HBM) for value, _ in operands.values()))
        if fused:
            outs = pl.pallas_call(
                hand_out,
                out_shape=[jax.ShapeDtypeStruct(*v) for v in results.values()],
                in_specs=[vmem] * len(results),
                out_specs=[any_space] * len(results),
                scratch_shapes=[dma((len(results),))],
                name="hand_out",
            )(*(pltpu.with_memory_space_constraint(out, pltpu.VMEM) for out in outs))
        o = types.SimpleNamespace(**dict(zip(results, outs)))
        activations = o.activations.reshape(T, 1, H)
        tokens_grad = o.tokens_grad.reshape(T, 1, H)
        if fused:
            return (
                activations, tokens_grad, o.norm_gain_grad, o.in_proj_grad,
                jnp.swapaxes(o.out_proj_grad, 2, 3), o.skip_gain_grad, o.glu_weight_grad,
                o.glu_bias_grad, o.decay_log_grad, o.frequency_grad, o.step_log_grad,
            )
        both = ("seq", "blk")
        sums = lax.psum_scatter(o.matrix_sums, both, scatter_dimension=1, tiled=True)
        rows = sums.shape[1]
        vectors, last = lax.psum((o.vector_sums.reshape(8, H), o.last_vector_sums.reshape(4, N)), both)
        start = lax.axis_index(both) * rows

        def owned(value, axis):
            return lax.dynamic_slice_in_dim(value, start, rows, axis)

        mine = owned(vectors, 1)
        skip_grad = jnp.stack([mine[6], mine[0]])
        bias_grad = jnp.stack([mine[7], mine[1]])
        totals = [jnp.stack([last[i], vectors[2 + i, 0:N]]) for i in range(4)]
        grads = discretize_grad(discretize(decay_log, frequency, step_log), *totals)
        in_grad = sums[:, :, CE:].reshape(2, rows, 2, N)
        along = jnp.sum(in_grad * owned(in_proj, 1).astype(F32), axis=(2, 3))
        gain_grad = (along + owned(skip_gain, 1) * skip_grad) / owned(norm_gain, 1)
        return (
            activations, tokens_grad, gain_grad, in_grad,
            jnp.moveaxis(sums[:, :, H:CE].reshape(2, rows, 2, N), 1, 3), skip_grad, sums[:, :, 0:H],
            bias_grad, *grads,
        )

    split = P("seq", "blk", None)
    owned = ("seq", "blk")
    return jax.shard_map(
        on_device,
        mesh=mesh,
        in_specs=(split,) + (P(),) * 10 + (split,),
        out_specs=(
            split, split, P(None, owned), P(None, owned, None, None), P(None, None, None, owned),
            P(None, owned), P(None, owned, None), P(None, owned), P(), P(), P(),
        ),
        check_vma=False,
    )
```

```python
import types

import jax
import jax.numpy as jnp
from jax import lax
from jax.experimental import pallas as pl
from jax.experimental.pallas import tpu as pltpu
from jax.sharding import PartitionSpec as P

EPS = 1e-6
F32 = jnp.float32
LOW = jnp.bfloat16
GELU_A = 0.7978845608028654
GELU_B = 0.044715
LANES = 128
SUB = 8
BLOCK = 16
LINKS = 160
SMALL = ("lengths", "norm_gain", "skip_gain", "glu_bias", "decay_log", "frequency", "step_log")

E1, N1, E0, N0, SIDE0, OUT, VECTORS, VA, VB, LOCAL = range(10)
SEND = 100
PLAN = (
    ((384, "ylhx"), (256, "lyxh"), (384, "ylhx"), (256, "zyx"),),
    ((128, "xhly"), (384, "hlxy"), (128, "yxz"), (128, "xhly"),),
    ((128, "lhyx"), (512, "xylh"), (384, "ylhx"), (256, "yxz"),),
    ((256, "yxz"), (256, "xyz"), (256, "xyz"),),
)
SCHEDULE = (
    (E1, SEND + 10, SEND + 11, SEND + 12, SEND + 13,),
    (N1, VECTORS, SIDE0, SEND + 22, SEND + 21, 11, 10, SEND + 20, SEND + 23, VA, E0, SEND + 32, SEND + 33, SEND + 30,
     SEND + 31, LOCAL, 13, 12, 22, 20, 11,),
    (23, OUT, VA, N0, SEND + 40, VB, SEND + 41, 10, SEND + 42, 32, 30, 21, 31, 33, 12, 22, 13, 11, VA, VB, 20, 23, 41,
     40, 10, 32, 42, 31, 30, 21, VB, 33, 13, 41, 12, 40, 10, 11, 20, 22, 23, 42, VA, 21, 32, 30, 31, VA, 12, VB, 20,
     33, 23, 41, 21, VB, 32, 40, 30, 42, 31,),
)


def cmul(are, aim, bre, bim):
    return are * bre - aim * bim, are * bim + aim * bre


def expm1(value):
    series = jnp.ones_like(value)
    for order in range(9, 1, -1):
        series = 1.0 + value * series * (1.0 / order)
    return jnp.where(value > -0.35, value * series, jnp.exp(value) - 1.0)


def discretize(decay, freq, step_log):
    lam_re = -jnp.exp(decay)
    step = jnp.exp(step_log)
    rotation = freq * step
    shrink = expm1(lam_re * step)
    cosine, sine = jnp.cos(rotation), jnp.sin(rotation)
    half = jnp.sin(0.5 * rotation)
    bar_re = (shrink + 1.0) * cosine
    bar_im = (shrink + 1.0) * sine
    minus_re = shrink * cosine - 2.0 * half * half
    scale = 1.0 / (lam_re * lam_re + freq * freq)
    coef_re = (minus_re * lam_re + bar_im * freq) * scale
    coef_im = (bar_im * lam_re - minus_re * freq) * scale
    return types.SimpleNamespace(
        lam_re=lam_re, freq=freq, step=step, scale=scale,
        bar_re=bar_re, bar_im=bar_im, coef_re=coef_re, coef_im=coef_im,
    )


def discretize_grad(d, bar_gre, bar_gim, coef_gre, coef_gim):
    over_re, over_im = d.lam_re * d.scale, d.freq * d.scale
    part_re, part_im = cmul(coef_gre, coef_gim, over_re, over_im)
    all_re, all_im = bar_gre + part_re, bar_gim + part_im
    one_re, one_im = cmul(all_re, all_im, d.bar_re, -d.bar_im)
    two_re, two_im = cmul(part_re, part_im, d.coef_re, -d.coef_im)
    lam_gre = one_re * d.step - two_re
    lam_gim = one_im * d.step - two_im
    step_g = one_re * d.lam_re + one_im * d.freq
    return lam_gre * d.lam_re, lam_gim, step_g * d.step


def mm(a, b):
    return jnp.dot(a, b, preferred_element_type=F32)


def mm_nt(a, b):
    return lax.dot_general(a, b, (((1,), (1,)), ((), ())), preferred_element_type=F32)


def wide(mask, width):
    return jnp.concatenate([mask] * (width // LANES), axis=1)


class Wire:
    def __init__(self, send_sems, recv_sems):
        self.send_sems, self.recv_sems = send_sems, recv_sems
        self.count = 0
        self.open = []

    def send(self, src, dst, device):
        at = self.count
        self.count += 1
        copy = pltpu.make_async_remote_copy(
            src_ref=src, dst_ref=dst,
            send_sem=self.send_sems.at[at], recv_sem=self.recv_sems.at[at],
            device_id=device, device_id_type=pl.DeviceIdType.MESH,
        )
        copy.start()
        self.open.append(copy)
        return copy

    def close(self):
        for copy in self.open:
            copy.wait_send()


def hand_out(*refs):
    count = len(refs) // 2
    copies = [
        pltpu.make_async_copy(refs[i], refs[count + i], refs[-1].at[i]) for i in range(count)
    ]
    for copy in copies:
        copy.start()
    for copy in copies:
        copy.wait()


def make_kernel(names, z):
    T, H, N, S, nseq, nblk, fused = z.T, z.H, z.N, z.S, z.nseq, z.nblk, z.fused
    W = 2 * N
    CE = H + W

    def kernel(*refs):
        r = types.SimpleNamespace(**dict(zip(names, refs, strict=True)))
        seq = lax.axis_index("seq")
        blk = lax.axis_index("blk")
        wire = Wire(r.send_sems, r.recv_sems)
        core, yy = blk % 2, blk // 2
        xx, zz = seq % 2, seq // 2
        nz = nseq // 2
        sibling = {"blk": yy * 2 + (1 - core)}
        y_peer = {"blk": (1 - yy) * 2 + core}
        x_peer = {"seq": zz * 2 + (1 - xx)}

        loads = {}

        def load(name, src, dst):
            copy = pltpu.make_async_copy(src, dst, r.load_sems.at[len(loads)])
            copy.start()
            loads[name] = copy

        load("tok", r.tokens, r.tok)
        for name in SMALL:
            load(name, getattr(r, name), getattr(r, name + "_here"))
            setattr(r, name, getattr(r, name + "_here"))
        load("wi0", r.in_proj.at[0], r.wi_raw.at[0])
        load("wo0", r.out_proj.at[0], r.wo.at[0])
        load("wg0", r.glu_weight.at[0], r.wg.at[0])
        load("wi1", r.in_proj.at[1], r.wi_raw.at[1])
        load("wo1", r.out_proj.at[1], r.wo.at[1])
        load("wg1", r.glu_weight.at[1], r.wg.at[1])
        load("cot", r.cotangent, r.cot)

        barrier = pltpu.get_barrier_semaphore()
        greeted = [{"seq": (seq + o) % nseq} for o in range(1, nseq)]
        if fused:
            greeted += [sibling, y_peer]
        for device in greeted:
            pl.semaphore_signal(barrier, inc=1, device_id=device, device_id_type=pl.DeviceIdType.MESH)

        for name in SMALL:
            loads[name].wait()
        disc, powers = [], []
        for l in range(2):
            d = discretize(
                r.decay_log[l : l + 1, :], r.frequency[l : l + 1, :], r.step_log[l : l + 1, :]
            )
            disc.append(d)
            chain = [(d.bar_re, d.bar_im)]
            while len(chain) < 12:
                chain.append(cmul(*chain[-1], *chain[-1]))
            powers.append(chain)
        step_bits = S.bit_length() - 1
        seg_bits = T.bit_length() - 1

        def power_rows(l, first, exponent, bits):
            rows = exponent.shape[0]
            out_re = jnp.ones((rows, N), F32)
            out_im = jnp.zeros((rows, N), F32)
            for bit in range(bits):
                use = wide(((exponent >> bit) & 1) == 1, N)
                pre, pim = powers[l][first + bit]
                new_re, new_im = cmul(out_re, out_im, pre, pim)
                out_re = jnp.where(use, new_re, out_re)
                out_im = jnp.where(use, new_im, out_im)
            return out_re, out_im

        ends, starts = [], []
        total = jnp.int32(0)
        for i in range(r.lengths.shape[1]):
            starts.append(total)
            total = total + r.lengths[blk, i]
            ends.append(total - 1)

        def keep(position, marks):
            hit = position == marks[0]
            for mark in marks[1:]:
                hit = hit | (position == mark)
            return jnp.where(hit, 0.0, 1.0).astype(F32)

        row = lax.broadcasted_iota(jnp.int32, (T, LANES), 0)
        here = seq * T + (row % SUB) * S + row // SUB
        r.keep[0] = keep(here, starts)
        r.keep[1] = keep(here, ends)
        offset = lax.broadcasted_iota(jnp.int32, (nseq, T), 0)
        lane = lax.broadcasted_iota(jnp.int32, (nseq, T), 1)
        there = ((seq - offset + nseq) % nseq) * T + lane
        k8 = lax.broadcasted_iota(jnp.int32, (SUB, LANES), 0)
        n_row = lax.broadcasted_iota(jnp.int32, (nseq, LANES), 0)
        for way in range(2):
            chunk = jnp.ones((SUB, LANES), F32)
            for s in range(S):
                chunk = chunk * r.keep[way, s * SUB : (s + 1) * SUB, :]
            for level in range(3):
                delta = 1 << level
                if way == 0:
                    inside, rolled = k8 >= delta, pltpu.roll(chunk, delta, 0)
                else:
                    inside, rolled = k8 < SUB - delta, pltpu.roll(chunk, SUB - delta, 0)
                r.chunk_keep[way, level] = jnp.where(inside, chunk, 0.0)
                chunk = jnp.where(inside, chunk * rolled, chunk)
            if way == 0:
                before = jnp.where(k8 >= 1, pltpu.roll(chunk, 1, 0), 1.0)
                chunks_before = k8
            else:
                before = jnp.where(k8 < SUB - 1, pltpu.roll(chunk, SUB - 1, 0), 1.0)
                chunks_before = SUB - 1 - k8
            whole = jnp.min(keep(there, starts if way == 0 else ends), axis=1, keepdims=True)
            whole = jnp.broadcast_to(whole, (nseq, LANES))
            gates = [None] * nseq
            running = jnp.ones((1, LANES), F32)
            for o in range(1, nseq) if way == 0 else range(nseq - 1, 0, -1):
                gates[o] = running
                running = running * whole[o : o + 1, :]
            gates[0] = jnp.zeros((1, LANES), F32)
            gate = jnp.concatenate(gates, axis=0)
            if way == 0:
                valid = (n_row >= 1) & (n_row <= seq)
                hops = n_row - 1
            else:
                valid = n_row > seq
                hops = nseq - 1 - n_row
            gate = jnp.where(valid, gate, 0.0)
            hops = jnp.where(valid, hops, 0)
            for l in range(2):
                index = (0, 2)[l] if way == 0 else (3, 1)[l]
                sign = 1.0 if index < 2 else -1.0
                pre, pim = power_rows(l, step_bits, chunks_before, 3)
                r.chunk_table[index, :, 0:N] = pre * wide(before, N)
                r.chunk_table[index, :, N:W] = pim * wide(before, N) * sign
                pre, pim = power_rows(l, seg_bits, hops, (nseq - 1).bit_length())
                r.seq_table[index, :, 0:N] = pre * wide(gate, N)
                r.seq_table[index, :, N:W] = pim * wide(gate, N) * sign
        for index in range(4):
            r.carry_in[index, 0] = jnp.zeros((1, W), F32)

        def scan(index, l, way, conj, source, between, finish):
            bre, bim = disc[l].bar_re, disc[l].bar_im
            sign = -1.0 if conj else 1.0
            bre = jnp.broadcast_to(bre, (SUB, N))
            bim = jnp.broadcast_to(bim * sign, (SUB, N))
            order = list(range(S)) if way == 0 else list(range(S - 1, -1, -1))

            def advance(s, yre, yim, dre, dim):
                k = wide(r.keep[way, s * SUB : (s + 1) * SUB, :], N)
                pre, pim = cmul(bre, bim, yre * k, yim * k)
                return pre + dre, pim + dim

            yre = jnp.zeros((SUB, N), F32)
            yim = jnp.zeros((SUB, N), F32)
            for s in order:
                dre, dim = source(s, True)
                yre, yim = advance(s, yre, yim, dre, dim)
            for level in range(3):
                delta = 1 << level
                shift = delta if way == 0 else SUB - delta
                m = wide(r.chunk_keep[way, level], N)
                pre, pim = powers[l][step_bits + level]
                gre, gim = cmul(pre, pim * sign, pltpu.roll(yre, shift, 0) * m, pltpu.roll(yim, shift, 0) * m)
                yre, yim = yre + gre, yim + gim
            last = SUB - 1 if way == 0 else 0
            r.carry_out[index, 0:1, 0:N] = yre[last : last + 1, :]
            r.carry_out[index, 0:1, N:W] = yim[last : last + 1, :]
            if index == 0:
                pl.semaphore_wait(barrier, len(greeted))
            copies = [
                wire.send(r.carry_out.at[index], r.carry_in.at[index, o], {"seq": (seq + o) % nseq})
                for o in range(1, nseq)
            ]
            edge = wide(k8 >= 1 if way == 0 else k8 < SUB - 1, N)
            shift = 1 if way == 0 else SUB - 1
            r.shifted[index, :, 0:N] = jnp.where(edge, pltpu.roll(yre, shift, 0), 0.0)
            r.shifted[index, :, N:W] = jnp.where(edge, pltpu.roll(yim, shift, 0), 0.0)

            def local():
                yre, yim = r.shifted[index, :, 0:N], r.shifted[index, :, N:W]
                qre, qim = r.chunk_table[index, :, 0:N], r.chunk_table[index, :, N:W]
                for s in order:
                    rows = slice(s * SUB, (s + 1) * SUB)
                    dre, dim = source(s, False)
                    yre, yim = advance(s, yre, yim, dre, dim)
                    qre, qim = advance(s, qre, qim, 0.0, 0.0)
                    for ref, re, im in ((r.local, yre, yim), (r.factor, qre, qim)):
                        ref[index, rows, 0:N] = re
                        ref[index, rows, N:W] = im
                    if conj:
                        cre, cim = disc[l].coef_re, -disc[l].coef_im
                        for ref, pair in ((r.proj_local, (yre, yim)), (r.proj_factor, (qre, qim))):
                            re, im = cmul(*pair, cre, cim)
                            ref[rows, 0:N] = re
                            ref[rows, N:W] = im

            between(local)
            for copy in copies:
                copy.wait_recv()
            got = r.carry_in[index, :, 0, :]
            gre, gim = cmul(got[:, 0:N], got[:, N:W], r.seq_table[index, :, 0:N], r.seq_table[index, :, N:W])
            gre = jnp.sum(gre, axis=0, keepdims=True)
            gim = jnp.sum(gim, axis=0, keepdims=True)
            r.entered[index, :, 0:N] = gre
            r.entered[index, :, N:W] = gim
            base, factor, out, at = finish

            def add(rows):
                re, im = cmul(factor[rows, 0:N], factor[rows, N:W], gre, gim)
                out[l, rows, at : at + N] = (base[rows, 0:N] + re).astype(LOW)
                out[l, rows, at + N : at + W] = (base[rows, N:W] + im).astype(LOW)

            each(add)

        def state_at(index, rows):
            re, im = cmul(
                r.factor[index, rows, 0:N], r.factor[index, rows, N:W],
                r.entered[index, :, 0:N], r.entered[index, :, N:W],
            )
            return r.local[index, rows, 0:N] + re, r.local[index, rows, N:W] + im

        def each(body):
            for first in range(0, T, BLOCK):
                body(slice(first, first + BLOCK))

        def turn(l, value_ref, lt, rt):
            for j in range(H // LANES):
                block = value_ref[:, j * LANES : (j + 1) * LANES].T
                lt[l, 4 * j : 4 * j + 4] = block.reshape(4, 2, BLOCK, LANES)
            if fused:
                return wire.send(lt.at[l, :, 1 - core], rt.at[l], sibling)

        def share(l, ref, first, last):
            if fused:
                return wire.send(
                    ref.at[l, 0:T, first:last], ref.at[l, T : 2 * T, first:last], sibling
                )

        def outer(l, lt, rt, right, first, last, dest, waits, at):
            if fused:
                for copy in waits:
                    copy.wait_recv()
                mine = lt[l, :, core].reshape(H // 2, LANES)
                left = jnp.concatenate([mine, rt[l].reshape(H // 2, LANES)], axis=1)
                for c in range(first, last, 256):
                    g = mm(left, right[l, :, c : c + 256]).astype(LOW)
                    dest[l, :, :, :, :, :, c : c + 256] = g.reshape(2, 2, 2, 2, BLOCK, 256)
            else:
                left = lt[l].reshape(H, LANES)
                for c in range(first, last, 256):
                    r.matrix_sums[l, :, at + c - first : at + c - first + 256] = mm(
                        left, right[l, 0:T, c : c + 256]
                    )

        hh, ll = zz // 2, zz % 2
        place = {"h": hh, "l": ll, "x": xx, "y": yy}

        def z_peer(at):
            return {"seq": at * 2 + xx}

        def peers(axis):
            if axis == "z":
                others = [(zz + o) % nz for o in range(1, nz)]
                return [({"h": to // 2, "l": to % 2}, z_peer(to)) for to in others]
            device = {
                "x": x_peer, "y": y_peer, "l": z_peer(hh * 2 + 1 - ll), "h": z_peer((1 - hh) * 2 + ll),
            }
            return [({axis: 1 - place[axis]}, device[axis])]

        class Part:
            def __init__(self, whole, first, last, order, got, sums):
                self.ref, self.columns = whole, pl.ds(first, last - first)
                self.axes, self.order, self.stage = "hlxy", order, 0
                self.got, self.sums = got, sums

            def index(self, at):
                return tuple(at.get(a, slice(None)) for a in self.axes) + (slice(None), self.columns)

            def begin(self):
                self.copies = [
                    wire.send(self.ref.at[self.index(at)], self.got[self.stage].at[i], device)
                    for i, (at, device) in enumerate(peers(self.order[self.stage]))
                ]

            def total(self):
                for copy in self.copies:
                    copy.wait_recv()
                axis, got = self.order[self.stage], self.got[self.stage]
                gone = "hl" if axis == "z" else axis
                mine = {a: place[a] for a in gone}
                rest = "".join(a for a in self.axes if a not in gone)
                if not rest:
                    value = self.ref[self.index(mine)].astype(F32)
                    for i in range(len(self.copies)):
                        value = value + got[i].astype(F32)
                    return value
                out = self.sums[self.stage]
                for q in range(2):
                    here = self.ref[self.index(mine | {rest[0]: q})]
                    if len(self.copies) == 1:
                        out[q] = here + got[0, q]
                    else:
                        value = here.astype(F32)
                        for i in range(len(self.copies)):
                            value = value + got[i, q].astype(F32)
                        out[q] = value.astype(LOW)
                self.ref, self.columns, self.axes = out, slice(None), rest
                self.stage += 1

            def step(self):
                value = self.total()
                if value is None:
                    self.begin()
                else:
                    self.sink(value)

        along = {}

        def sink_of(l, whole, first, last):
            def early(value):
                for low, high, out in (
                    (0, H, r.glu_weight_grad.at[l]),
                    (H, H + N, r.out_proj_grad.at[l, 0]),
                    (H + N, CE, r.out_proj_grad.at[l, 1]),
                ):
                    a, b = max(low, first), min(high, last)
                    if a < b:
                        out[:, a - low : b - low] = value[:, a - first : b - first]

            def late(value):
                for c in range(2):
                    a, b = max(c * N, first), min((c + 1) * N, last)
                    if a < b:
                        r.in_proj_grad[l, :, c, a - c * N : b - c * N] = value[:, a - first : b - first]
                weights = r.wi[l, own_rows, first:last].astype(F32)
                along.setdefault(l, []).append(jnp.sum(value * weights, axis=1, keepdims=True))

            return early if whole == "p_e" else late

        parts = {}
        for l, whole, label, first, last, order in z.plan:
            got = [getattr(r, f"got_{label}_{stage}") for stage in range(len(order))]
            sums = [getattr(r, f"sum_{label}_{stage}") for stage in range(len(order) - 1)]
            part = Part(getattr(r, whole).at[l], first, last, order, got, sums)
            part.sink = sink_of(l, whole, first, last)
            parts[label] = part

        device = seq * nblk + blk
        own_rows = pl.ds(pl.multiple_of(device * BLOCK, BLOCK), BLOCK)

        def owned(value):
            return pltpu.roll(value, (H - device * BLOCK) % H, 1)[:, 0:BLOCK]

        def out_vectors(l, totals):
            grads = discretize_grad(disc[l], *totals)
            r.decay_log_grad[l : l + 1, :] = grads[0]
            r.frequency_grad[l : l + 1, :] = grads[1]
            r.step_log_grad[l : l + 1, :] = grads[2]

        class Vector:
            def __init__(self, name):
                self.own, self.got = getattr(r, name), getattr(r, name + "_in")
                self.mid, self.mid_got = getattr(r, name + "_mid"), getattr(r, name + "_mid_in")
                self.last, self.full = getattr(r, name + "_z"), getattr(r, name + "_full")
                self.stage = 0

            def begin(self):
                self.copies = [wire.send(self.own, self.got, sibling)]

            def step(self):
                for copy in self.copies:
                    copy.wait_recv()
                stage = self.stage
                self.stage += 1
                if stage == 0:
                    self.mid[0] = self.own[core] + self.got[core]
                    self.copies = [wire.send(self.mid.at[0], self.mid_got.at[0], x_peer)]
                elif stage == 1:
                    self.mid[1] = self.mid[0] + self.mid_got[0]
                    self.copies = [wire.send(self.mid.at[1], self.mid_got.at[1], y_peer)]
                elif stage == 2:
                    self.last[zz] = self.mid[1] + self.mid_got[1]
                    mine = self.last.at[zz]
                    self.copies = [
                        wire.send(mine, mine, z_peer((zz + o) % nz)) for o in range(1, nz)
                    ]
                elif stage == 3:
                    total = self.last[0]
                    for o in range(1, nz):
                        total = total + self.last[o]
                    self.full[core] = total
                    mine = self.full.at[core]
                    self.copies = [wire.send(mine, mine, sibling)]
                else:
                    self.sink(jnp.concatenate([self.full[0], self.full[1]], axis=0))

        if fused:
            first_vector, last_vector = Vector("vec_a"), Vector("vec_b")

            def first_sink(sums):
                mine["sums"] = owned(sums)
                for l, at in ((1, 0), (0, 6)):
                    r.skip_gain_grad[l : l + 1, :] = mine["sums"][at : at + 1]
                    r.glu_bias_grad[l : l + 1, :] = mine["sums"][at + 1 : at + 2]
                out_vectors(1, [sums[2 + i : 3 + i, 0:N] for i in range(4)])

            mine = {}
            first_vector.sink = first_sink
            last_vector.sink = lambda sums: out_vectors(0, [sums[i : i + 1] for i in range(4)])
            parts[VA], parts[VB] = first_vector, last_vector
        waits = {}

        def gain(l):
            return r.norm_gain[l : l + 1, :]

        def skip(l):
            return r.skip_gain[l : l + 1, :]

        def pack_in(l):
            loads[f"wi{l}"].wait()

            def step(i, carry):
                rows = pl.ds(pl.multiple_of(i * BLOCK, BLOCK), BLOCK)
                r.wi[l, rows, :] = r.wi_raw[l, rows].reshape(BLOCK, W)
                return carry

            lax.fori_loop(0, H // BLOCK, step, 0, unroll=4)

        def normalize(l, rows, u):
            inv = lax.rsqrt(jnp.mean(u * u, axis=1, keepdims=True) + EPS)
            unit = u * inv
            r.u[l, rows, :] = u
            r.inv[l, rows, :] = jnp.broadcast_to(inv, (BLOCK, LANES))
            r.unit[l, rows, :] = unit
            r.normed_low[l, rows, :] = (unit * gain(l)).astype(LOW)

        def states(l, between):
            cre = jnp.broadcast_to(disc[l].coef_re, (SUB, N))
            cim = jnp.broadcast_to(disc[l].coef_im, (SUB, N))

            def source(s, first):
                rows = slice(s * SUB, (s + 1) * SUB)
                if first:
                    dre, dim = cmul(cre, cim, r.proj[l, rows, 0:N], r.proj[l, rows, N:W])
                    r.drive[rows, 0:N] = dre
                    r.drive[rows, N:W] = dim
                    return dre, dim
                return r.drive[rows, 0:N], r.drive[rows, N:W]

            scan(l, l, l, False, source, between, (r.local.at[l], r.factor.at[l], r.right_e, H))

        def sigmoid(value):
            return 0.5 + 0.5 * jnp.tanh(0.5 * value)

        def mix(l):
            waits["x", l] = share(l, r.right_e, H, CE)
            loads[f"wo{l}"].wait()
            r.tmp[...] = mm(r.right_e[l, 0:T, H:CE], r.wo[l])
            through = skip(l) * gain(l)

            def gelu(rows):
                mixed = r.tmp[rows, :] + through * r.unit[l, rows, :]
                th = jnp.tanh(mixed * (GELU_A + (GELU_A * GELU_B) * (mixed * mixed)))
                half = 0.5 * mixed
                act = half + half * th
                r.mixed[l, rows, :] = mixed
                r.th[l, rows, :] = th
                r.act[l, rows, :] = act
                r.act_low[l, rows, :] = act.astype(LOW)

            each(gelu)
            loads[f"wg{l}"].wait()
            r.tmp[...] = mm(r.act_low[l], r.wg[l])

        def slope(l):
            def gelu_slope(rows):
                mixed, th = r.mixed[l, rows, :], r.th[l, rows, :]
                inner = mixed * (0.5 * GELU_A + (1.5 * GELU_A * GELU_B) * (mixed * mixed))
                r.slope[l, rows, :] = 0.5 + 0.5 * th + (1.0 - th * th) * inner

            each(gelu_slope)

        def adjoint_in(l):
            waits["gate", l] = share(l, r.right_e, 0, H)
            r.tmp[...] = mm_nt(r.right_e[l, 0:T, 0:H], r.wg[l])

            def gelu(rows):
                act_grad = r.og[rows, :] * r.gate[l, rows, :] + r.tmp[rows, :]
                r.mixed_grad[l, rows, :] = (act_grad * r.slope[l, rows, :]).astype(LOW)

            each(gelu)
            r.xg[l] = mm_nt(r.mixed_grad[l], r.wo[l])

        def beside_adjoint(l):
            sums = [jnp.zeros((SUB, H), F32), jnp.zeros((SUB, H), F32)]

            def add(rows):
                grad = r.mixed_grad[l, rows, :].astype(F32)
                r.mixed_skip[rows, :] = grad * (gain(l) * skip(l))
                grad = grad * r.unit[l, rows, :]
                gate_grad = r.right_e[l, rows, 0:H].astype(F32)
                sums[0] = sums[0] + grad[0:SUB] + grad[SUB:BLOCK]
                sums[1] = sums[1] + gate_grad[0:SUB] + gate_grad[SUB:BLOCK]

            each(add)
            at = 0 if l == 1 else 6
            r.vec_a[at // 4, at % 4, :] = jnp.sum(sums[0], axis=0) * r.norm_gain[l, :]
            r.vec_a[at // 4, at % 4 + 1, :] = jnp.sum(sums[1], axis=0)

        def adjoints(l, between):
            def source(s, first):
                rows = slice(s * SUB, (s + 1) * SUB)
                return r.xg[l, rows, 0:N], r.xg[l, rows, N:W]

            scan(3 - l, l, 1 - l, True, source, between, (r.proj_local, r.proj_factor, r.right_n, 0))

        def recurrence_sums(l):
            sums = [jnp.zeros((SUB, N), F32) for _ in range(4)]
            re, im = cmul(
                r.chunk_table[l, :, 0:N], r.chunk_table[l, :, N:W],
                r.entered[l, :, 0:N], r.entered[l, :, N:W],
            )
            xre, xim = r.shifted[l, :, 0:N] + re, r.shifted[l, :, N:W] + im
            for s in range(S) if l == 0 else range(S - 1, -1, -1):
                rows = slice(s * SUB, (s + 1) * SUB)
                are, aim = state_at(3 - l, rows)
                k = wide(r.keep[l, rows, :], N)
                xre, xim = xre * k, xim * k
                pre, pim = r.proj[l, rows, 0:N], r.proj[l, rows, N:W]
                sums[0] = sums[0] + (are * xre + aim * xim)
                sums[1] = sums[1] + (aim * xre - are * xim)
                sums[2] = sums[2] + (are * pre + aim * pim)
                sums[3] = sums[3] + (aim * pre - are * pim)
                xre, xim = state_at(l, rows)
            pad = jnp.zeros((1, H - N), F32)
            for i in range(4):
                value = jnp.sum(sums[i], axis=0, keepdims=True)
                if l == 1:
                    row = (2 + i) % 4
                    r.vec_a[(2 + i) // 4, row : row + 1, :] = jnp.concatenate([value, pad], axis=1)
                else:
                    r.vec_b[i // 2, i % 2 : i % 2 + 1, :] = value

        def input_grad(l, rows):
            v = gain(l) * r.tmp[rows, :] + r.mixed_skip[rows, :]
            unit = r.unit[l, rows, :]
            along = jnp.mean(unit * v, axis=1, keepdims=True)
            out = r.og[rows, :] + wide(r.inv[l, rows, :], H) * (v - unit * along)
            r.og[rows, :] = out
            return out

        def early_products(l):
            dest = r.p_e if fused else None
            outer(l, r.lt_g, r.rt_g, r.right_e, 0, H, dest, (waits["lg", l], waits["gate", l]), 0)
            outer(l, r.lt_o, r.rt_o, r.right_e, H, CE, dest, (waits["lo", l], waits["x", l]), H)

        def late_products(l):
            dest = r.p_n if fused else None
            outer(l, r.lt_n, r.rt_n, r.right_n, 0, W, dest, (waits["ln", l], waits["pg", l]), CE)

        loads["tok"].wait()
        at = lax.broadcasted_iota(jnp.int32, (T, T), 0)
        of = lax.broadcasted_iota(jnp.int32, (T, T), 1)
        to_rows = jnp.where(of == (at % SUB) * S + at // SUB, 1.0, 0.0).astype(LOW)
        to_time = jnp.where(at == (of % SUB) * S + of // SUB, 1.0, 0.0).astype(LOW)
        r.tmp[...] = mm(to_rows, r.tok[...])
        each(lambda rows: normalize(0, rows, r.tmp[rows, :]))
        pack_in(0)
        r.proj[0] = mm(r.normed_low[0], r.wi[0])

        def fill0(local):
            local()
            pack_in(1)
            waits["ln", 0] = turn(0, r.normed_low.at[0], r.lt_n, r.rt_n)

        states(0, fill0)
        mix(0)

        def between_layers(rows):
            gate = sigmoid(r.tmp[rows, :] + r.glu_bias[0:1, :])
            r.gate[0, rows, :] = gate
            normalize(1, rows, r.u[0, rows, :] + r.act[0, rows, :] * gate)

        each(between_layers)
        r.proj[1] = mm(r.normed_low[1], r.wi[1])

        def fill1(local):
            local()
            waits["lg", 0] = turn(0, r.act_low.at[0], r.lt_g, r.rt_g)
            waits["ln", 1] = turn(1, r.normed_low.at[1], r.lt_n, r.rt_n)
            loads["cot"].wait()
            r.og[...] = mm(to_rows, r.cot[...])
            for j in range(W // LANES):
                r.wi_t[j * LANES : (j + 1) * LANES, :] = r.wi[1, :, j * LANES : (j + 1) * LANES].T
            slope(0)

            def gate_slope(rows):
                gate = r.gate[0, rows, :]
                r.gate_slope[rows, :] = r.act[0, rows, :] * (gate * (1.0 - gate))

            each(gate_slope)

        states(1, fill1)
        mix(1)
        slope(1)

        def last_gate(rows):
            gate = sigmoid(r.tmp[rows, :] + r.glu_bias[1:2, :])
            r.gate[1, rows, :] = gate
            grad = r.og[rows, :] * (r.act[1, rows, :] * (gate * (1.0 - gate)))
            r.right_e[1, rows, 0:H] = grad.astype(LOW)

        each(last_gate)
        adjoint_in(1)

        def run(tokens):
            for token in tokens:
                if token in tasks:
                    tasks[token]()
                elif fused and token >= SEND:
                    parts[token - SEND].begin()
                elif fused:
                    parts[token].step()

        def task_vec():
            beside_adjoint(0)
            recurrence_sums(1)
            if fused:
                first_vector.begin()

        def task_m0():
            waits["lo", 0] = turn(0, r.mixed_grad.at[0], r.lt_o, r.rt_o)

        def task_out():
            r.tmp[...] = mm_nt(r.right_n[0, 0:T, :], r.wi[0])
            each(lambda rows: input_grad(0, rows))
            for s in range(S):
                for j in range(H // LANES):
                    into = pl.ds(s * (H // LANES) + j, SUB, stride=S * (H // LANES))
                    r.tokens_grad[into, :] = r.og[s * SUB : (s + 1) * SUB, j * LANES : (j + 1) * LANES]

        tasks = {
            N1: lambda: late_products(1), VECTORS: task_vec, SIDE0: task_m0, E0: lambda: early_products(0),
            N0: lambda: late_products(0), OUT: task_out, E1: lambda: early_products(1),
        }

        def fill2(local):
            waits["lo", 1] = turn(1, r.mixed_grad.at[1], r.lt_o, r.rt_o)
            waits["lg", 1] = turn(1, r.act_low.at[1], r.lt_g, r.rt_g)

            def result(rows):
                out = r.u[1, rows, :] + r.act[1, rows, :] * r.gate[1, rows, :]
                r.act_out[rows, :] = out.astype(LOW)

            each(result)
            beside_adjoint(1)
            run(z.schedule[0])
            local()
            r.activations[...] = mm(to_time, r.act_out[...]).astype(LOW)

        adjoints(1, fill2)
        waits["pg", 1] = share(1, r.right_n, 0, W)
        r.tmp[...] = mm(r.right_n[1, 0:T, :], r.wi_t[...])

        def between_adjoints(rows):
            grad = input_grad(1, rows)
            r.right_e[0, rows, 0:H] = (grad * r.gate_slope[rows, :]).astype(LOW)

        each(between_adjoints)
        adjoint_in(0)

        def fill3(local):
            tasks[LOCAL] = local
            run(z.schedule[1])

        adjoints(0, fill3)
        waits["pg", 0] = share(0, r.right_n, 0, W)
        recurrence_sums(0)
        if fused:
            last_vector.begin()
        run(z.schedule[2])

        if not fused:
            r.vector_sums[...] = r.vec_a[...]
            r.last_vector_sums[...] = r.vec_b[...]
            wire.close()
            return

        gains = owned(jnp.concatenate([r.norm_gain[...], r.skip_gain[...], jnp.zeros((4, H), F32)], axis=0))
        diagonal = lax.broadcasted_iota(jnp.int32, (BLOCK, BLOCK), 0) == lax.broadcasted_iota(
            jnp.int32, (BLOCK, BLOCK), 1
        )
        for l, at in ((1, 0), (0, 6)):
            total = jnp.sum(jnp.where(diagonal, sum(along[l]), 0.0), axis=0, keepdims=True)
            total = total + gains[2 + l : 3 + l] * mine["sums"][at : at + 1]
            r.norm_gain_grad[l : l + 1, :] = total / gains[l : l + 1]
        wire.close()

    return kernel


def solution(mesh):
    nseq, nblk = mesh.shape["seq"], mesh.shape["blk"]

    def on_device(
        tokens, lengths, norm_gain, in_proj, out_proj, skip_gain,
        glu_weight, glu_bias, decay_log, frequency, step_log, cotangent,
    ):
        T, streams, H = tokens.shape
        N = decay_log.shape[1]
        W = 2 * N
        CE = H + W
        assert streams == 1 and T == LANES and H == 512
        fused = nseq == 8 and nblk == 4
        plan = []
        for unit, pieces in enumerate(PLAN if fused else ()):
            first = 0
            for i, (width, order) in enumerate(pieces):
                whole = ("p_e", "p_n")[unit % 2]
                plan.append((1 - unit // 2, whole, 10 * (unit + 1) + i, first, first + width, order))
                first += width
            assert first == (CE, W)[unit % 2]
        z = types.SimpleNamespace(
            T=T, H=H, N=N, S=T // SUB, nseq=nseq, nblk=nblk, fused=fused, plan=plan,
            schedule=SCHEDULE,
        )
        any_space = pl.BlockSpec(memory_space=pl.ANY)
        vmem = pl.BlockSpec(memory_space=pltpu.VMEM)
        operands = dict(
            tokens=(tokens.reshape(T, H), any_space),
            lengths=(lengths, any_space),
            norm_gain=(norm_gain, any_space),
            in_proj=(in_proj, any_space),
            out_proj=(out_proj.reshape(2, W, H), any_space),
            skip_gain=(skip_gain, any_space),
            glu_weight=(glu_weight, any_space),
            glu_bias=(glu_bias, any_space),
            decay_log=(decay_log, any_space),
            frequency=(frequency, any_space),
            step_log=(step_log, any_space),
            cotangent=(cotangent.reshape(T, H), any_space),
        )
        results = dict(
            activations=((T, H), LOW),
            tokens_grad=((T * H // LANES, LANES), F32),
        )
        if fused:
            results |= dict(
                norm_gain_grad=((2, BLOCK), F32),
                in_proj_grad=((2, BLOCK, 2, N), F32),
                out_proj_grad=((2, 2, BLOCK, N), F32),
                skip_gain_grad=((2, BLOCK), F32),
                glu_weight_grad=((2, BLOCK, H), F32),
                glu_bias_grad=((2, BLOCK), F32),
                decay_log_grad=((2, N), F32),
                frequency_grad=((2, N), F32),
                step_log_grad=((2, N), F32),
            )
        else:
            results |= dict(
                matrix_sums=((2, H, CE + W), F32),
                vector_sums=((2, 4, H), F32),
                last_vector_sums=((2, 2, N), F32),
            )
        dma = pltpu.SemaphoreType.DMA
        scratch = dict(
            wi_raw=pltpu.VMEM((2, H, 2, N), LOW),
            wi=pltpu.VMEM((2, H, W), LOW),
            wi_t=pltpu.VMEM((W, H), LOW),
            wo=pltpu.VMEM((2, W, H), LOW),
            wg=pltpu.VMEM((2, H, H), LOW),
            tok=pltpu.VMEM((T, H), LOW),
            cot=pltpu.VMEM((T, H), LOW),
            u=pltpu.VMEM((2, T, H), F32),
            inv=pltpu.VMEM((2, T, LANES), F32),
            unit=pltpu.VMEM((2, T, H), F32),
            act=pltpu.VMEM((2, T, H), F32),
            slope=pltpu.VMEM((2, T, H), F32),
            gate_slope=pltpu.VMEM((T, H), F32),
            mixed_skip=pltpu.VMEM((T, H), F32),
            normed_low=pltpu.VMEM((2, T, H), LOW),
            proj=pltpu.VMEM((2, T, W), F32),
            drive=pltpu.VMEM((T, W), F32),
            shifted=pltpu.VMEM((4, SUB, W), F32),
            local=pltpu.VMEM((4, T, W), F32),
            factor=pltpu.VMEM((4, T, W), F32),
            entered=pltpu.VMEM((4, 1, W), F32),
            proj_local=pltpu.VMEM((T, W), F32),
            proj_factor=pltpu.VMEM((T, W), F32),
            mixed=pltpu.VMEM((2, T, H), F32),
            th=pltpu.VMEM((2, T, H), F32),
            gate=pltpu.VMEM((2, T, H), F32),
            act_low=pltpu.VMEM((2, T, H), LOW),
            act_out=pltpu.VMEM((T, H), LOW),
            og=pltpu.VMEM((T, H), F32),
            tmp=pltpu.VMEM((T, H), F32),
            xg=pltpu.VMEM((2, T, W), F32),
            mixed_grad=pltpu.VMEM((2, T, H), LOW),
            right_e=pltpu.VMEM((2, 2 * T, CE), LOW),
            right_n=pltpu.VMEM((2, 2 * T, W), LOW),
            keep=pltpu.VMEM((2, T, LANES), F32),
            chunk_keep=pltpu.VMEM((2, 3, SUB, LANES), F32),
            chunk_table=pltpu.VMEM((4, SUB, W), F32),
            seq_table=pltpu.VMEM((4, nseq, W), F32),
            carry_out=pltpu.VMEM((4, 1, W), F32),
            carry_in=pltpu.VMEM((4, nseq, 1, W), F32),
            vec_a=pltpu.VMEM((2, 4, H), F32),
            vec_b=pltpu.VMEM((2, 2, N), F32),
        )
        for name in "gon":
            scratch[f"lt_{name}"] = pltpu.VMEM((2, H // 32, 2, BLOCK, LANES), LOW)
            scratch[f"rt_{name}"] = pltpu.VMEM((2, H // 32, BLOCK, LANES), LOW)
        if fused:
            nz = nseq // 2
            for name, width in (("e", CE), ("n", W)):
                scratch[f"p_{name}"] = pltpu.VMEM((2, 2, 2, 2, 2, BLOCK, width), LOW)
            for _, _, label, first, last, order in plan:
                left = 4
                for stage, axis in enumerate(order):
                    others = 3 if axis == "z" else 1
                    left -= 2 if axis == "z" else 1
                    shape = (2,) * left + (BLOCK, last - first)
                    scratch[f"got_{label}_{stage}"] = pltpu.VMEM((others,) + shape, LOW)
                    if left:
                        scratch[f"sum_{label}_{stage}"] = pltpu.VMEM(shape, LOW)
            for name, shape in (("vec_a", (4, H)), ("vec_b", (2, N))):
                scratch[name + "_in"] = pltpu.VMEM((2,) + shape, F32)
                scratch[name + "_mid"] = pltpu.VMEM((2,) + shape, F32)
                scratch[name + "_mid_in"] = pltpu.VMEM((2,) + shape, F32)
                scratch[name + "_z"] = pltpu.VMEM((nz,) + shape, F32)
                scratch[name + "_full"] = pltpu.VMEM((2,) + shape, F32)
        links = LINKS if fused else 4 * (nseq - 1)
        scratch["send_sems"] = dma((links,))
        scratch["recv_sems"] = dma((links,))
        scratch["load_sems"] = dma((8 + len(SMALL),))
        for name in SMALL:
            value = operands[name][0]
            space = pltpu.SMEM if name == "lengths" else pltpu.VMEM
            scratch[name + "_here"] = space(value.shape, value.dtype)
        names = list(operands) + list(results) + list(scratch)
        outs = pl.pallas_call(
            make_kernel(names, z),
            out_shape=[(pltpu.VMEM if fused else jax.ShapeDtypeStruct)(*v) for v in results.values()],
            in_specs=[spec for _, spec in operands.values()],
            out_specs=[vmem] * len(results),
            scratch_shapes=list(scratch.values()),
            compiler_params=pltpu.CompilerParams(
                collective_id=0, has_side_effects=True, vmem_limit_bytes=48 * 2**20
            ),
            name="two_layers",
        )(*(pltpu.with_memory_space_constraint(value, pltpu.HBM) for value, _ in operands.values()))
        if fused:
            outs = pl.pallas_call(
                hand_out,
                out_shape=[jax.ShapeDtypeStruct(*v) for v in results.values()],
                in_specs=[vmem] * len(results),
                out_specs=[any_space] * len(results),
                scratch_shapes=[dma((len(results),))],
                name="hand_out",
            )(*(pltpu.with_memory_space_constraint(out, pltpu.VMEM) for out in outs))
        o = types.SimpleNamespace(**dict(zip(results, outs)))
        activations = o.activations.reshape(T, 1, H)
        tokens_grad = o.tokens_grad.reshape(T, 1, H)
        if fused:
            return (
                activations, tokens_grad, o.norm_gain_grad, o.in_proj_grad,
                jnp.swapaxes(o.out_proj_grad, 2, 3), o.skip_gain_grad, o.glu_weight_grad,
                o.glu_bias_grad, o.decay_log_grad, o.frequency_grad, o.step_log_grad,
            )
        both = ("seq", "blk")
        sums = lax.psum_scatter(o.matrix_sums, both, scatter_dimension=1, tiled=True)
        rows = sums.shape[1]
        vectors, last = lax.psum((o.vector_sums.reshape(8, H), o.last_vector_sums.reshape(4, N)), both)
        start = lax.axis_index(both) * rows

        def owned(value, axis):
            return lax.dynamic_slice_in_dim(value, start, rows, axis)

        mine = owned(vectors, 1)
        skip_grad = jnp.stack([mine[6], mine[0]])
        bias_grad = jnp.stack([mine[7], mine[1]])
        totals = [jnp.stack([last[i], vectors[2 + i, 0:N]]) for i in range(4)]
        grads = discretize_grad(discretize(decay_log, frequency, step_log), *totals)
        in_grad = sums[:, :, CE:].reshape(2, rows, 2, N)
        along = jnp.sum(in_grad * owned(in_proj, 1).astype(F32), axis=(2, 3))
        gain_grad = (along + owned(skip_gain, 1) * skip_grad) / owned(norm_gain, 1)
        return (
            activations, tokens_grad, gain_grad, in_grad,
            jnp.moveaxis(sums[:, :, H:CE].reshape(2, rows, 2, N), 1, 3), skip_grad, sums[:, :, 0:H],
            bias_grad, *grads,
        )

    split = P("seq", "blk", None)
    owned = ("seq", "blk")
    return jax.shard_map(
        on_device,
        mesh=mesh,
        in_specs=(split,) + (P(),) * 10 + (split,),
        out_specs=(
            split, split, P(None, owned), P(None, owned, None, None), P(None, None, None, owned),
            P(None, owned), P(None, owned, None), P(None, owned), P(), P(), P(),
        ),
        check_vma=False,
    )
```

```python
import types

import jax
import jax.numpy as jnp
from jax import lax
from jax.experimental import pallas as pl
from jax.experimental.pallas import tpu as pltpu
from jax.sharding import PartitionSpec as P

EPS = 1e-6
F32 = jnp.float32
LOW = jnp.bfloat16
GELU_A = 0.7978845608028654
GELU_B = 0.044715
LANES = 128
SUB = 8
BLOCK = 16
LINKS = 160
SMALL = ("lengths", "norm_gain", "skip_gain", "glu_bias", "decay_log", "frequency", "step_log")

E1, N1, E0, N0, SIDE0, OUT, VECTORS, VA, VB, LOCAL, O0 = range(11)
SEND = 100
PLAN = (
    ((384, "xlhy"), (256, "zyx"), (256, "lyxh"), (384, "yxlh"),),
    ((384, "zyx"), (384, "yhlx"),),
    ((512, "xlyh"),),
    ((256, "yxz"), (256, "xyz"), (128, "yxz"), (128, "xzy"),),
    ((128, "lxh"), (128, "xlh"), (128, "lxh"), (384, "xz"),),
)
SCHEDULE = (
    (E1, SEND + 20, SEND + 21, SEND + 22, SEND + 23,),
    (N1, VECTORS, SIDE0, SEND + 31, 20, SEND + 30, 23, VA, 21, E0, SEND + 40, LOCAL, 22, 20, 23, O0,),
    (SEND + 61, SEND + 63, VA, SEND + 60, SEND + 62, OUT, N0, VB, SEND + 51, SEND + 53, 31, SEND + 52, SEND + 50, 21,
     40, 22, 30, 61, VA, 23, 20, 63, 60, VB, 62, 52, 51, 53, 50, 31, 21, 30, 40, 22, 60, 20, 62, 61, VB, 52, 51, 23,
     VA, 50, 63, VA, 30, 31, 40, 53, 22, 60, 62, 61, VB, 52, 51, 31, VB, 50, 53, 40,),
)


def cmul(are, aim, bre, bim):
    return are * bre - aim * bim, are * bim + aim * bre


def expm1(value):
    series = jnp.ones_like(value)
    for order in range(9, 1, -1):
        series = 1.0 + value * series * (1.0 / order)
    return jnp.where(value > -0.35, value * series, jnp.exp(value) - 1.0)


def discretize(decay, freq, step_log):
    lam_re = -jnp.exp(decay)
    step = jnp.exp(step_log)
    rotation = freq * step
    shrink = expm1(lam_re * step)
    cosine, sine = jnp.cos(rotation), jnp.sin(rotation)
    half = jnp.sin(0.5 * rotation)
    bar_re = (shrink + 1.0) * cosine
    bar_im = (shrink + 1.0) * sine
    minus_re = shrink * cosine - 2.0 * half * half
    scale = 1.0 / (lam_re * lam_re + freq * freq)
    coef_re = (minus_re * lam_re + bar_im * freq) * scale
    coef_im = (bar_im * lam_re - minus_re * freq) * scale
    return types.SimpleNamespace(
        lam_re=lam_re, freq=freq, step=step, scale=scale,
        bar_re=bar_re, bar_im=bar_im, coef_re=coef_re, coef_im=coef_im,
    )


def discretize_grad(d, bar_gre, bar_gim, coef_gre, coef_gim):
    over_re, over_im = d.lam_re * d.scale, d.freq * d.scale
    part_re, part_im = cmul(coef_gre, coef_gim, over_re, over_im)
    all_re, all_im = bar_gre + part_re, bar_gim + part_im
    one_re, one_im = cmul(all_re, all_im, d.bar_re, -d.bar_im)
    two_re, two_im = cmul(part_re, part_im, d.coef_re, -d.coef_im)
    lam_gre = one_re * d.step - two_re
    lam_gim = one_im * d.step - two_im
    step_g = one_re * d.lam_re + one_im * d.freq
    return lam_gre * d.lam_re, lam_gim, step_g * d.step


def mm(a, b):
    return jnp.dot(a, b, preferred_element_type=F32)


def mm_nt(a, b):
    return lax.dot_general(a, b, (((1,), (1,)), ((), ())), preferred_element_type=F32)


def wide(mask, width):
    return jnp.concatenate([mask] * (width // LANES), axis=1)


class Wire:
    def __init__(self, send_sems, recv_sems):
        self.send_sems, self.recv_sems = send_sems, recv_sems
        self.count = 0
        self.open = []

    def send(self, src, dst, device):
        at = self.count
        self.count += 1
        copy = pltpu.make_async_remote_copy(
            src_ref=src, dst_ref=dst,
            send_sem=self.send_sems.at[at], recv_sem=self.recv_sems.at[at],
            device_id=device, device_id_type=pl.DeviceIdType.MESH,
        )
        copy.start()
        self.open.append(copy)
        return copy

    def close(self):
        for copy in self.open:
            copy.wait_send()


def hand_out(*refs):
    count = len(refs) // 2
    copies = [
        pltpu.make_async_copy(refs[i], refs[count + i], refs[-1].at[i]) for i in range(count)
    ]
    for copy in copies:
        copy.start()
    for copy in copies:
        copy.wait()


def make_kernel(names, z):
    T, H, N, S, nseq, nblk, fused = z.T, z.H, z.N, z.S, z.nseq, z.nblk, z.fused
    W = 2 * N
    CE = H + W

    def kernel(*refs):
        r = types.SimpleNamespace(**dict(zip(names, refs, strict=True)))
        seq = lax.axis_index("seq")
        blk = lax.axis_index("blk")
        wire = Wire(r.send_sems, r.recv_sems)
        core, yy = blk % 2, blk // 2
        xx, zz = seq % 2, seq // 2
        nz = nseq // 2
        sibling = {"blk": yy * 2 + (1 - core)}
        y_peer = {"blk": (1 - yy) * 2 + core}
        across = {"blk": (1 - yy) * 2 + (1 - core)}
        x_peer = {"seq": zz * 2 + (1 - xx)}

        loads = {}

        def load(name, src, dst):
            copy = pltpu.make_async_copy(src, dst, r.load_sems.at[len(loads)])
            copy.start()
            loads[name] = copy

        load("tok", r.tokens, r.tok)
        for name in SMALL:
            load(name, getattr(r, name), getattr(r, name + "_here"))
            setattr(r, name, getattr(r, name + "_here"))
        load("wi0", r.in_proj.at[0], r.wi_raw.at[0])
        load("wo0", r.out_proj.at[0], r.wo.at[0])
        load("wg0", r.glu_weight.at[0], r.wg.at[0])
        load("wi1", r.in_proj.at[1], r.wi_raw.at[1])
        load("wo1", r.out_proj.at[1], r.wo.at[1])
        load("wg1", r.glu_weight.at[1], r.wg.at[1])
        load("cot", r.cotangent, r.cot)

        barrier = pltpu.get_barrier_semaphore()
        greeted = [{"seq": (seq + o) % nseq} for o in range(1, nseq)]
        if fused:
            greeted += [sibling, y_peer, across]
        for device in greeted:
            pl.semaphore_signal(barrier, inc=1, device_id=device, device_id_type=pl.DeviceIdType.MESH)

        for name in SMALL:
            loads[name].wait()
        disc, powers = [], []
        for l in range(2):
            d = discretize(
                r.decay_log[l : l + 1, :], r.frequency[l : l + 1, :], r.step_log[l : l + 1, :]
            )
            disc.append(d)
            chain = [(d.bar_re, d.bar_im)]
            while len(chain) < 12:
                chain.append(cmul(*chain[-1], *chain[-1]))
            powers.append(chain)
        step_bits = S.bit_length() - 1
        seg_bits = T.bit_length() - 1

        def power_rows(l, first, exponent, bits):
            rows = exponent.shape[0]
            out_re = jnp.ones((rows, N), F32)
            out_im = jnp.zeros((rows, N), F32)
            for bit in range(bits):
                use = wide(((exponent >> bit) & 1) == 1, N)
                pre, pim = powers[l][first + bit]
                new_re, new_im = cmul(out_re, out_im, pre, pim)
                out_re = jnp.where(use, new_re, out_re)
                out_im = jnp.where(use, new_im, out_im)
            return out_re, out_im

        ends, starts = [], []
        total = jnp.int32(0)
        for i in range(r.lengths.shape[1]):
            starts.append(total)
            total = total + r.lengths[blk, i]
            ends.append(total - 1)

        def keep(position, marks):
            hit = position == marks[0]
            for mark in marks[1:]:
                hit = hit | (position == mark)
            return jnp.where(hit, 0.0, 1.0).astype(F32)

        row = lax.broadcasted_iota(jnp.int32, (T, LANES), 0)
        here = seq * T + (row % SUB) * S + row // SUB
        r.keep[0] = keep(here, starts)
        r.keep[1] = keep(here, ends)
        offset = lax.broadcasted_iota(jnp.int32, (nseq, T), 0)
        lane = lax.broadcasted_iota(jnp.int32, (nseq, T), 1)
        there = ((seq - offset + nseq) % nseq) * T + lane
        k8 = lax.broadcasted_iota(jnp.int32, (SUB, LANES), 0)
        n_row = lax.broadcasted_iota(jnp.int32, (nseq, LANES), 0)
        for way in range(2):
            chunk = jnp.ones((SUB, LANES), F32)
            for s in range(S):
                chunk = chunk * r.keep[way, s * SUB : (s + 1) * SUB, :]
            for level in range(3):
                delta = 1 << level
                if way == 0:
                    inside, rolled = k8 >= delta, pltpu.roll(chunk, delta, 0)
                else:
                    inside, rolled = k8 < SUB - delta, pltpu.roll(chunk, SUB - delta, 0)
                r.chunk_keep[way, level] = jnp.where(inside, chunk, 0.0)
                chunk = jnp.where(inside, chunk * rolled, chunk)
            if way == 0:
                before = jnp.where(k8 >= 1, pltpu.roll(chunk, 1, 0), 1.0)
                chunks_before = k8
            else:
                before = jnp.where(k8 < SUB - 1, pltpu.roll(chunk, SUB - 1, 0), 1.0)
                chunks_before = SUB - 1 - k8
            whole = jnp.min(keep(there, starts if way == 0 else ends), axis=1, keepdims=True)
            whole = jnp.broadcast_to(whole, (nseq, LANES))
            gates = [None] * nseq
            running = jnp.ones((1, LANES), F32)
            for o in range(1, nseq) if way == 0 else range(nseq - 1, 0, -1):
                gates[o] = running
                running = running * whole[o : o + 1, :]
            gates[0] = jnp.zeros((1, LANES), F32)
            gate = jnp.concatenate(gates, axis=0)
            if way == 0:
                valid = (n_row >= 1) & (n_row <= seq)
                hops = n_row - 1
            else:
                valid = n_row > seq
                hops = nseq - 1 - n_row
            gate = jnp.where(valid, gate, 0.0)
            hops = jnp.where(valid, hops, 0)
            for l in range(2):
                index = (0, 2)[l] if way == 0 else (3, 1)[l]
                sign = 1.0 if index < 2 else -1.0
                pre, pim = power_rows(l, step_bits, chunks_before, 3)
                r.chunk_table[index, :, 0:N] = pre * wide(before, N)
                r.chunk_table[index, :, N:W] = pim * wide(before, N) * sign
                pre, pim = power_rows(l, seg_bits, hops, (nseq - 1).bit_length())
                r.seq_table[index, :, 0:N] = pre * wide(gate, N)
                r.seq_table[index, :, N:W] = pim * wide(gate, N) * sign
        for index in range(4):
            r.carry_in[index, 0] = jnp.zeros((1, W), F32)

        def scan(index, l, way, conj, source, between, finish):
            bre, bim = disc[l].bar_re, disc[l].bar_im
            sign = -1.0 if conj else 1.0
            bre = jnp.broadcast_to(bre, (SUB, N))
            bim = jnp.broadcast_to(bim * sign, (SUB, N))
            order = list(range(S)) if way == 0 else list(range(S - 1, -1, -1))

            def advance(s, yre, yim, dre, dim):
                k = wide(r.keep[way, s * SUB : (s + 1) * SUB, :], N)
                pre, pim = cmul(bre, bim, yre * k, yim * k)
                return pre + dre, pim + dim

            yre = jnp.zeros((SUB, N), F32)
            yim = jnp.zeros((SUB, N), F32)
            for s in order:
                dre, dim = source(s, True)
                yre, yim = advance(s, yre, yim, dre, dim)
            for level in range(3):
                delta = 1 << level
                shift = delta if way == 0 else SUB - delta
                m = wide(r.chunk_keep[way, level], N)
                pre, pim = powers[l][step_bits + level]
                gre, gim = cmul(pre, pim * sign, pltpu.roll(yre, shift, 0) * m, pltpu.roll(yim, shift, 0) * m)
                yre, yim = yre + gre, yim + gim
            last = SUB - 1 if way == 0 else 0
            r.carry_out[index, 0:1, 0:N] = yre[last : last + 1, :]
            r.carry_out[index, 0:1, N:W] = yim[last : last + 1, :]
            if index == 0:
                pl.semaphore_wait(barrier, len(greeted))
            copies = [
                wire.send(r.carry_out.at[index], r.carry_in.at[index, o], {"seq": (seq + o) % nseq})
                for o in range(1, nseq)
            ]
            edge = wide(k8 >= 1 if way == 0 else k8 < SUB - 1, N)
            shift = 1 if way == 0 else SUB - 1
            r.shifted[index, :, 0:N] = jnp.where(edge, pltpu.roll(yre, shift, 0), 0.0)
            r.shifted[index, :, N:W] = jnp.where(edge, pltpu.roll(yim, shift, 0), 0.0)

            def local():
                yre, yim = r.shifted[index, :, 0:N], r.shifted[index, :, N:W]
                qre, qim = r.chunk_table[index, :, 0:N], r.chunk_table[index, :, N:W]
                for s in order:
                    rows = slice(s * SUB, (s + 1) * SUB)
                    dre, dim = source(s, False)
                    yre, yim = advance(s, yre, yim, dre, dim)
                    qre, qim = advance(s, qre, qim, 0.0, 0.0)
                    for ref, re, im in ((r.local, yre, yim), (r.factor, qre, qim)):
                        ref[index, rows, 0:N] = re
                        ref[index, rows, N:W] = im
                    if conj:
                        cre, cim = disc[l].coef_re, -disc[l].coef_im
                        for ref, pair in ((r.proj_local, (yre, yim)), (r.proj_factor, (qre, qim))):
                            re, im = cmul(*pair, cre, cim)
                            ref[rows, 0:N] = re
                            ref[rows, N:W] = im

            between(local)
            for copy in copies:
                copy.wait_recv()
            got = r.carry_in[index, :, 0, :]
            gre, gim = cmul(got[:, 0:N], got[:, N:W], r.seq_table[index, :, 0:N], r.seq_table[index, :, N:W])
            gre = jnp.sum(gre, axis=0, keepdims=True)
            gim = jnp.sum(gim, axis=0, keepdims=True)
            r.entered[index, :, 0:N] = gre
            r.entered[index, :, N:W] = gim
            base, factor, out, at = finish

            def add(rows):
                re, im = cmul(factor[rows, 0:N], factor[rows, N:W], gre, gim)
                out[rows, at : at + N] = (base[rows, 0:N] + re).astype(LOW)
                out[rows, at + N : at + W] = (base[rows, N:W] + im).astype(LOW)

            each(add)

        def state_at(index, rows):
            re, im = cmul(
                r.factor[index, rows, 0:N], r.factor[index, rows, N:W],
                r.entered[index, :, 0:N], r.entered[index, :, N:W],
            )
            return r.local[index, rows, 0:N] + re, r.local[index, rows, N:W] + im

        def each(body):
            for first in range(0, T, BLOCK):
                body(slice(first, first + BLOCK))

        def turn(l, value_ref, lt, rt):
            for j in range(H // LANES):
                block = value_ref[:, j * LANES : (j + 1) * LANES].T
                lt[l, 4 * j : 4 * j + 4] = block.reshape(4, 2, BLOCK, LANES)
            if fused:
                return wire.send(lt.at[l, :, 1 - core], rt.at[l], sibling)

        def share(l, ref, first, last):
            if fused:
                return wire.send(
                    ref.at[l, 0:T, first:last], ref.at[l, T : 2 * T, first:last], sibling
                )

        four = (sibling, y_peer, across)
        block_of = ((yy, 1 - core), (1 - yy, core), (1 - yy, 1 - core))

        def share_four(ref):
            if fused:
                return [wire.send(ref.at[0], ref.at[m + 1], device) for m, device in enumerate(four)]

        def turn_four(value_ref):
            for j in range(H // LANES):
                block = value_ref[:, j * LANES : (j + 1) * LANES].T
                r.lt_y[2 * j : 2 * j + 2] = block.reshape(2, 2, 2, BLOCK, LANES)
            if fused:
                return [
                    wire.send(r.lt_y.at[:, block_of[m][0], block_of[m][1]], r.rt_y.at[m], device)
                    for m, device in enumerate(four)
                ]

        def outer_four():
            if fused:
                for copy in waits["lo", 0] + waits["x", 0]:
                    copy.wait_recv()
                rows = H // 4
                left = [r.lt_y[:, yy, core].reshape(rows, LANES)]
                left += [r.rt_y[m].reshape(rows, LANES) for m in range(3)]
                left = jnp.concatenate(left, axis=1)
                for c in range(0, W, 256):
                    g = mm(left, r.right_o[:, :, c : c + 256].reshape(4 * T, 256)).astype(LOW)
                    r.p_o[0, :, :, :, :, c : c + 256] = g.reshape(2, 2, 2, BLOCK, 256)
            else:
                left = r.lt_y[...].reshape(H, LANES)
                for c in range(0, W, 256):
                    r.matrix_sums[0, :, H + c : H + c + 256] = mm(left, r.right_o[0, :, c : c + 256])

        def outer(l, lt, rt, right, first, last, dest, waits, at):
            if fused:
                for copy in waits:
                    copy.wait_recv()
                mine = lt[l, :, core].reshape(H // 2, LANES)
                left = jnp.concatenate([mine, rt[l].reshape(H // 2, LANES)], axis=1)
                for c in range(first, last, 256):
                    g = mm(left, right[l, :, c : c + 256]).astype(LOW)
                    dest[l, :, :, :, :, :, c : c + 256] = g.reshape(2, 2, 2, 2, BLOCK, 256)
            else:
                left = lt[l].reshape(H, LANES)
                for c in range(first, last, 256):
                    r.matrix_sums[l, :, at + c - first : at + c - first + 256] = mm(
                        left, right[l, 0:T, c : c + 256]
                    )

        hh, ll = zz // 2, zz % 2
        place = {"h": hh, "l": ll, "x": xx, "y": yy}

        def z_peer(at):
            return {"seq": at * 2 + xx}

        def peers(axis):
            if axis == "z":
                others = [(zz + o) % nz for o in range(1, nz)]
                return [({"h": to // 2, "l": to % 2}, z_peer(to)) for to in others]
            device = {
                "x": x_peer, "y": y_peer, "l": z_peer(hh * 2 + 1 - ll), "h": z_peer((1 - hh) * 2 + ll),
            }
            return [({axis: 1 - place[axis]}, device[axis])]

        class Part:
            def __init__(self, whole, axes, first, last, order, got, sums):
                self.ref, self.columns = whole, pl.ds(first, last - first)
                self.axes, self.order, self.stage = axes, order, 0
                self.got, self.sums = got, sums

            def index(self, at):
                return tuple(at.get(a, slice(None)) for a in self.axes) + (slice(None), self.columns)

            def begin(self):
                self.copies = [
                    wire.send(self.ref.at[self.index(at)], self.got[self.stage].at[i], device)
                    for i, (at, device) in enumerate(peers(self.order[self.stage]))
                ]

            def total(self):
                for copy in self.copies:
                    copy.wait_recv()
                axis, got = self.order[self.stage], self.got[self.stage]
                gone = "hl" if axis == "z" else axis
                mine = {a: place[a] for a in gone}
                rest = "".join(a for a in self.axes if a not in gone)
                if not rest:
                    value = self.ref[self.index(mine)].astype(F32)
                    for i in range(len(self.copies)):
                        value = value + got[i].astype(F32)
                    return value
                out = self.sums[self.stage]
                for q in range(2):
                    here = self.ref[self.index(mine | {rest[0]: q})]
                    if len(self.copies) == 1:
                        out[q] = here + got[0, q]
                    else:
                        value = here.astype(F32)
                        for i in range(len(self.copies)):
                            value = value + got[i, q].astype(F32)
                        out[q] = value.astype(LOW)
                self.ref, self.columns, self.axes = out, slice(None), rest
                self.stage += 1

            def step(self):
                value = self.total()
                if value is None:
                    self.begin()
                else:
                    self.sink(value)

        along = {}

        def sink_of(l, whole, first, last):
            def early(value):
                for low, high, out in (
                    (0, H, r.glu_weight_grad.at[l]),
                    (H, H + N, r.out_proj_grad.at[l, 0]),
                    (H + N, CE, r.out_proj_grad.at[l, 1]),
                ):
                    a, b = max(low, first), min(high, last)
                    if a < b:
                        out[:, a - low : b - low] = value[:, a - first : b - first]

            def late(value):
                for c in range(2):
                    a, b = max(c * N, first), min((c + 1) * N, last)
                    if a < b:
                        r.in_proj_grad[l, :, c, a - c * N : b - c * N] = value[:, a - first : b - first]
                weights = r.wi[l, own_rows, first:last].astype(F32)
                along.setdefault(l, []).append(jnp.sum(value * weights, axis=1, keepdims=True))

            if whole == "p_o":
                first, last = first + H, last + H
            return late if whole == "p_n" else early

        parts = {}
        for l, whole, label, first, last, order in z.plan:
            got = [getattr(r, f"got_{label}_{stage}") for stage in range(len(order))]
            sums = [getattr(r, f"sum_{label}_{stage}") for stage in range(len(order) - 1)]
            part = Part(getattr(r, whole).at[l], "hlx" if whole == "p_o" else "hlxy", first, last, order, got, sums)
            part.sink = sink_of(l, whole, first, last)
            parts[label] = part

        device = seq * nblk + blk
        own_rows = pl.ds(pl.multiple_of(device * BLOCK, BLOCK), BLOCK)

        def owned(value):
            return pltpu.roll(value, (H - device * BLOCK) % H, 1)[:, 0:BLOCK]

        def out_vectors(l, totals):
            grads = discretize_grad(disc[l], *totals)
            r.decay_log_grad[l : l + 1, :] = grads[0]
            r.frequency_grad[l : l + 1, :] = grads[1]
            r.step_log_grad[l : l + 1, :] = grads[2]

        class Vector:
            def __init__(self, name):
                self.own, self.got = getattr(r, name), getattr(r, name + "_in")
                self.mid, self.mid_got = getattr(r, name + "_mid"), getattr(r, name + "_mid_in")
                self.last, self.full = getattr(r, name + "_z"), getattr(r, name + "_full")
                self.stage = 0

            def begin(self):
                self.copies = [wire.send(self.own, self.got, sibling)]

            def step(self):
                for copy in self.copies:
                    copy.wait_recv()
                stage = self.stage
                self.stage += 1
                if stage == 0:
                    self.mid[0] = self.own[core] + self.got[core]
                    self.copies = [wire.send(self.mid.at[0], self.mid_got.at[0], x_peer)]
                elif stage == 1:
                    self.mid[1] = self.mid[0] + self.mid_got[0]
                    self.copies = [wire.send(self.mid.at[1], self.mid_got.at[1], y_peer)]
                elif stage == 2:
                    self.last[zz] = self.mid[1] + self.mid_got[1]
                    mine = self.last.at[zz]
                    self.copies = [
                        wire.send(mine, mine, z_peer((zz + o) % nz)) for o in range(1, nz)
                    ]
                elif stage == 3:
                    total = self.last[0]
                    for o in range(1, nz):
                        total = total + self.last[o]
                    self.full[core] = total
                    mine = self.full.at[core]
                    self.copies = [wire.send(mine, mine, sibling)]
                else:
                    self.sink(jnp.concatenate([self.full[0], self.full[1]], axis=0))

        if fused:
            first_vector, last_vector = Vector("vec_a"), Vector("vec_b")

            def first_sink(sums):
                mine["sums"] = owned(sums)
                for l, at in ((1, 0), (0, 6)):
                    r.skip_gain_grad[l : l + 1, :] = mine["sums"][at : at + 1]
                    r.glu_bias_grad[l : l + 1, :] = mine["sums"][at + 1 : at + 2]
                out_vectors(1, [sums[2 + i : 3 + i, 0:N] for i in range(4)])

            mine = {}
            first_vector.sink = first_sink
            last_vector.sink = lambda sums: out_vectors(0, [sums[i : i + 1] for i in range(4)])
            parts[VA], parts[VB] = first_vector, last_vector
        waits = {}

        def gain(l):
            return r.norm_gain[l : l + 1, :]

        def skip(l):
            return r.skip_gain[l : l + 1, :]

        def pack_in(l):
            loads[f"wi{l}"].wait()

            def step(i, carry):
                rows = pl.ds(pl.multiple_of(i * BLOCK, BLOCK), BLOCK)
                r.wi[l, rows, :] = r.wi_raw[l, rows].reshape(BLOCK, W)
                return carry

            lax.fori_loop(0, H // BLOCK, step, 0, unroll=4)

        def normalize(l, rows, u):
            inv = lax.rsqrt(jnp.mean(u * u, axis=1, keepdims=True) + EPS)
            unit = u * inv
            r.u[l, rows, :] = u
            r.inv[l, rows, :] = jnp.broadcast_to(inv, (BLOCK, LANES))
            r.unit[l, rows, :] = unit
            r.normed_low[l, rows, :] = (unit * gain(l)).astype(LOW)

        def low_states(l):
            return (r.right_o.at[0], 0) if l == 0 else (r.right_e.at[l], H)

        def states(l, between):
            cre = jnp.broadcast_to(disc[l].coef_re, (SUB, N))
            cim = jnp.broadcast_to(disc[l].coef_im, (SUB, N))

            def source(s, first):
                rows = slice(s * SUB, (s + 1) * SUB)
                if first:
                    dre, dim = cmul(cre, cim, r.proj[l, rows, 0:N], r.proj[l, rows, N:W])
                    r.drive[rows, 0:N] = dre
                    r.drive[rows, N:W] = dim
                    return dre, dim
                return r.drive[rows, 0:N], r.drive[rows, N:W]

            scan(l, l, l, False, source, between, (r.local.at[l], r.factor.at[l], *low_states(l)))

        def sigmoid(value):
            return 0.5 + 0.5 * jnp.tanh(0.5 * value)

        def mix(l):
            waits["x", l] = share(l, r.right_e, H, CE) if l == 1 else share_four(r.right_o)
            if loads[f"wo{l}"] is not None:
                loads[f"wo{l}"].wait()
            x_low, at = low_states(l)
            r.tmp[...] = mm(x_low[0:T, at : at + W], r.wo[l])
            through = skip(l) * gain(l)

            def gelu(rows):
                mixed = r.tmp[rows, :] + through * r.unit[l, rows, :]
                th = jnp.tanh(mixed * (GELU_A + (GELU_A * GELU_B) * (mixed * mixed)))
                half = 0.5 * mixed
                act = half + half * th
                r.mixed[l, rows, :] = mixed
                r.th[l, rows, :] = th
                r.act[l, rows, :] = act
                r.act_low[l, rows, :] = act.astype(LOW)

            each(gelu)
            loads[f"wg{l}"].wait()
            r.tmp[...] = mm(r.act_low[l], r.wg[l])

        def slope(l):
            def gelu_slope(rows):
                mixed, th = r.mixed[l, rows, :], r.th[l, rows, :]
                inner = mixed * (0.5 * GELU_A + (1.5 * GELU_A * GELU_B) * (mixed * mixed))
                r.slope[l, rows, :] = 0.5 + 0.5 * th + (1.0 - th * th) * inner

            each(gelu_slope)

        def adjoint_in(l):
            waits["gate", l] = share(l, r.right_e, 0, H)
            r.tmp[...] = mm_nt(r.right_e[l, 0:T, 0:H], r.wg[l])

            def gelu(rows):
                act_grad = r.og[rows, :] * r.gate[l, rows, :] + r.tmp[rows, :]
                r.mixed_grad[l, rows, :] = (act_grad * r.slope[l, rows, :]).astype(LOW)

            each(gelu)
            r.xg[l] = mm(r.mixed_grad[l], r.wo_t[l])

        def beside_adjoint(l):
            sums = [jnp.zeros((SUB, H), F32), jnp.zeros((SUB, H), F32)]

            def add(rows):
                grad = r.mixed_grad[l, rows, :].astype(F32)
                r.mixed_skip[rows, :] = grad * (gain(l) * skip(l))
                grad = grad * r.unit[l, rows, :]
                gate_grad = r.right_e[l, rows, 0:H].astype(F32)
                sums[0] = sums[0] + grad[0:SUB] + grad[SUB:BLOCK]
                sums[1] = sums[1] + gate_grad[0:SUB] + gate_grad[SUB:BLOCK]

            each(add)
            at = 0 if l == 1 else 6
            r.vec_a[at // 4, at % 4, :] = jnp.sum(sums[0], axis=0) * r.norm_gain[l, :]
            r.vec_a[at // 4, at % 4 + 1, :] = jnp.sum(sums[1], axis=0)

        def adjoints(l, between):
            def source(s, first):
                rows = slice(s * SUB, (s + 1) * SUB)
                return r.xg[l, rows, 0:N], r.xg[l, rows, N:W]

            scan(3 - l, l, 1 - l, True, source, between, (r.proj_local, r.proj_factor, r.right_n.at[l], 0))

        def recurrence_sums(l):
            sums = [jnp.zeros((SUB, N), F32) for _ in range(4)]
            re, im = cmul(
                r.chunk_table[l, :, 0:N], r.chunk_table[l, :, N:W],
                r.entered[l, :, 0:N], r.entered[l, :, N:W],
            )
            xre, xim = r.shifted[l, :, 0:N] + re, r.shifted[l, :, N:W] + im
            for s in range(S) if l == 0 else range(S - 1, -1, -1):
                rows = slice(s * SUB, (s + 1) * SUB)
                are, aim = state_at(3 - l, rows)
                k = wide(r.keep[l, rows, :], N)
                xre, xim = xre * k, xim * k
                pre, pim = r.proj[l, rows, 0:N], r.proj[l, rows, N:W]
                sums[0] = sums[0] + (are * xre + aim * xim)
                sums[1] = sums[1] + (aim * xre - are * xim)
                sums[2] = sums[2] + (are * pre + aim * pim)
                sums[3] = sums[3] + (aim * pre - are * pim)
                xre, xim = state_at(l, rows)
            pad = jnp.zeros((1, H - N), F32)
            for i in range(4):
                value = jnp.sum(sums[i], axis=0, keepdims=True)
                if l == 1:
                    row = (2 + i) % 4
                    r.vec_a[(2 + i) // 4, row : row + 1, :] = jnp.concatenate([value, pad], axis=1)
                else:
                    r.vec_b[i // 2, i % 2 : i % 2 + 1, :] = value

        def input_grad(l, rows):
            v = gain(l) * r.tmp[rows, :] + r.mixed_skip[rows, :]
            unit = r.unit[l, rows, :]
            along = jnp.mean(unit * v, axis=1, keepdims=True)
            out = r.og[rows, :] + wide(r.inv[l, rows, :], H) * (v - unit * along)
            r.og[rows, :] = out
            return out

        def early_products(l):
            dest = r.p_e if fused else None
            outer(l, r.lt_g, r.rt_g, r.right_e, 0, H, dest, (waits["lg", l], waits["gate", l]), 0)
            if l == 1:
                outer(l, r.lt_o, r.rt_o, r.right_e, H, CE, dest, (waits["lo", l], waits["x", l]), H)

        def late_products(l):
            dest = r.p_n if fused else None
            outer(l, r.lt_n, r.rt_n, r.right_n, 0, W, dest, (waits["ln", l], waits["pg", l]), CE)

        loads["tok"].wait()
        at = lax.broadcasted_iota(jnp.int32, (T, T), 0)
        of = lax.broadcasted_iota(jnp.int32, (T, T), 1)
        to_rows = jnp.where(of == (at % SUB) * S + at // SUB, 1.0, 0.0).astype(LOW)
        to_time = jnp.where(at == (of % SUB) * S + of // SUB, 1.0, 0.0).astype(LOW)
        r.tmp[...] = mm(to_rows, r.tok[...])
        each(lambda rows: normalize(0, rows, r.tmp[rows, :]))
        pack_in(0)
        r.proj[0] = mm(r.normed_low[0], r.wi[0])

        def fill0(local):
            local()
            pack_in(1)
            waits["ln", 0] = turn(0, r.normed_low.at[0], r.lt_n, r.rt_n)

        states(0, fill0)
        mix(0)

        def between_layers(rows):
            gate = sigmoid(r.tmp[rows, :] + r.glu_bias[0:1, :])
            r.gate[0, rows, :] = gate
            normalize(1, rows, r.u[0, rows, :] + r.act[0, rows, :] * gate)

        each(between_layers)
        r.proj[1] = mm(r.normed_low[1], r.wi[1])

        def fill1(local):
            local()
            waits["lg", 0] = turn(0, r.act_low.at[0], r.lt_g, r.rt_g)
            waits["ln", 1] = turn(1, r.normed_low.at[1], r.lt_n, r.rt_n)
            loads["cot"].wait()
            r.og[...] = mm(to_rows, r.cot[...])
            for j in range(W // LANES):
                r.wi_t[j * LANES : (j + 1) * LANES, :] = r.wi[1, :, j * LANES : (j + 1) * LANES].T
            slope(0)
            loads["wo1"].wait()
            loads["wo1"] = None
            for l in range(2):
                for j in range(W // LANES):
                    r.wo_t[l, :, j * LANES : (j + 1) * LANES] = r.wo[l, j * LANES : (j + 1) * LANES, :].T

            def gate_slope(rows):
                gate = r.gate[0, rows, :]
                r.gate_slope[rows, :] = r.act[0, rows, :] * (gate * (1.0 - gate))

            each(gate_slope)

        states(1, fill1)
        mix(1)
        slope(1)

        def last_gate(rows):
            gate = sigmoid(r.tmp[rows, :] + r.glu_bias[1:2, :])
            r.gate[1, rows, :] = gate
            grad = r.og[rows, :] * (r.act[1, rows, :] * (gate * (1.0 - gate)))
            r.right_e[1, rows, 0:H] = grad.astype(LOW)

        each(last_gate)
        adjoint_in(1)

        def run(tokens):
            for token in tokens:
                if token in tasks:
                    tasks[token]()
                elif fused and token >= SEND:
                    parts[token - SEND].begin()
                elif fused:
                    parts[token].step()

        def task_vec():
            beside_adjoint(0)
            recurrence_sums(1)
            if fused:
                first_vector.begin()

        def task_m0():
            waits["lo", 0] = turn_four(r.mixed_grad.at[0])

        def task_out():
            r.tmp[...] = mm_nt(r.right_n[0, 0:T, :], r.wi[0])
            each(lambda rows: input_grad(0, rows))
            for s in range(S):
                for j in range(H // LANES):
                    into = pl.ds(s * (H // LANES) + j, SUB, stride=S * (H // LANES))
                    r.tokens_grad[into, :] = r.og[s * SUB : (s + 1) * SUB, j * LANES : (j + 1) * LANES]

        tasks = {
            N1: lambda: late_products(1), VECTORS: task_vec, SIDE0: task_m0, E0: lambda: early_products(0),
            N0: lambda: late_products(0), OUT: task_out, O0: outer_four, E1: lambda: early_products(1),
        }

        def fill2(local):
            waits["lo", 1] = turn(1, r.mixed_grad.at[1], r.lt_o, r.rt_o)
            waits["lg", 1] = turn(1, r.act_low.at[1], r.lt_g, r.rt_g)

            def result(rows):
                out = r.u[1, rows, :] + r.act[1, rows, :] * r.gate[1, rows, :]
                r.act_out[rows, :] = out.astype(LOW)

            each(result)
            beside_adjoint(1)
            run(z.schedule[0])
            local()
            r.activations[...] = mm(to_time, r.act_out[...]).astype(LOW)

        adjoints(1, fill2)
        waits["pg", 1] = share(1, r.right_n, 0, W)
        r.tmp[...] = mm(r.right_n[1, 0:T, :], r.wi_t[...])

        def between_adjoints(rows):
            grad = input_grad(1, rows)
            r.right_e[0, rows, 0:H] = (grad * r.gate_slope[rows, :]).astype(LOW)

        each(between_adjoints)
        adjoint_in(0)

        def fill3(local):
            tasks[LOCAL] = local
            run(z.schedule[1])

        adjoints(0, fill3)
        waits["pg", 0] = share(0, r.right_n, 0, W)
        recurrence_sums(0)
        if fused:
            last_vector.begin()
        run(z.schedule[2])

        if not fused:
            r.vector_sums[...] = r.vec_a[...]
            r.last_vector_sums[...] = r.vec_b[...]
            wire.close()
            return

        gains = owned(jnp.concatenate([r.norm_gain[...], r.skip_gain[...], jnp.zeros((4, H), F32)], axis=0))
        diagonal = lax.broadcasted_iota(jnp.int32, (BLOCK, BLOCK), 0) == lax.broadcasted_iota(
            jnp.int32, (BLOCK, BLOCK), 1
        )
        for l, at in ((1, 0), (0, 6)):
            total = jnp.sum(jnp.where(diagonal, sum(along[l]), 0.0), axis=0, keepdims=True)
            total = total + gains[2 + l : 3 + l] * mine["sums"][at : at + 1]
            r.norm_gain_grad[l : l + 1, :] = total / gains[l : l + 1]
        wire.close()

    return kernel


def solution(mesh):
    nseq, nblk = mesh.shape["seq"], mesh.shape["blk"]

    def on_device(
        tokens, lengths, norm_gain, in_proj, out_proj, skip_gain,
        glu_weight, glu_bias, decay_log, frequency, step_log, cotangent,
    ):
        T, streams, H = tokens.shape
        N = decay_log.shape[1]
        W = 2 * N
        CE = H + W
        assert streams == 1 and T == LANES and H == 512
        fused = nseq == 8 and nblk == 4
        plan = []
        for unit, pieces in enumerate(PLAN if fused else ()):
            first = 0
            for i, (width, order) in enumerate(pieces):
                whole = ("p_e", "p_n", "p_e", "p_n", "p_o")[unit]
                plan.append((int(unit < 2), whole, 10 * (unit + 2) + i, first, first + width, order))
                first += width
            assert first == (CE, W, H, W, W)[unit]
        z = types.SimpleNamespace(
            T=T, H=H, N=N, S=T // SUB, nseq=nseq, nblk=nblk, fused=fused, plan=plan,
            schedule=SCHEDULE,
        )
        any_space = pl.BlockSpec(memory_space=pl.ANY)
        vmem = pl.BlockSpec(memory_space=pltpu.VMEM)
        operands = dict(
            tokens=(tokens.reshape(T, H), any_space),
            lengths=(lengths, any_space),
            norm_gain=(norm_gain, any_space),
            in_proj=(in_proj, any_space),
            out_proj=(out_proj.reshape(2, W, H), any_space),
            skip_gain=(skip_gain, any_space),
            glu_weight=(glu_weight, any_space),
            glu_bias=(glu_bias, any_space),
            decay_log=(decay_log, any_space),
            frequency=(frequency, any_space),
            step_log=(step_log, any_space),
            cotangent=(cotangent.reshape(T, H), any_space),
        )
        results = dict(
            activations=((T, H), LOW),
            tokens_grad=((T * H // LANES, LANES), F32),
        )
        if fused:
            results |= dict(
                norm_gain_grad=((2, BLOCK), F32),
                in_proj_grad=((2, BLOCK, 2, N), F32),
                out_proj_grad=((2, 2, BLOCK, N), F32),
                skip_gain_grad=((2, BLOCK), F32),
                glu_weight_grad=((2, BLOCK, H), F32),
                glu_bias_grad=((2, BLOCK), F32),
                decay_log_grad=((2, N), F32),
                frequency_grad=((2, N), F32),
                step_log_grad=((2, N), F32),
            )
        else:
            results |= dict(
                matrix_sums=((2, H, CE + W), F32),
                vector_sums=((2, 4, H), F32),
                last_vector_sums=((2, 2, N), F32),
            )
        dma = pltpu.SemaphoreType.DMA
        scratch = dict(
            wi_raw=pltpu.VMEM((2, H, 2, N), LOW),
            wi=pltpu.VMEM((2, H, W), LOW),
            wi_t=pltpu.VMEM((W, H), LOW),
            wo_t=pltpu.VMEM((2, H, W), LOW),
            wo=pltpu.VMEM((2, W, H), LOW),
            wg=pltpu.VMEM((2, H, H), LOW),
            tok=pltpu.VMEM((T, H), LOW),
            cot=pltpu.VMEM((T, H), LOW),
            u=pltpu.VMEM((2, T, H), F32),
            inv=pltpu.VMEM((2, T, LANES), F32),
            unit=pltpu.VMEM((2, T, H), F32),
            act=pltpu.VMEM((2, T, H), F32),
            slope=pltpu.VMEM((2, T, H), F32),
            gate_slope=pltpu.VMEM((T, H), F32),
            mixed_skip=pltpu.VMEM((T, H), F32),
            normed_low=pltpu.VMEM((2, T, H), LOW),
            proj=pltpu.VMEM((2, T, W), F32),
            drive=pltpu.VMEM((T, W), F32),
            shifted=pltpu.VMEM((4, SUB, W), F32),
            local=pltpu.VMEM((4, T, W), F32),
            factor=pltpu.VMEM((4, T, W), F32),
            entered=pltpu.VMEM((4, 1, W), F32),
            proj_local=pltpu.VMEM((T, W), F32),
            proj_factor=pltpu.VMEM((T, W), F32),
            mixed=pltpu.VMEM((2, T, H), F32),
            th=pltpu.VMEM((2, T, H), F32),
            gate=pltpu.VMEM((2, T, H), F32),
            act_low=pltpu.VMEM((2, T, H), LOW),
            act_out=pltpu.VMEM((T, H), LOW),
            og=pltpu.VMEM((T, H), F32),
            tmp=pltpu.VMEM((T, H), F32),
            xg=pltpu.VMEM((2, T, W), F32),
            mixed_grad=pltpu.VMEM((2, T, H), LOW),
            right_e=pltpu.VMEM((2, 2 * T, CE), LOW),
            right_n=pltpu.VMEM((2, 2 * T, W), LOW),
            right_o=pltpu.VMEM((4, T, W), LOW),
            lt_y=pltpu.VMEM((H // 64, 2, 2, BLOCK, LANES), LOW),
            rt_y=pltpu.VMEM((3, H // 64, BLOCK, LANES), LOW),
            keep=pltpu.VMEM((2, T, LANES), F32),
            chunk_keep=pltpu.VMEM((2, 3, SUB, LANES), F32),
            chunk_table=pltpu.VMEM((4, SUB, W), F32),
            seq_table=pltpu.VMEM((4, nseq, W), F32),
            carry_out=pltpu.VMEM((4, 1, W), F32),
            carry_in=pltpu.VMEM((4, nseq, 1, W), F32),
            vec_a=pltpu.VMEM((2, 4, H), F32),
            vec_b=pltpu.VMEM((2, 2, N), F32),
        )
        for name in "gon":
            scratch[f"lt_{name}"] = pltpu.VMEM((2, H // 32, 2, BLOCK, LANES), LOW)
            scratch[f"rt_{name}"] = pltpu.VMEM((2, H // 32, BLOCK, LANES), LOW)
        if fused:
            nz = nseq // 2
            scratch["p_o"] = pltpu.VMEM((1, 2, 2, 2, BLOCK, W), LOW)
            for name, width in (("e", CE), ("n", W)):
                scratch[f"p_{name}"] = pltpu.VMEM((2, 2, 2, 2, 2, BLOCK, width), LOW)
            for _, _, label, first, last, order in plan:
                left = len(order) + order.count("z")
                for stage, axis in enumerate(order):
                    others = 3 if axis == "z" else 1
                    left -= 2 if axis == "z" else 1
                    shape = (2,) * left + (BLOCK, last - first)
                    scratch[f"got_{label}_{stage}"] = pltpu.VMEM((others,) + shape, LOW)
                    if left:
                        scratch[f"sum_{label}_{stage}"] = pltpu.VMEM(shape, LOW)
            for name, shape in (("vec_a", (4, H)), ("vec_b", (2, N))):
                scratch[name + "_in"] = pltpu.VMEM((2,) + shape, F32)
                scratch[name + "_mid"] = pltpu.VMEM((2,) + shape, F32)
                scratch[name + "_mid_in"] = pltpu.VMEM((2,) + shape, F32)
                scratch[name + "_z"] = pltpu.VMEM((nz,) + shape, F32)
                scratch[name + "_full"] = pltpu.VMEM((2,) + shape, F32)
        links = LINKS if fused else 4 * (nseq - 1)
        scratch["send_sems"] = dma((links,))
        scratch["recv_sems"] = dma((links,))
        scratch["load_sems"] = dma((8 + len(SMALL),))
        for name in SMALL:
            value = operands[name][0]
            space = pltpu.SMEM if name == "lengths" else pltpu.VMEM
            scratch[name + "_here"] = space(value.shape, value.dtype)
        names = list(operands) + list(results) + list(scratch)
        outs = pl.pallas_call(
            make_kernel(names, z),
            out_shape=[(pltpu.VMEM if fused else jax.ShapeDtypeStruct)(*v) for v in results.values()],
            in_specs=[spec for _, spec in operands.values()],
            out_specs=[vmem] * len(results),
            scratch_shapes=list(scratch.values()),
            compiler_params=pltpu.CompilerParams(
                collective_id=0, has_side_effects=True, vmem_limit_bytes=48 * 2**20
            ),
            name="two_layers",
        )(*(pltpu.with_memory_space_constraint(value, pltpu.HBM) for value, _ in operands.values()))
        if fused:
            outs = pl.pallas_call(
                hand_out,
                out_shape=[jax.ShapeDtypeStruct(*v) for v in results.values()],
                in_specs=[vmem] * len(results),
                out_specs=[any_space] * len(results),
                scratch_shapes=[dma((len(results),))],
                name="hand_out",
            )(*(pltpu.with_memory_space_constraint(out, pltpu.VMEM) for out in outs))
        o = types.SimpleNamespace(**dict(zip(results, outs)))
        activations = o.activations.reshape(T, 1, H)
        tokens_grad = o.tokens_grad.reshape(T, 1, H)
        if fused:
            return (
                activations, tokens_grad, o.norm_gain_grad, o.in_proj_grad,
                jnp.swapaxes(o.out_proj_grad, 2, 3), o.skip_gain_grad, o.glu_weight_grad,
                o.glu_bias_grad, o.decay_log_grad, o.frequency_grad, o.step_log_grad,
            )
        both = ("seq", "blk")
        sums = lax.psum_scatter(o.matrix_sums, both, scatter_dimension=1, tiled=True)
        rows = sums.shape[1]
        vectors, last = lax.psum((o.vector_sums.reshape(8, H), o.last_vector_sums.reshape(4, N)), both)
        start = lax.axis_index(both) * rows

        def owned(value, axis):
            return lax.dynamic_slice_in_dim(value, start, rows, axis)

        mine = owned(vectors, 1)
        skip_grad = jnp.stack([mine[6], mine[0]])
        bias_grad = jnp.stack([mine[7], mine[1]])
        totals = [jnp.stack([last[i], vectors[2 + i, 0:N]]) for i in range(4)]
        grads = discretize_grad(discretize(decay_log, frequency, step_log), *totals)
        in_grad = sums[:, :, CE:].reshape(2, rows, 2, N)
        along = jnp.sum(in_grad * owned(in_proj, 1).astype(F32), axis=(2, 3))
        gain_grad = (along + owned(skip_gain, 1) * skip_grad) / owned(norm_gain, 1)
        return (
            activations, tokens_grad, gain_grad, in_grad,
            jnp.moveaxis(sums[:, :, H:CE].reshape(2, rows, 2, N), 1, 3), skip_grad, sums[:, :, 0:H],
            bias_grad, *grads,
        )

    split = P("seq", "blk", None)
    owned = ("seq", "blk")
    return jax.shard_map(
        on_device,
        mesh=mesh,
        in_specs=(split,) + (P(),) * 10 + (split,),
        out_specs=(
            split, split, P(None, owned), P(None, owned, None, None), P(None, None, None, owned),
            P(None, owned), P(None, owned, None), P(None, owned), P(), P(), P(),
        ),
        check_vma=False,
    )
```

```python
import types

import jax
import jax.numpy as jnp
from jax import lax
from jax.experimental import pallas as pl
from jax.experimental.pallas import tpu as pltpu
from jax.sharding import PartitionSpec as P

EPS = 1e-6
F32 = jnp.float32
LOW = jnp.bfloat16
GELU_A = 0.7978845608028654
GELU_B = 0.044715
LANES = 128
SUB = 8
BLOCK = 16
LINKS = 160
SMALL = ("lengths", "norm_gain", "skip_gain", "glu_bias", "decay_log", "frequency", "step_log")

E1, N1, E0, N0, SIDE0, OUT, VECTORS, VA, VB, LOCAL, O0 = range(11)
SEND = 100
PLAN = (
    ((384, "xlhy"), (256, "zyx"), (256, "lyxh"), (384, "yxlh"),),
    ((384, "zyx"), (384, "yhlx"),),
    ((512, "xlyh"),),
    ((256, "yxz"), (256, "xyz"), (128, "yxz"), (128, "xzy"),),
    ((128, "lxh"), (128, "xlh"), (128, "lxh"), (384, "xz"),),
)
SCHEDULE = (
    (E1, SEND + 20, SEND + 21, SEND + 22, SEND + 23,),
    (N1, VECTORS, SIDE0, SEND + 31, 20, SEND + 30, 23, VA, 21, E0, SEND + 40, LOCAL, 22, 20, 23, O0,),
    (SEND + 61, SEND + 63, VA, SEND + 60, SEND + 62, OUT, N0, VB, SEND + 51, SEND + 53, 31, SEND + 52, SEND + 50, 21,
     40, 22, 30, 61, VA, 23, 20, 63, 60, VB, 62, 52, 51, 53, 50, 31, 21, 30, 40, 22, 60, 20, 62, 61, VB, 52, 51, 23,
     VA, 50, 63, VA, 30, 31, 40, 53, 22, 60, 62, 61, VB, 52, 51, 31, VB, 50, 53, 40,),
)


def cmul(are, aim, bre, bim):
    return are * bre - aim * bim, are * bim + aim * bre


def expm1(value):
    series = jnp.ones_like(value)
    for order in range(9, 1, -1):
        series = 1.0 + value * series * (1.0 / order)
    return jnp.where(value > -0.35, value * series, jnp.exp(value) - 1.0)


def discretize(decay, freq, step_log):
    lam_re = -jnp.exp(decay)
    step = jnp.exp(step_log)
    rotation = freq * step
    shrink = expm1(lam_re * step)
    cosine, sine = jnp.cos(rotation), jnp.sin(rotation)
    half = jnp.sin(0.5 * rotation)
    bar_re = (shrink + 1.0) * cosine
    bar_im = (shrink + 1.0) * sine
    minus_re = shrink * cosine - 2.0 * half * half
    scale = 1.0 / (lam_re * lam_re + freq * freq)
    coef_re = (minus_re * lam_re + bar_im * freq) * scale
    coef_im = (bar_im * lam_re - minus_re * freq) * scale
    return types.SimpleNamespace(
        lam_re=lam_re, freq=freq, step=step, scale=scale,
        bar_re=bar_re, bar_im=bar_im, coef_re=coef_re, coef_im=coef_im,
    )


def discretize_grad(d, bar_gre, bar_gim, coef_gre, coef_gim):
    over_re, over_im = d.lam_re * d.scale, d.freq * d.scale
    part_re, part_im = cmul(coef_gre, coef_gim, over_re, over_im)
    all_re, all_im = bar_gre + part_re, bar_gim + part_im
    one_re, one_im = cmul(all_re, all_im, d.bar_re, -d.bar_im)
    two_re, two_im = cmul(part_re, part_im, d.coef_re, -d.coef_im)
    lam_gre = one_re * d.step - two_re
    lam_gim = one_im * d.step - two_im
    step_g = one_re * d.lam_re + one_im * d.freq
    return lam_gre * d.lam_re, lam_gim, step_g * d.step


def mm(a, b):
    return jnp.dot(a, b, preferred_element_type=F32)


def mm_nt(a, b):
    return lax.dot_general(a, b, (((1,), (1,)), ((), ())), preferred_element_type=F32)


def wide(mask, width):
    return jnp.concatenate([mask] * (width // LANES), axis=1)


class Wire:
    def __init__(self, send_sems, recv_sems):
        self.send_sems, self.recv_sems = send_sems, recv_sems
        self.count = 0
        self.open = []

    def send(self, src, dst, device):
        at = self.count
        self.count += 1
        copy = pltpu.make_async_remote_copy(
            src_ref=src, dst_ref=dst,
            send_sem=self.send_sems.at[at], recv_sem=self.recv_sems.at[at],
            device_id=device, device_id_type=pl.DeviceIdType.MESH,
        )
        copy.start()
        self.open.append(copy)
        return copy

    def close(self):
        for copy in self.open:
            copy.wait_send()


def hand_out(*refs):
    count = len(refs) // 2
    copies = [
        pltpu.make_async_copy(refs[i], refs[count + i], refs[-1].at[i]) for i in range(count)
    ]
    for copy in copies:
        copy.start()
    for copy in copies:
        copy.wait()


def make_kernel(names, z):
    T, H, N, S, nseq, nblk, fused = z.T, z.H, z.N, z.S, z.nseq, z.nblk, z.fused
    W = 2 * N
    CE = H + W

    def kernel(*refs):
        r = types.SimpleNamespace(**dict(zip(names, refs, strict=True)))
        seq = lax.axis_index("seq")
        blk = lax.axis_index("blk")
        wire = Wire(r.send_sems, r.recv_sems)
        core, yy = blk % 2, blk // 2
        xx, zz = seq % 2, seq // 2
        nz = nseq // 2
        sibling = {"blk": yy * 2 + (1 - core)}
        y_peer = {"blk": (1 - yy) * 2 + core}
        across = {"blk": (1 - yy) * 2 + (1 - core)}
        x_peer = {"seq": zz * 2 + (1 - xx)}

        loads = {}

        def load(name, src, dst):
            copy = pltpu.make_async_copy(src, dst, r.load_sems.at[len(loads)])
            copy.start()
            loads[name] = copy

        load("tok", r.tokens, r.tok)
        for name in SMALL:
            load(name, getattr(r, name), getattr(r, name + "_here"))
            setattr(r, name, getattr(r, name + "_here"))
        load("wi0", r.in_proj.at[0], r.wi_raw.at[0])
        load("wo0", r.out_proj.at[0], r.wo.at[0])
        load("wg0", r.glu_weight.at[0], r.wg.at[0])
        load("wi1", r.in_proj.at[1], r.wi_raw.at[1])
        load("wo1", r.out_proj.at[1], r.wo.at[1])
        load("wg1", r.glu_weight.at[1], r.wg.at[1])
        load("cot", r.cotangent, r.cot)

        barrier = pltpu.get_barrier_semaphore()
        greeted = [{"seq": (seq + o) % nseq} for o in range(1, nseq)]
        if fused:
            greeted += [sibling, y_peer, across]
        for device in greeted:
            pl.semaphore_signal(barrier, inc=1, device_id=device, device_id_type=pl.DeviceIdType.MESH)

        for name in SMALL:
            loads[name].wait()
        disc, powers = [], []
        for l in range(2):
            d = discretize(
                r.decay_log[l : l + 1, :], r.frequency[l : l + 1, :], r.step_log[l : l + 1, :]
            )
            disc.append(d)
            chain = [(d.bar_re, d.bar_im)]
            while len(chain) < 12:
                chain.append(cmul(*chain[-1], *chain[-1]))
            powers.append(chain)
        step_bits = S.bit_length() - 1
        seg_bits = T.bit_length() - 1

        def power_rows(l, first, exponent, bits):
            rows = exponent.shape[0]
            out_re = jnp.ones((rows, N), F32)
            out_im = jnp.zeros((rows, N), F32)
            for bit in range(bits):
                use = wide(((exponent >> bit) & 1) == 1, N)
                pre, pim = powers[l][first + bit]
                new_re, new_im = cmul(out_re, out_im, pre, pim)
                out_re = jnp.where(use, new_re, out_re)
                out_im = jnp.where(use, new_im, out_im)
            return out_re, out_im

        ends, starts = [], []
        total = jnp.int32(0)
        for i in range(r.lengths.shape[1]):
            starts.append(total)
            total = total + r.lengths[blk, i]
            ends.append(total - 1)

        def keep(position, marks):
            hit = position == marks[0]
            for mark in marks[1:]:
                hit = hit | (position == mark)
            return jnp.where(hit, 0.0, 1.0).astype(F32)

        row = lax.broadcasted_iota(jnp.int32, (T, LANES), 0)
        here = seq * T + (row % SUB) * S + row // SUB
        r.keep[0] = keep(here, starts)
        r.keep[1] = keep(here, ends)
        offset = lax.broadcasted_iota(jnp.int32, (nseq, T), 0)
        lane = lax.broadcasted_iota(jnp.int32, (nseq, T), 1)
        there = ((seq - offset + nseq) % nseq) * T + lane
        k8 = lax.broadcasted_iota(jnp.int32, (SUB, LANES), 0)
        n_row = lax.broadcasted_iota(jnp.int32, (nseq, LANES), 0)
        for way in range(2):
            chunk = jnp.ones((SUB, LANES), F32)
            for s in range(S):
                chunk = chunk * r.keep[way, s * SUB : (s + 1) * SUB, :]
            for level in range(3):
                delta = 1 << level
                if way == 0:
                    inside, rolled = k8 >= delta, pltpu.roll(chunk, delta, 0)
                else:
                    inside, rolled = k8 < SUB - delta, pltpu.roll(chunk, SUB - delta, 0)
                r.chunk_keep[way, level] = jnp.where(inside, chunk, 0.0)
                chunk = jnp.where(inside, chunk * rolled, chunk)
            if way == 0:
                before = jnp.where(k8 >= 1, pltpu.roll(chunk, 1, 0), 1.0)
                chunks_before = k8
            else:
                before = jnp.where(k8 < SUB - 1, pltpu.roll(chunk, SUB - 1, 0), 1.0)
                chunks_before = SUB - 1 - k8
            whole = jnp.min(keep(there, starts if way == 0 else ends), axis=1, keepdims=True)
            whole = jnp.broadcast_to(whole, (nseq, LANES))
            gates = [None] * nseq
            running = jnp.ones((1, LANES), F32)
            for o in range(1, nseq) if way == 0 else range(nseq - 1, 0, -1):
                gates[o] = running
                running = running * whole[o : o + 1, :]
            gates[0] = jnp.zeros((1, LANES), F32)
            gate = jnp.concatenate(gates, axis=0)
            if way == 0:
                valid = (n_row >= 1) & (n_row <= seq)
                hops = n_row - 1
            else:
                valid = n_row > seq
                hops = nseq - 1 - n_row
            gate = jnp.where(valid, gate, 0.0)
            hops = jnp.where(valid, hops, 0)
            for l in range(2):
                index = (0, 2)[l] if way == 0 else (3, 1)[l]
                sign = 1.0 if index < 2 else -1.0
                pre, pim = power_rows(l, step_bits, chunks_before, 3)
                r.chunk_table[index, :, 0:N] = pre * wide(before, N)
                r.chunk_table[index, :, N:W] = pim * wide(before, N) * sign
                pre, pim = power_rows(l, seg_bits, hops, (nseq - 1).bit_length())
                r.seq_table[index, :, 0:N] = pre * wide(gate, N)
                r.seq_table[index, :, N:W] = pim * wide(gate, N) * sign
        for index in range(4):
            r.carry_in[index, 0] = jnp.zeros((1, W), F32)

        def scan(index, l, way, conj, source, between, finish):
            bre, bim = disc[l].bar_re, disc[l].bar_im
            sign = -1.0 if conj else 1.0
            bre = jnp.broadcast_to(bre, (SUB, N))
            bim = jnp.broadcast_to(bim * sign, (SUB, N))
            order = list(range(S)) if way == 0 else list(range(S - 1, -1, -1))

            def advance(s, yre, yim, dre, dim):
                k = wide(r.keep[way, s * SUB : (s + 1) * SUB, :], N)
                pre, pim = cmul(bre, bim, yre * k, yim * k)
                return pre + dre, pim + dim

            yre = jnp.zeros((SUB, N), F32)
            yim = jnp.zeros((SUB, N), F32)
            for s in order:
                dre, dim = source(s, True)
                yre, yim = advance(s, yre, yim, dre, dim)
            for level in range(3):
                delta = 1 << level
                shift = delta if way == 0 else SUB - delta
                m = wide(r.chunk_keep[way, level], N)
                pre, pim = powers[l][step_bits + level]
                gre, gim = cmul(pre, pim * sign, pltpu.roll(yre, shift, 0) * m, pltpu.roll(yim, shift, 0) * m)
                yre, yim = yre + gre, yim + gim
            last = SUB - 1 if way == 0 else 0
            r.carry_out[index, 0:1, 0:N] = yre[last : last + 1, :]
            r.carry_out[index, 0:1, N:W] = yim[last : last + 1, :]
            if index == 0:
                pl.semaphore_wait(barrier, len(greeted))
            copies = [
                wire.send(r.carry_out.at[index], r.carry_in.at[index, o], {"seq": (seq + o) % nseq})
                for o in range(1, nseq)
            ]
            edge = wide(k8 >= 1 if way == 0 else k8 < SUB - 1, N)
            shift = 1 if way == 0 else SUB - 1
            r.shifted[index, :, 0:N] = jnp.where(edge, pltpu.roll(yre, shift, 0), 0.0)
            r.shifted[index, :, N:W] = jnp.where(edge, pltpu.roll(yim, shift, 0), 0.0)

            def local():
                yre, yim = r.shifted[index, :, 0:N], r.shifted[index, :, N:W]
                qre, qim = r.chunk_table[index, :, 0:N], r.chunk_table[index, :, N:W]
                for s in order:
                    rows = slice(s * SUB, (s + 1) * SUB)
                    dre, dim = source(s, False)
                    yre, yim = advance(s, yre, yim, dre, dim)
                    qre, qim = advance(s, qre, qim, 0.0, 0.0)
                    for ref, re, im in ((r.local, yre, yim), (r.factor, qre, qim)):
                        ref[index, rows, 0:N] = re
                        ref[index, rows, N:W] = im
                    if conj:
                        cre, cim = disc[l].coef_re, -disc[l].coef_im
                        for ref, pair in ((r.proj_local, (yre, yim)), (r.proj_factor, (qre, qim))):
                            re, im = cmul(*pair, cre, cim)
                            ref[rows, 0:N] = re
                            ref[rows, N:W] = im

            between(local)
            for copy in copies:
                copy.wait_recv()
            got = r.carry_in[index, :, 0, :]
            gre, gim = cmul(got[:, 0:N], got[:, N:W], r.seq_table[index, :, 0:N], r.seq_table[index, :, N:W])
            gre = jnp.sum(gre, axis=0, keepdims=True)
            gim = jnp.sum(gim, axis=0, keepdims=True)
            r.entered[index, :, 0:N] = gre
            r.entered[index, :, N:W] = gim
            base, factor, out, at = finish

            def add(rows):
                re, im = cmul(factor[rows, 0:N], factor[rows, N:W], gre, gim)
                out[rows, at : at + N] = (base[rows, 0:N] + re).astype(LOW)
                out[rows, at + N : at + W] = (base[rows, N:W] + im).astype(LOW)

            each(add)

        def state_at(index, rows):
            re, im = cmul(
                r.factor[index, rows, 0:N], r.factor[index, rows, N:W],
                r.entered[index, :, 0:N], r.entered[index, :, N:W],
            )
            return r.local[index, rows, 0:N] + re, r.local[index, rows, N:W] + im

        def each(body):
            for first in range(0, T, BLOCK):
                body(slice(first, first + BLOCK))

        def turn(l, value_ref, lt, rt):
            for j in range(H // LANES):
                block = value_ref[:, j * LANES : (j + 1) * LANES].T
                lt[l, 4 * j : 4 * j + 4] = block.reshape(4, 2, BLOCK, LANES)
            if fused:
                return wire.send(lt.at[l, :, 1 - core], rt.at[l], sibling)

        def share(l, ref, first, last):
            if fused:
                return wire.send(
                    ref.at[l, 0:T, first:last], ref.at[l, T : 2 * T, first:last], sibling
                )

        four = (sibling, y_peer, across)
        block_of = ((yy, 1 - core), (1 - yy, core), (1 - yy, 1 - core))

        def share_four(ref):
            if fused:
                return [wire.send(ref.at[0], ref.at[m + 1], device) for m, device in enumerate(four)]

        def turn_four(value_ref):
            for j in range(H // LANES):
                block = value_ref[:, j * LANES : (j + 1) * LANES].T
                r.lt_y[2 * j : 2 * j + 2] = block.reshape(2, 2, 2, BLOCK, LANES)
            if fused:
                return [
                    wire.send(r.lt_y.at[:, block_of[m][0], block_of[m][1]], r.rt_y.at[m], device)
                    for m, device in enumerate(four)
                ]

        def outer_four():
            if fused:
                for copy in waits["lo", 0] + waits["x", 0]:
                    copy.wait_recv()
                rows = H // 4
                left = [r.lt_y[:, yy, core].reshape(rows, LANES)]
                left += [r.rt_y[m].reshape(rows, LANES) for m in range(3)]
                left = jnp.concatenate(left, axis=1)
                for c in range(0, W, 256):
                    g = mm(left, r.right_o[:, :, c : c + 256].reshape(4 * T, 256)).astype(LOW)
                    r.p_o[0, :, :, :, :, c : c + 256] = g.reshape(2, 2, 2, BLOCK, 256)
            else:
                left = r.lt_y[...].reshape(H, LANES)
                for c in range(0, W, 256):
                    r.matrix_sums[0, :, H + c : H + c + 256] = mm(left, r.right_o[0, :, c : c + 256])

        def outer(l, lt, rt, right, first, last, dest, waits, at):
            if fused:
                for copy in waits:
                    copy.wait_recv()
                mine = lt[l, :, core].reshape(H // 2, LANES)
                left = jnp.concatenate([mine, rt[l].reshape(H // 2, LANES)], axis=1)
                for c in range(first, last, 256):
                    g = mm(left, right[l, :, c : c + 256]).astype(LOW)
                    dest[l, :, :, :, :, :, c : c + 256] = g.reshape(2, 2, 2, 2, BLOCK, 256)
            else:
                left = lt[l].reshape(H, LANES)
                for c in range(first, last, 256):
                    r.matrix_sums[l, :, at + c - first : at + c - first + 256] = mm(
                        left, right[l, 0:T, c : c + 256]
                    )

        hh, ll = zz // 2, zz % 2
        place = {"h": hh, "l": ll, "x": xx, "y": yy}

        def z_peer(at):
            return {"seq": at * 2 + xx}

        def peers(axis):
            if axis == "z":
                others = [(zz + o) % nz for o in range(1, nz)]
                return [({"h": to // 2, "l": to % 2}, z_peer(to)) for to in others]
            device = {
                "x": x_peer, "y": y_peer, "l": z_peer(hh * 2 + 1 - ll), "h": z_peer((1 - hh) * 2 + ll),
            }
            return [({axis: 1 - place[axis]}, device[axis])]

        class Part:
            def __init__(self, whole, axes, first, last, order, got, sums):
                self.ref, self.columns = whole, pl.ds(first, last - first)
                self.axes, self.order, self.stage = axes, order, 0
                self.got, self.sums = got, sums

            def index(self, at):
                return tuple(at.get(a, slice(None)) for a in self.axes) + (slice(None), self.columns)

            def begin(self):
                self.copies = [
                    wire.send(self.ref.at[self.index(at)], self.got[self.stage].at[i], device)
                    for i, (at, device) in enumerate(peers(self.order[self.stage]))
                ]

            def total(self):
                for copy in self.copies:
                    copy.wait_recv()
                axis, got = self.order[self.stage], self.got[self.stage]
                gone = "hl" if axis == "z" else axis
                mine = {a: place[a] for a in gone}
                rest = "".join(a for a in self.axes if a not in gone)
                if not rest:
                    value = self.ref[self.index(mine)].astype(F32)
                    for i in range(len(self.copies)):
                        value = value + got[i].astype(F32)
                    return value
                out = self.sums[self.stage]
                for q in range(2):
                    here = self.ref[self.index(mine | {rest[0]: q})]
                    if len(self.copies) == 1:
                        out[q] = here + got[0, q]
                    else:
                        value = here.astype(F32)
                        for i in range(len(self.copies)):
                            value = value + got[i, q].astype(F32)
                        out[q] = value.astype(LOW)
                self.ref, self.columns, self.axes = out, slice(None), rest
                self.stage += 1

            def step(self):
                value = self.total()
                if value is None:
                    self.begin()
                else:
                    self.sink(value)

        along = {}

        def sink_of(l, whole, first, last):
            def early(value):
                for low, high, out in (
                    (0, H, r.glu_weight_grad.at[l]),
                    (H, H + N, r.out_proj_grad.at[l, 0]),
                    (H + N, CE, r.out_proj_grad.at[l, 1]),
                ):
                    a, b = max(low, first), min(high, last)
                    if a < b:
                        out[:, a - low : b - low] = value[:, a - first : b - first]

            def late(value):
                for c in range(2):
                    a, b = max(c * N, first), min((c + 1) * N, last)
                    if a < b:
                        r.in_proj_grad[l, :, c, a - c * N : b - c * N] = value[:, a - first : b - first]
                weights = r.wi[l, own_rows, first:last].astype(F32)
                along.setdefault(l, []).append(jnp.sum(value * weights, axis=1, keepdims=True))

            if whole == "p_o":
                first, last = first + H, last + H
            return late if whole == "p_n" else early

        parts = {}
        for l, whole, label, first, last, order in z.plan:
            got = [getattr(r, f"got_{label}_{stage}") for stage in range(len(order))]
            sums = [getattr(r, f"sum_{label}_{stage}") for stage in range(len(order) - 1)]
            part = Part(getattr(r, whole).at[l], "hlx" if whole == "p_o" else "hlxy", first, last, order, got, sums)
            part.sink = sink_of(l, whole, first, last)
            parts[label] = part

        device = seq * nblk + blk
        own_rows = pl.ds(pl.multiple_of(device * BLOCK, BLOCK), BLOCK)

        def owned(value):
            return pltpu.roll(value, (H - device * BLOCK) % H, 1)[:, 0:BLOCK]

        def out_vectors(l, totals):
            grads = discretize_grad(disc[l], *totals)
            r.decay_log_grad[l : l + 1, :] = grads[0]
            r.frequency_grad[l : l + 1, :] = grads[1]
            r.step_log_grad[l : l + 1, :] = grads[2]

        class Vector:
            def __init__(self, name):
                self.own, self.got = getattr(r, name), getattr(r, name + "_in")
                self.mid, self.mid_got = getattr(r, name + "_mid"), getattr(r, name + "_mid_in")
                self.last, self.full = getattr(r, name + "_z"), getattr(r, name + "_full")
                self.stage = 0

            def begin(self):
                self.copies = [wire.send(self.own, self.got, sibling)]

            def step(self):
                for copy in self.copies:
                    copy.wait_recv()
                stage = self.stage
                self.stage += 1
                if stage == 0:
                    self.mid[0] = self.own[core] + self.got[core]
                    self.copies = [wire.send(self.mid.at[0], self.mid_got.at[0], x_peer)]
                elif stage == 1:
                    self.mid[1] = self.mid[0] + self.mid_got[0]
                    self.copies = [wire.send(self.mid.at[1], self.mid_got.at[1], y_peer)]
                elif stage == 2:
                    self.last[zz] = self.mid[1] + self.mid_got[1]
                    mine = self.last.at[zz]
                    self.copies = [
                        wire.send(mine, mine, z_peer((zz + o) % nz)) for o in range(1, nz)
                    ]
                elif stage == 3:
                    total = self.last[0]
                    for o in range(1, nz):
                        total = total + self.last[o]
                    self.full[core] = total
                    mine = self.full.at[core]
                    self.copies = [wire.send(mine, mine, sibling)]
                else:
                    self.sink(jnp.concatenate([self.full[0], self.full[1]], axis=0))

        if fused:
            first_vector, last_vector = Vector("vec_a"), Vector("vec_b")

            def first_sink(sums):
                mine["sums"] = owned(sums)
                for l, at in ((1, 0), (0, 6)):
                    r.skip_gain_grad[l : l + 1, :] = mine["sums"][at : at + 1]
                    r.glu_bias_grad[l : l + 1, :] = mine["sums"][at + 1 : at + 2]
                out_vectors(1, [sums[2 + i : 3 + i, 0:N] for i in range(4)])

            mine = {}
            first_vector.sink = first_sink
            last_vector.sink = lambda sums: out_vectors(0, [sums[i : i + 1] for i in range(4)])
            parts[VA], parts[VB] = first_vector, last_vector
        waits = {}

        def gain(l):
            return r.norm_gain[l : l + 1, :]

        def skip(l):
            return r.skip_gain[l : l + 1, :]

        def pack_in(l):
            loads[f"wi{l}"].wait()

            def step(i, carry):
                rows = pl.ds(pl.multiple_of(i * BLOCK, BLOCK), BLOCK)
                r.wi[l, rows, :] = r.wi_raw[l, rows].reshape(BLOCK, W)
                return carry

            lax.fori_loop(0, H // BLOCK, step, 0, unroll=4)

        def normalize(l, rows, u):
            inv = lax.rsqrt(jnp.mean(u * u, axis=1, keepdims=True) + EPS)
            unit = u * inv
            r.u[l, rows, :] = u
            r.inv[l, rows, :] = jnp.broadcast_to(inv, (BLOCK, LANES))
            r.unit[l, rows, :] = unit
            r.normed_low[l, rows, :] = (unit * gain(l)).astype(LOW)

        def low_states(l):
            return (r.right_o.at[0], 0) if l == 0 else (r.right_e.at[l], H)

        def states(l, between):
            cre = jnp.broadcast_to(disc[l].coef_re, (SUB, N))
            cim = jnp.broadcast_to(disc[l].coef_im, (SUB, N))

            def source(s, first):
                rows = slice(s * SUB, (s + 1) * SUB)
                if first:
                    dre, dim = cmul(cre, cim, r.proj[l, rows, 0:N], r.proj[l, rows, N:W])
                    r.drive[rows, 0:N] = dre
                    r.drive[rows, N:W] = dim
                    return dre, dim
                return r.drive[rows, 0:N], r.drive[rows, N:W]

            scan(l, l, l, False, source, between, (r.local.at[l], r.factor.at[l], *low_states(l)))

        def sigmoid(value):
            return 0.5 + 0.5 * jnp.tanh(0.5 * value)

        def mix(l):
            waits["x", l] = share(l, r.right_e, H, CE) if l == 1 else share_four(r.right_o)
            if loads[f"wo{l}"] is not None:
                loads[f"wo{l}"].wait()
            x_low, at = low_states(l)
            r.tmp[...] = mm(x_low[0:T, at : at + W], r.wo[l])
            through = skip(l) * gain(l)

            def gelu(rows):
                mixed = r.tmp[rows, :] + through * r.unit[l, rows, :]
                th = jnp.tanh(mixed * (GELU_A + (GELU_A * GELU_B) * (mixed * mixed)))
                half = 0.5 * mixed
                act = half + half * th
                r.mixed[l, rows, :] = mixed
                r.th[l, rows, :] = th
                r.act[l, rows, :] = act
                r.act_low[l, rows, :] = act.astype(LOW)

            each(gelu)
            loads[f"wg{l}"].wait()
            r.tmp[...] = mm(r.act_low[l], r.wg[l])

        def slope(l):
            def gelu_slope(rows):
                mixed, th = r.mixed[l, rows, :], r.th[l, rows, :]
                inner = mixed * (0.5 * GELU_A + (1.5 * GELU_A * GELU_B) * (mixed * mixed))
                r.slope[l, rows, :] = 0.5 + 0.5 * th + (1.0 - th * th) * inner

            each(gelu_slope)

        def adjoint_in(l):
            waits["gate", l] = share(l, r.right_e, 0, H)
            r.tmp[...] = mm_nt(r.right_e[l, 0:T, 0:H], r.wg[l])

            def gelu(rows):
                act_grad = r.og[rows, :] * r.gate[l, rows, :] + r.tmp[rows, :]
                r.mixed_grad[l, rows, :] = (act_grad * r.slope[l, rows, :]).astype(LOW)

            each(gelu)
            r.xg[l] = mm(r.mixed_grad[l], r.wo_t[l])

        def beside_adjoint(l):
            sums = [jnp.zeros((SUB, H), F32), jnp.zeros((SUB, H), F32)]

            def add(rows):
                grad = r.mixed_grad[l, rows, :].astype(F32)
                r.mixed_skip[rows, :] = grad * (gain(l) * skip(l))
                grad = grad * r.unit[l, rows, :]
                gate_grad = r.right_e[l, rows, 0:H].astype(F32)
                sums[0] = sums[0] + grad[0:SUB] + grad[SUB:BLOCK]
                sums[1] = sums[1] + gate_grad[0:SUB] + gate_grad[SUB:BLOCK]

            each(add)
            at = 0 if l == 1 else 6
            r.vec_a[at // 4, at % 4, :] = jnp.sum(sums[0], axis=0) * r.norm_gain[l, :]
            r.vec_a[at // 4, at % 4 + 1, :] = jnp.sum(sums[1], axis=0)

        def adjoints(l, between):
            def source(s, first):
                rows = slice(s * SUB, (s + 1) * SUB)
                return r.xg[l, rows, 0:N], r.xg[l, rows, N:W]

            scan(3 - l, l, 1 - l, True, source, between, (r.proj_local, r.proj_factor, r.right_n.at[l], 0))

        def recurrence_sums(l):
            sums = [jnp.zeros((SUB, N), F32) for _ in range(4)]
            re, im = cmul(
                r.chunk_table[l, :, 0:N], r.chunk_table[l, :, N:W],
                r.entered[l, :, 0:N], r.entered[l, :, N:W],
            )
            xre, xim = r.shifted[l, :, 0:N] + re, r.shifted[l, :, N:W] + im
            for s in range(S) if l == 0 else range(S - 1, -1, -1):
                rows = slice(s * SUB, (s + 1) * SUB)
                are, aim = state_at(3 - l, rows)
                k = wide(r.keep[l, rows, :], N)
                xre, xim = xre * k, xim * k
                pre, pim = r.proj[l, rows, 0:N], r.proj[l, rows, N:W]
                sums[0] = sums[0] + (are * xre + aim * xim)
                sums[1] = sums[1] + (aim * xre - are * xim)
                sums[2] = sums[2] + (are * pre + aim * pim)
                sums[3] = sums[3] + (aim * pre - are * pim)
                xre, xim = state_at(l, rows)
            pad = jnp.zeros((1, H - N), F32)
            for i in range(4):
                value = jnp.sum(sums[i], axis=0, keepdims=True)
                if l == 1:
                    row = (2 + i) % 4
                    r.vec_a[(2 + i) // 4, row : row + 1, :] = jnp.concatenate([value, pad], axis=1)
                else:
                    r.vec_b[i // 2, i % 2 : i % 2 + 1, :] = value

        def input_grad(l, rows):
            v = gain(l) * r.tmp[rows, :] + r.mixed_skip[rows, :]
            unit = r.unit[l, rows, :]
            along = jnp.mean(unit * v, axis=1, keepdims=True)
            out = r.og[rows, :] + wide(r.inv[l, rows, :], H) * (v - unit * along)
            r.og[rows, :] = out
            return out

        def early_products(l):
            dest = r.p_e if fused else None
            outer(l, r.lt_g, r.rt_g, r.right_e, 0, H, dest, (waits["lg", l], waits["gate", l]), 0)
            if l == 1:
                outer(l, r.lt_o, r.rt_o, r.right_e, H, CE, dest, (waits["lo", l], waits["x", l]), H)

        def late_products(l):
            dest = r.p_n if fused else None
            outer(l, r.lt_n, r.rt_n, r.right_n, 0, W, dest, (waits["ln", l], waits["pg", l]), CE)

        loads["tok"].wait()
        at = lax.broadcasted_iota(jnp.int32, (T, T), 0)
        of = lax.broadcasted_iota(jnp.int32, (T, T), 1)
        to_rows = jnp.where(of == (at % SUB) * S + at // SUB, 1.0, 0.0).astype(LOW)
        to_time = jnp.where(at == (of % SUB) * S + of // SUB, 1.0, 0.0).astype(LOW)
        r.tmp[...] = mm(to_rows, r.tok[...])
        each(lambda rows: normalize(0, rows, r.tmp[rows, :]))
        pack_in(0)
        r.proj[0] = mm(r.normed_low[0], r.wi[0])

        def fill0(local):
            local()
            pack_in(1)
            waits["ln", 0] = turn(0, r.normed_low.at[0], r.lt_n, r.rt_n)

        states(0, fill0)
        mix(0)

        def between_layers(rows):
            gate = sigmoid(r.tmp[rows, :] + r.glu_bias[0:1, :])
            r.gate[0, rows, :] = gate
            normalize(1, rows, r.u[0, rows, :] + r.act[0, rows, :] * gate)

        each(between_layers)
        r.proj[1] = mm(r.normed_low[1], r.wi[1])

        def fill1(local):
            local()
            waits["lg", 0] = turn(0, r.act_low.at[0], r.lt_g, r.rt_g)
            waits["ln", 1] = turn(1, r.normed_low.at[1], r.lt_n, r.rt_n)
            loads["cot"].wait()
            r.og[...] = mm(to_rows, r.cot[...])
            for j in range(W // LANES):
                r.wi_t[j * LANES : (j + 1) * LANES, :] = r.wi[1, :, j * LANES : (j + 1) * LANES].T
            slope(0)
            loads["wo1"].wait()
            loads["wo1"] = None
            for l in range(2):
                for j in range(W // LANES):
                    r.wo_t[l, :, j * LANES : (j + 1) * LANES] = r.wo[l, j * LANES : (j + 1) * LANES, :].T

            def gate_slope(rows):
                gate = r.gate[0, rows, :]
                r.gate_slope[rows, :] = r.act[0, rows, :] * (gate * (1.0 - gate))

            each(gate_slope)

        states(1, fill1)
        mix(1)
        slope(1)

        def last_gate(rows):
            gate = sigmoid(r.tmp[rows, :] + r.glu_bias[1:2, :])
            r.gate[1, rows, :] = gate
            grad = r.og[rows, :] * (r.act[1, rows, :] * (gate * (1.0 - gate)))
            r.right_e[1, rows, 0:H] = grad.astype(LOW)

        each(last_gate)
        adjoint_in(1)

        def out_gain(l, at):
            gains = owned(jnp.concatenate([r.norm_gain[...], r.skip_gain[...], jnp.zeros((4, H), F32)], axis=0))
            diagonal = lax.broadcasted_iota(jnp.int32, (BLOCK, BLOCK), 0) == lax.broadcasted_iota(
                jnp.int32, (BLOCK, BLOCK), 1
            )
            total = jnp.sum(jnp.where(diagonal, sum(along[l]), 0.0), axis=0, keepdims=True)
            total = total + gains[2 + l : 3 + l] * mine["sums"][at : at + 1]
            r.norm_gain_grad[l : l + 1, :] = total / gains[l : l + 1]

        def run(tokens):
            for token in tokens:
                if token in tasks:
                    tasks[token]()
                elif fused and token >= SEND:
                    parts[token - SEND].begin()
                elif fused:
                    parts[token].step()

        def task_vec():
            beside_adjoint(0)
            recurrence_sums(1)
            if fused:
                first_vector.begin()

        def task_m0():
            waits["lo", 0] = turn_four(r.mixed_grad.at[0])

        def task_out():
            r.tmp[...] = mm_nt(r.right_n[0, 0:T, :], r.wi[0])
            each(lambda rows: input_grad(0, rows))
            for s in range(S):
                for j in range(H // LANES):
                    into = pl.ds(s * (H // LANES) + j, SUB, stride=S * (H // LANES))
                    r.tokens_grad[into, :] = r.og[s * SUB : (s + 1) * SUB, j * LANES : (j + 1) * LANES]

        tasks = {
            N1: lambda: late_products(1), VECTORS: task_vec, SIDE0: task_m0, E0: lambda: early_products(0),
            N0: lambda: late_products(0), OUT: task_out, O0: outer_four, E1: lambda: early_products(1),
        }

        def fill2(local):
            waits["lo", 1] = turn(1, r.mixed_grad.at[1], r.lt_o, r.rt_o)
            waits["lg", 1] = turn(1, r.act_low.at[1], r.lt_g, r.rt_g)

            def result(rows):
                out = r.u[1, rows, :] + r.act[1, rows, :] * r.gate[1, rows, :]
                r.act_out[rows, :] = out.astype(LOW)

            each(result)
            beside_adjoint(1)
            run(z.schedule[0])
            local()
            r.activations[...] = mm(to_time, r.act_out[...]).astype(LOW)

        adjoints(1, fill2)
        waits["pg", 1] = share(1, r.right_n, 0, W)
        r.tmp[...] = mm(r.right_n[1, 0:T, :], r.wi_t[...])

        def between_adjoints(rows):
            grad = input_grad(1, rows)
            r.right_e[0, rows, 0:H] = (grad * r.gate_slope[rows, :]).astype(LOW)

        each(between_adjoints)
        adjoint_in(0)

        def fill3(local):
            tasks[LOCAL] = local
            run(z.schedule[1])

        adjoints(0, fill3)
        waits["pg", 0] = share(0, r.right_n, 0, W)
        recurrence_sums(0)
        if fused:
            last_vector.begin()
        run(z.schedule[2][:-1])
        if fused:
            out_gain(1, 0)
        run(z.schedule[2][-1:])

        if not fused:
            r.vector_sums[...] = r.vec_a[...]
            r.last_vector_sums[...] = r.vec_b[...]
            wire.close()
            return

        out_gain(0, 6)
        wire.close()

    return kernel


def solution(mesh):
    nseq, nblk = mesh.shape["seq"], mesh.shape["blk"]

    def on_device(
        tokens, lengths, norm_gain, in_proj, out_proj, skip_gain,
        glu_weight, glu_bias, decay_log, frequency, step_log, cotangent,
    ):
        T, streams, H = tokens.shape
        N = decay_log.shape[1]
        W = 2 * N
        CE = H + W
        assert streams == 1 and T == LANES and H == 512
        fused = nseq == 8 and nblk == 4
        plan = []
        for unit, pieces in enumerate(PLAN if fused else ()):
            first = 0
            for i, (width, order) in enumerate(pieces):
                whole = ("p_e", "p_n", "p_e", "p_n", "p_o")[unit]
                plan.append((int(unit < 2), whole, 10 * (unit + 2) + i, first, first + width, order))
                first += width
            assert first == (CE, W, H, W, W)[unit]
        z = types.SimpleNamespace(
            T=T, H=H, N=N, S=T // SUB, nseq=nseq, nblk=nblk, fused=fused, plan=plan,
            schedule=SCHEDULE,
        )
        any_space = pl.BlockSpec(memory_space=pl.ANY)
        vmem = pl.BlockSpec(memory_space=pltpu.VMEM)
        operands = dict(
            tokens=(tokens.reshape(T, H), any_space),
            lengths=(lengths, any_space),
            norm_gain=(norm_gain, any_space),
            in_proj=(in_proj, any_space),
            out_proj=(out_proj.reshape(2, W, H), any_space),
            skip_gain=(skip_gain, any_space),
            glu_weight=(glu_weight, any_space),
            glu_bias=(glu_bias, any_space),
            decay_log=(decay_log, any_space),
            frequency=(frequency, any_space),
            step_log=(step_log, any_space),
            cotangent=(cotangent.reshape(T, H), any_space),
        )
        results = dict(
            activations=((T, H), LOW),
            tokens_grad=((T * H // LANES, LANES), F32),
        )
        if fused:
            results |= dict(
                norm_gain_grad=((2, BLOCK), F32),
                in_proj_grad=((2, BLOCK, 2, N), F32),
                out_proj_grad=((2, 2, BLOCK, N), F32),
                skip_gain_grad=((2, BLOCK), F32),
                glu_weight_grad=((2, BLOCK, H), F32),
                glu_bias_grad=((2, BLOCK), F32),
                decay_log_grad=((2, N), F32),
                frequency_grad=((2, N), F32),
                step_log_grad=((2, N), F32),
            )
        else:
            results |= dict(
                matrix_sums=((2, H, CE + W), F32),
                vector_sums=((2, 4, H), F32),
                last_vector_sums=((2, 2, N), F32),
            )
        dma = pltpu.SemaphoreType.DMA
        scratch = dict(
            wi_raw=pltpu.VMEM((2, H, 2, N), LOW),
            wi=pltpu.VMEM((2, H, W), LOW),
            wi_t=pltpu.VMEM((W, H), LOW),
            wo_t=pltpu.VMEM((2, H, W), LOW),
            wo=pltpu.VMEM((2, W, H), LOW),
            wg=pltpu.VMEM((2, H, H), LOW),
            tok=pltpu.VMEM((T, H), LOW),
            cot=pltpu.VMEM((T, H), LOW),
            u=pltpu.VMEM((2, T, H), F32),
            inv=pltpu.VMEM((2, T, LANES), F32),
            unit=pltpu.VMEM((2, T, H), F32),
            act=pltpu.VMEM((2, T, H), F32),
            slope=pltpu.VMEM((2, T, H), F32),
            gate_slope=pltpu.VMEM((T, H), F32),
            mixed_skip=pltpu.VMEM((T, H), F32),
            normed_low=pltpu.VMEM((2, T, H), LOW),
            proj=pltpu.VMEM((2, T, W), F32),
            drive=pltpu.VMEM((T, W), F32),
            shifted=pltpu.VMEM((4, SUB, W), F32),
            local=pltpu.VMEM((4, T, W), F32),
            factor=pltpu.VMEM((4, T, W), F32),
            entered=pltpu.VMEM((4, 1, W), F32),
            proj_local=pltpu.VMEM((T, W), F32),
            proj_factor=pltpu.VMEM((T, W), F32),
            mixed=pltpu.VMEM((2, T, H), F32),
            th=pltpu.VMEM((2, T, H), F32),
            gate=pltpu.VMEM((2, T, H), F32),
            act_low=pltpu.VMEM((2, T, H), LOW),
            act_out=pltpu.VMEM((T, H), LOW),
            og=pltpu.VMEM((T, H), F32),
            tmp=pltpu.VMEM((T, H), F32),
            xg=pltpu.VMEM((2, T, W), F32),
            mixed_grad=pltpu.VMEM((2, T, H), LOW),
            right_e=pltpu.VMEM((2, 2 * T, CE), LOW),
            right_n=pltpu.VMEM((2, 2 * T, W), LOW),
            right_o=pltpu.VMEM((4, T, W), LOW),
            lt_y=pltpu.VMEM((H // 64, 2, 2, BLOCK, LANES), LOW),
            rt_y=pltpu.VMEM((3, H // 64, BLOCK, LANES), LOW),
            keep=pltpu.VMEM((2, T, LANES), F32),
            chunk_keep=pltpu.VMEM((2, 3, SUB, LANES), F32),
            chunk_table=pltpu.VMEM((4, SUB, W), F32),
            seq_table=pltpu.VMEM((4, nseq, W), F32),
            carry_out=pltpu.VMEM((4, 1, W), F32),
            carry_in=pltpu.VMEM((4, nseq, 1, W), F32),
            vec_a=pltpu.VMEM((2, 4, H), F32),
            vec_b=pltpu.VMEM((2, 2, N), F32),
        )
        for name in "gon":
            scratch[f"lt_{name}"] = pltpu.VMEM((2, H // 32, 2, BLOCK, LANES), LOW)
            scratch[f"rt_{name}"] = pltpu.VMEM((2, H // 32, BLOCK, LANES), LOW)
        if fused:
            nz = nseq // 2
            scratch["p_o"] = pltpu.VMEM((1, 2, 2, 2, BLOCK, W), LOW)
            for name, width in (("e", CE), ("n", W)):
                scratch[f"p_{name}"] = pltpu.VMEM((2, 2, 2, 2, 2, BLOCK, width), LOW)
            for _, _, label, first, last, order in plan:
                left = len(order) + order.count("z")
                for stage, axis in enumerate(order):
                    others = 3 if axis == "z" else 1
                    left -= 2 if axis == "z" else 1
                    shape = (2,) * left + (BLOCK, last - first)
                    scratch[f"got_{label}_{stage}"] = pltpu.VMEM((others,) + shape, LOW)
                    if left:
                        scratch[f"sum_{label}_{stage}"] = pltpu.VMEM(shape, LOW)
            for name, shape in (("vec_a", (4, H)), ("vec_b", (2, N))):
                scratch[name + "_in"] = pltpu.VMEM((2,) + shape, F32)
                scratch[name + "_mid"] = pltpu.VMEM((2,) + shape, F32)
                scratch[name + "_mid_in"] = pltpu.VMEM((2,) + shape, F32)
                scratch[name + "_z"] = pltpu.VMEM((nz,) + shape, F32)
                scratch[name + "_full"] = pltpu.VMEM((2,) + shape, F32)
        links = LINKS if fused else 4 * (nseq - 1)
        scratch["send_sems"] = dma((links,))
        scratch["recv_sems"] = dma((links,))
        scratch["load_sems"] = dma((8 + len(SMALL),))
        for name in SMALL:
            value = operands[name][0]
            space = pltpu.SMEM if name == "lengths" else pltpu.VMEM
            scratch[name + "_here"] = space(value.shape, value.dtype)
        names = list(operands) + list(results) + list(scratch)
        outs = pl.pallas_call(
            make_kernel(names, z),
            out_shape=[(pltpu.VMEM if fused else jax.ShapeDtypeStruct)(*v) for v in results.values()],
            in_specs=[spec for _, spec in operands.values()],
            out_specs=[vmem] * len(results),
            scratch_shapes=list(scratch.values()),
            compiler_params=pltpu.CompilerParams(
                collective_id=0, has_side_effects=True, vmem_limit_bytes=48 * 2**20
            ),
            name="two_layers",
        )(*(pltpu.with_memory_space_constraint(value, pltpu.HBM) for value, _ in operands.values()))
        if fused:
            outs = pl.pallas_call(
                hand_out,
                out_shape=[jax.ShapeDtypeStruct(*v) for v in results.values()],
                in_specs=[vmem] * len(results),
                out_specs=[any_space] * len(results),
                scratch_shapes=[dma((len(results),))],
                name="hand_out",
            )(*(pltpu.with_memory_space_constraint(out, pltpu.VMEM) for out in outs))
        o = types.SimpleNamespace(**dict(zip(results, outs)))
        activations = o.activations.reshape(T, 1, H)
        tokens_grad = o.tokens_grad.reshape(T, 1, H)
        if fused:
            return (
                activations, tokens_grad, o.norm_gain_grad, o.in_proj_grad,
                jnp.swapaxes(o.out_proj_grad, 2, 3), o.skip_gain_grad, o.glu_weight_grad,
                o.glu_bias_grad, o.decay_log_grad, o.frequency_grad, o.step_log_grad,
            )
        both = ("seq", "blk")
        sums = lax.psum_scatter(o.matrix_sums, both, scatter_dimension=1, tiled=True)
        rows = sums.shape[1]
        vectors, last = lax.psum((o.vector_sums.reshape(8, H), o.last_vector_sums.reshape(4, N)), both)
        start = lax.axis_index(both) * rows

        def owned(value, axis):
            return lax.dynamic_slice_in_dim(value, start, rows, axis)

        mine = owned(vectors, 1)
        skip_grad = jnp.stack([mine[6], mine[0]])
        bias_grad = jnp.stack([mine[7], mine[1]])
        totals = [jnp.stack([last[i], vectors[2 + i, 0:N]]) for i in range(4)]
        grads = discretize_grad(discretize(decay_log, frequency, step_log), *totals)
        in_grad = sums[:, :, CE:].reshape(2, rows, 2, N)
        along = jnp.sum(in_grad * owned(in_proj, 1).astype(F32), axis=(2, 3))
        gain_grad = (along + owned(skip_gain, 1) * skip_grad) / owned(norm_gain, 1)
        return (
            activations, tokens_grad, gain_grad, in_grad,
            jnp.moveaxis(sums[:, :, H:CE].reshape(2, rows, 2, N), 1, 3), skip_grad, sums[:, :, 0:H],
            bias_grad, *grads,
        )

    split = P("seq", "blk", None)
    owned = ("seq", "blk")
    return jax.shard_map(
        on_device,
        mesh=mesh,
        in_specs=(split,) + (P(),) * 10 + (split,),
        out_specs=(
            split, split, P(None, owned), P(None, owned, None, None), P(None, None, None, owned),
            P(None, owned), P(None, owned, None), P(None, owned), P(), P(), P(),
        ),
        check_vma=False,
    )
```
